32 devices in a mesh: section: 2 (over core), tensor: 2 (over x), dp: 8 (over z, y).
Axes of the slice: x: 2, y: 2, z: 4, core: 2. Of those that a mesh axis runs over, the one named last changes fastest.
Arguments:
- enc_in: bfloat16 [2, 784, 768], P(None, 'dp'), may hold values from -6 to 6
- keep_index: int32 [2, 16, 49], P(None, 'dp'), may hold values from 0 to 195, as said below
- image_count: int32 [2, 8], P(None, 'dp'), may hold values from 1 to 2
- enc_vec: bfloat16 [6, 768], replicated, may hold values from -0.8 to 1.5
- enc_qkv: bfloat16 [768, 3, 768], P(None, None, 'tensor'), may hold values from -0.21875 to 0.21875
- enc_qv_bias: bfloat16 [2, 768], P(None, 'tensor'), may hold values from -0.5 to 0.5
- enc_out_w: bfloat16 [768, 768], P('tensor'), may hold values from -0.875 to 0.875
- enc_fc1: bfloat16 [768, 3072], P(None, 'tensor'), may hold values from -0.21875 to 0.21875
- enc_fc1_bias: bfloat16 [3072], P('tensor'), may hold values from -1.5 to 1.5
- enc_fc2: bfloat16 [3072, 768], P('tensor'), may hold values from -0.109375 to 0.109375
- bridge_w: bfloat16 [768, 512], replicated, may hold values from -0.21875 to 0.21875
- dec_vec: bfloat16 [8, 512], replicated, may hold values from -4 to 4
- dec_pos: bfloat16 [196, 512], replicated, may hold values from -3 to 3
- dec_qkv: bfloat16 [512, 3, 512], P(None, None, 'tensor'), may hold values from -0.25 to 0.25
- dec_qv_bias: bfloat16 [2, 512], P(None, 'tensor'), may hold values from -0.5 to 0.5
- dec_out_w: bfloat16 [512, 512], P('tensor'), may hold values from -1.5 to 1.5
- dec_fc1: bfloat16 [512, 2048], P(None, 'tensor'), may hold values from -0.25 to 0.25
- dec_fc1_bias: bfloat16 [2048], P('tensor'), may hold values from -1.5 to 1.5
- dec_fc2: bfloat16 [2048, 512], P('tensor'), may hold values from -0.125 to 0.125
- dec_cot: bfloat16 [2, 3136, 512], P(None, 'dp'), may hold values from -6 to 6
Outputs:
- enc_out: bfloat16 [2, 784, 768], P(None, 'dp')
- dec_out: bfloat16 [2, 3136, 512], P('section', 'dp')
- grad_in: float32 [2, 784, 768], P('section', 'dp')
- grad_enc_vec: float32 [6, 768], replicated
- grad_enc_qkv: float32 [768, 3, 768], P(None, None, 'tensor')
- grad_enc_qv_bias: float32 [2, 768], P(None, 'tensor')
- grad_enc_out_w: float32 [768, 768], P('tensor')
- grad_enc_fc1: float32 [768, 3072], P(None, 'tensor')
- grad_enc_fc1_bias: float32 [3072], P('tensor')
- grad_enc_fc2: float32 [3072, 768], P('tensor')
- grad_bridge_w: float32 [768, 512], replicated
- grad_dec_vec: float32 [8, 512], replicated
- grad_dec_pos: float32 [196, 512], replicated
- grad_dec_qkv: float32 [512, 3, 512], P(None, None, 'tensor')
- grad_dec_qv_bias: float32 [2, 512], P(None, 'tensor')
- grad_dec_out_w: float32 [512, 512], P('tensor')
- grad_dec_fc1: float32 [512, 2048], P(None, 'tensor')
- grad_dec_fc1_bias: float32 [2048], P('tensor')
- grad_dec_fc2: float32 [2048, 512], P('tensor')
The draws below stay inside these ranges and needn't reach their ends.
Inputs may be any that keep to these rules, and one draw needn't show every extreme that they name: `keep_index`: within one image slot the 49 numbers are different.
All inputs are finite; a program needn't handle non-finite values.
Results may differ from the reference program's by a relative error of at most 0.025.
Values may be sent and summed in bfloat16 or wider, within the bound.
No kernel may reach another device: no remote copies, remote signals or barrier semaphores. Data moves between devices by JAX's collectives and lax.ppermute only.
A program may use at most 192 MiB of HBM per device.

```python
import math
import jax
import jax.numpy as jnp
from jax import lax

DE = 768
HE = 12
FE = 3072
DD = 512
HD = 16
FD = 2048
PATCHES = 196
VIS = 49
MICRO = 2
IMG_CAP = 2
IMAGES = 16
ROWS_E = 784
ROWS_D = 3136


def stacked_rows(key, row_total, features, gain_rows, token_rows):
    gains = jax.random.uniform(jax.random.fold_in(key, 1), (row_total, features), jnp.float32, 0.5, 1.5)
    biases = 0.2 * jnp.clip(jax.random.normal(jax.random.fold_in(key, 2), (row_total, features), jnp.float32), -4.0, 4.0)
    tokens = jnp.clip(jax.random.normal(jax.random.fold_in(key, 3), (row_total, features), jnp.float32), -4.0, 4.0)
    row_index = jnp.arange(row_total)[:, None]
    is_gain = jnp.zeros((row_total, 1), jnp.bool_)
    for chosen in gain_rows:
        is_gain = is_gain | (row_index == chosen)
    is_token = jnp.zeros((row_total, 1), jnp.bool_)
    for chosen in token_rows:
        is_token = is_token | (row_index == chosen)
    return jnp.where(is_gain, gains, jnp.where(is_token, tokens, biases))


def draw_enc_vec(key, part):
    key = jax.random.fold_in(key, 21)
    return stacked_rows(key, 6, DE, (0, 3), ()).astype(jnp.bfloat16)


def draw_dec_vec(key, part):
    key = jax.random.fold_in(key, 22)
    return stacked_rows(key, 8, DD, (2, 5), (1,)).astype(jnp.bfloat16)


def draw_keep_index(key, part):
    key = jax.random.fold_in(key, 23)
    several = jax.random.split(key, MICRO * IMAGES)
    picks = jax.vmap(lambda single: jax.random.permutation(single, PATCHES)[:VIS])(several)
    return picks.reshape(MICRO, IMAGES, VIS).astype(jnp.int32)


def draw_image_count(key, part):
    key = jax.random.fold_in(key, 24)
    groups = IMAGES // IMG_CAP
    counts = jax.random.randint(jax.random.fold_in(key, 1), (MICRO * groups,), 1, IMG_CAP + 1)
    chosen = jax.random.randint(jax.random.fold_in(key, 2), (), 0, MICRO * groups)
    counts = counts.at[chosen].set(IMG_CAP)
    return counts.reshape(MICRO, groups).astype(jnp.int32)


def block_scale(own_key, shape, cuts, least, largest):
    def one(dim, parts):
        draws = jax.random.uniform(jax.random.fold_in(jax.random.fold_in(own_key, 6), dim), (parts,), jnp.float32, least / len(cuts), largest / len(cuts))
        return jnp.repeat(jnp.exp(draws), shape[dim] // parts).reshape((-1,) + (1,) * (len(shape) - dim - 1))

    level = one(*cuts[0])
    for cut in cuts[1:]:
        level = level * one(*cut)
    return level


def noise(stream_key, extent, width, bound, shards=(), held_as=jnp.bfloat16):
    entries = width * jax.random.normal(stream_key, extent, jnp.float32)
    if shards:
        entries = entries * block_scale(stream_key, extent, shards, -0.22, 0.18)
    return jnp.clip(entries, -bound, bound).astype(held_as)


def setup_inputs(seed: int = 0) -> dict:
    key_list = jax.random.split(jax.random.key(seed), 21)
    return {
        "enc_in": noise(key_list[0], (MICRO, ROWS_E, DE), 1.0, 6.0, ((1, 8),)),
        "keep_index": draw_keep_index(jax.random.fold_in(key_list[20], 71), 0),
        "image_count": draw_image_count(jax.random.fold_in(key_list[20], 71), 0),
        "enc_vec": draw_enc_vec(jax.random.fold_in(key_list[20], 71), 0),
        "enc_qkv": noise(key_list[4], (DE, 3, DE), DE ** -0.5, 0.21875, ((2, 2),)),
        "enc_qv_bias": noise(key_list[5], (2, DE), 0.1, 0.5, ((1, 2),)),
        "enc_out_w": noise(key_list[6], (DE, DE), (DE // 16) ** -0.5, 0.875, ((0, 2),)),
        "enc_fc1": noise(key_list[7], (DE, FE), DE ** -0.5, 0.21875, ((1, 2),)),
        "enc_fc1_bias": noise(key_list[8], (FE,), 0.3, 1.5, ((0, 2),)),
        "enc_fc2": noise(key_list[9], (FE, DE), FE ** -0.5, 0.109375, ((0, 2),)),
        "bridge_w": noise(key_list[10], (DE, DD), DE ** -0.5, 0.21875),
        "dec_vec": draw_dec_vec(jax.random.fold_in(key_list[20], 71), 0),
        "dec_pos": noise(key_list[12], (PATCHES, DD), 0.5, 3.0),
        "dec_qkv": noise(key_list[13], (DD, 3, DD), DD ** -0.5, 0.25, ((2, 2),)),
        "dec_qv_bias": noise(key_list[14], (2, DD), 0.1, 0.5, ((1, 2),)),
        "dec_out_w": noise(key_list[15], (DD, DD), (DD // 32) ** -0.5, 1.5, ((0, 2),)),
        "dec_fc1": noise(key_list[16], (DD, FD), DD ** -0.5, 0.25, ((1, 2),)),
        "dec_fc1_bias": noise(key_list[17], (FD,), 0.3, 1.5, ((0, 2),)),
        "dec_fc2": noise(key_list[18], (FD, DD), FD ** -0.5, 0.125, ((0, 2),)),
        "dec_cot": noise(key_list[19], (MICRO, ROWS_D, DD), 1.0, 6.0, ((1, 8),)),
    }


HIGHEST = lax.Precision.HIGHEST
EPSILON = 1e-06

@jax.custom_vjp
def low(v):
    return lax.optimization_barrier(v.astype(jnp.bfloat16)).astype(jnp.float32)

@jax.custom_vjp
def low_back(v):
    return v

def low_keep(v):
    return (low(v), None)

def low_pass(kept, grad):
    return (grad,)

def back_keep(v):
    return (v, None)

def back_low(kept, grad):
    return (low(grad),)
low.defvjp(low_keep, low_pass)
low_back.defvjp(back_keep, back_low)

def both_ways(values):
    return low_back(low(values))

def product(left, right):
    return jnp.dot(left, right, precision=HIGHEST)

def layer_norm(values, gain_row, offset_row):
    center = values - lax.optimization_barrier(jnp.mean(values, axis=-1, keepdims=True))
    spread = lax.optimization_barrier(jnp.mean(center * center, axis=-1, keepdims=True))
    return center * lax.rsqrt(spread + EPSILON) * gain_row + offset_row

def attention_core(queries, key_rows, value_rows, head_count, length):
    total_rows, features = queries.shape
    head_size = features // head_count
    shape_four = (total_rows // length, length, head_count, head_size)
    scores = jnp.einsum('bqhd,bkhd->bhqk', queries.reshape(shape_four), key_rows.reshape(shape_four), precision=HIGHEST)
    scores = low_back(scores * (1.0 / math.sqrt(head_size)))
    attention_weights = low(jax.nn.softmax(scores, axis=-1))
    mixture = jnp.einsum('bhqk,bkhd->bqhd', attention_weights, value_rows.reshape(shape_four), precision=HIGHEST)
    return mixture.reshape(total_rows, features)

def residual_block(inputs, vectors, qkv_weight, qv_bias, out_weight, up_weight, up_bias, down_weight, head_count, length):
    features = inputs.shape[1]
    normed = low(layer_norm(inputs, vectors[0], vectors[1]))
    projected = product(normed, qkv_weight.reshape(features, 3 * features))
    queries = both_ways(projected[:, :features] + qv_bias[0])
    key_rows = both_ways(projected[:, features:2 * features])
    value_rows = both_ways(projected[:, 2 * features:] + qv_bias[1])
    mixture = both_ways(jax.checkpoint(attention_core, static_argnums=(3, 4))(queries, key_rows, value_rows, head_count, length))
    middle = inputs + low_back(product(mixture, out_weight)) + vectors[2]
    normed_two = low(layer_norm(middle, vectors[3], vectors[4]))
    hidden_pre = low_back(product(normed_two, up_weight) + up_bias)
    hidden = low(jax.nn.gelu(hidden_pre, approximate=False))
    return middle + low_back(product(hidden, down_weight)) + vectors[5]

def forward(inputs, enc_vec, enc_qkv, enc_qv_bias, enc_out_w, enc_fc1, enc_fc1_bias, enc_fc2, bridge_w, dec_vec, dec_pos, dec_qkv, dec_qv_bias, dec_out_w, dec_fc1, dec_fc1_bias, dec_fc2, live_enc, live_dec, selector):
    encoded = residual_block(inputs, enc_vec, enc_qkv, enc_qv_bias, enc_out_w, enc_fc1, enc_fc1_bias, enc_fc2, HE, VIS)
    handed = both_ways(encoded * live_enc)
    lifted = low_back(product(handed, bridge_w) + dec_vec[0])
    images = selector.shape[0]
    placed = jnp.einsum('npj,njd->npd', selector, lifted.reshape(images, VIS, DD), precision=HIGHEST)
    visible = lax.optimization_barrier(jnp.sum(selector, axis=2, keepdims=True))
    starting = (placed + (1.0 - visible) * dec_vec[1] + dec_pos).reshape(images * PATCHES, DD)
    decoded = residual_block(starting, dec_vec[2:], dec_qkv, dec_qv_bias, dec_out_w, dec_fc1, dec_fc1_bias, dec_fc2, HD, PATCHES)
    return (handed, decoded * live_dec)

def reference(enc_in, keep_index, image_count, enc_vec, enc_qkv, enc_qv_bias, enc_out_w, enc_fc1, enc_fc1_bias, enc_fc2, bridge_w, dec_vec, dec_pos, dec_qkv, dec_qv_bias, dec_out_w, dec_fc1, dec_fc1_bias, dec_fc2, dec_cot):
    slots = jnp.arange(IMAGES, dtype=jnp.int32) % IMG_CAP
    counts = jnp.repeat(image_count, IMG_CAP, axis=1)
    live_image = (slots[None, :] < counts).astype(jnp.float32)
    live_enc = jnp.repeat(live_image, VIS, axis=1).reshape(-1, 1)
    live_dec = jnp.repeat(live_image, PATCHES, axis=1).reshape(-1, 1)
    patch_index = jnp.arange(PATCHES, dtype=jnp.int32)
    selector = (keep_index.reshape(-1, 1, VIS) == patch_index[None, :, None]).astype(jnp.float32)
    weights = tuple((weight.astype(jnp.float32) for weight in (enc_vec, enc_qkv, enc_qv_bias, enc_out_w, enc_fc1, enc_fc1_bias, enc_fc2, bridge_w, dec_vec, dec_pos, dec_qkv, dec_qv_bias, dec_out_w, dec_fc1, dec_fc1_bias, dec_fc2)))
    inputs = enc_in.astype(jnp.float32).reshape(-1, DE)

    def wrapped(inputs, *weights):
        return forward(inputs, *weights, live_enc, live_dec, selector)
    (handed, decoded), pullback = jax.vjp(wrapped, inputs, *weights)
    gradients = pullback((jnp.zeros_like(handed), dec_cot.astype(jnp.float32).reshape(-1, DD)))
    enc_out = handed.reshape(MICRO, ROWS_E, DE).astype(jnp.bfloat16)
    dec_out = decoded.reshape(MICRO, ROWS_D, DD).astype(jnp.bfloat16)
    grad_in = gradients[0].reshape(MICRO, ROWS_E, DE)
    return (enc_out, dec_out, grad_in, gradients[1], gradients[2], gradients[3], gradients[4], gradients[5], gradients[6], gradients[7], gradients[8], gradients[9], gradients[10], gradients[11], gradients[12], gradients[13], gradients[14], gradients[15], gradients[16])
```

```python
import math

import jax
import jax.numpy as jnp
from jax import lax
from jax.sharding import PartitionSpec as P

HE = 12
HD = 16
PATCHES = 196
VIS = 49
EPSILON = 1e-06
LOW = jnp.bfloat16
FULL = jnp.float32


def matmul(left, right):
    return jnp.dot(left, right, preferred_element_type=FULL)


def left_product(left, right):
    return lax.dot_general(left, right, (((0,), (0,)), ((), ())), preferred_element_type=FULL)


def right_product(left, right):
    return lax.dot_general(left, right, (((1,), (1,)), ((), ())), preferred_element_type=FULL)


def swap(value, axis):
    return lax.ppermute(value, axis, [(i, i ^ 1) for i in range(lax.axis_size(axis))])


def normalize(values):
    center = values - jnp.mean(values, axis=-1, keepdims=True)
    scale = lax.rsqrt(jnp.mean(center * center, axis=-1, keepdims=True) + EPSILON)
    return center * scale, scale


def norm_back(grad, gain, xhat, scale):
    inner = grad * gain
    return scale * (
        inner
        - jnp.mean(inner, axis=-1, keepdims=True)
        - xhat * jnp.mean(inner * xhat, axis=-1, keepdims=True)
    )


def gelu(values):
    return values * (0.5 * (1.0 + lax.erf(values * math.sqrt(0.5))))


def gelu_slope(values):
    return 0.5 * (1.0 + lax.erf(values * math.sqrt(0.5))) + values * jnp.exp(
        -0.5 * values * values
    ) * (1.0 / math.sqrt(2.0 * math.pi))


def low(values):
    return values.astype(LOW)


def full(values):
    return values.astype(FULL)


def heads_of(rows, head_count, length):
    return rows.reshape(rows.shape[0] // length, length, head_count, rows.shape[1] // head_count)


def attention_part(values, vectors, qkv, qv_bias, out_w, head_count, length):
    rows, features = values.shape
    width = qkv.shape[2]
    xhat, scale = normalize(values)
    normed = low(xhat * vectors[0] + vectors[1])
    projected = matmul(normed, qkv.reshape(features, 3 * width))
    queries = low(projected[:, :width] + qv_bias[0])
    key_rows = low(projected[:, width : 2 * width])
    value_rows = low(projected[:, 2 * width :] + qv_bias[1])
    factor = 1.0 / math.sqrt(width // head_count)
    scores = (
        jnp.einsum(
            "bqhd,bkhd->bhqk",
            heads_of(queries, head_count, length),
            heads_of(key_rows, head_count, length),
            preferred_element_type=FULL,
        )
        * factor
    )
    exponent = jnp.exp(scores - jnp.max(scores, axis=-1, keepdims=True))
    weights = exponent / jnp.sum(exponent, axis=-1, keepdims=True)
    weights_low = low(weights)
    mixture = low(
        jnp.einsum(
            "bhqk,bkhd->bqhd",
            weights_low,
            heads_of(value_rows, head_count, length),
            preferred_element_type=FULL,
        ).reshape(rows, width)
    )
    saved = (xhat, scale, normed, queries, key_rows, value_rows, weights_low, mixture)
    return low(matmul(mixture, out_w)), saved


def hidden_part(middle, vectors, fc1, fc1_bias, fc2):
    xhat, scale = normalize(middle)
    normed = low(xhat * vectors[3] + vectors[4])
    hidden_pre = matmul(normed, fc1) + fc1_bias
    hidden = low(gelu(hidden_pre))
    return low(matmul(hidden, fc2)), (xhat, scale, normed, hidden_pre, hidden)


def hidden_back(out_low, hidden_pre, fc1, fc2):
    up_grad = low(gelu_slope(hidden_pre) * right_product(out_low, fc2))
    return low(right_product(up_grad, fc1)), up_grad


def attention_back(middle_low, saved, qkv, out_w, head_count, length):
    xhat, scale, normed, queries, key_rows, value_rows, weights_low, mixture = saved
    rows, width = queries.shape
    factor = 1.0 / math.sqrt(width // head_count)
    mixture_grad = low(right_product(middle_low, out_w))
    upstream = heads_of(mixture_grad, head_count, length)
    weight_grad = jnp.einsum(
        "bqhd,bkhd->bhqk",
        upstream,
        heads_of(value_rows, head_count, length),
        preferred_element_type=FULL,
    )
    value_grad = jnp.einsum(
        "bhqk,bqhd->bkhd", weights_low, upstream, preferred_element_type=FULL
    )
    weights = full(weights_low)
    score_grad = low(
        weights * (weight_grad - jnp.sum(weights * weight_grad, axis=-1, keepdims=True))
    )
    query_grad = factor * jnp.einsum(
        "bhqk,bkhd->bqhd",
        score_grad,
        heads_of(key_rows, head_count, length),
        preferred_element_type=FULL,
    )
    key_grad = factor * jnp.einsum(
        "bhqk,bqhd->bkhd",
        score_grad,
        heads_of(queries, head_count, length),
        preferred_element_type=FULL,
    )
    stacked = low(
        jnp.concatenate(
            [member.reshape(rows, width) for member in (query_grad, key_grad, value_grad)], axis=1
        )
    )
    return low(right_product(stacked, qkv.reshape(qkv.shape[0], 3 * width))), stacked


def column_sum(values):
    return jnp.sum(full(values), axis=0)


def pair(first, second):
    return full(first) + full(second)


def pick(stacked, index):
    return lax.dynamic_index_in_dim(stacked, index, 0, keepdims=False)


def ordered(index, mine, other):
    return jnp.stack([jnp.where(index == 0, mine, other), jnp.where(index == 0, other, mine)])


def line_sum(value, length):
    if length == 4:
        inward = [(0, 2), (1, 3), (6, 4), (7, 5)]
        middle = [(2, 4), (4, 2), (3, 5), (5, 3)]
        outward = [(2, 0), (3, 1), (4, 6), (5, 7)]
        place = lax.axis_index("dp") // 2
        inner = (place == 1) | (place == 2)
        value = low(pair(value, lax.ppermute(value, "dp", inward)))
        value = low(pair(value, lax.ppermute(value, "dp", middle)))
        return jnp.where(inner, value, lax.ppermute(value, "dp", outward))
    step = 1
    while step < length:
        partner = [(i, i ^ (2 * step)) for i in range(2 * length)]
        value = low(pair(value, lax.ppermute(value, "dp", partner)))
        step *= 2
    return value


def grand_total(partial):
    rows, cols = partial.shape
    core = lax.axis_index("section")
    groups = lax.axis_size("dp")
    side = lax.axis_index("dp") % 2
    quarters = low(partial).reshape(2, 2, rows // 4, cols)
    half = low(pair(pick(quarters, core), swap(pick(quarters, 1 - core), "section")))
    block = low(pair(pick(half, side), swap(pick(half, 1 - side), "dp")))
    block = line_sum(block, groups // 2)
    half = ordered(side, block, swap(block, "dp"))
    whole = ordered(core, half, swap(half, "section"))
    return full(whole.reshape(rows, cols))


def body(
    enc_in,
    keep_index,
    image_count,
    enc_vec,
    enc_qkv,
    enc_qv_bias,
    enc_out_w,
    enc_fc1,
    enc_fc1_bias,
    enc_fc2,
    bridge_w,
    dec_vec,
    dec_pos,
    dec_qkv,
    dec_qv_bias,
    dec_out_w,
    dec_fc1,
    dec_fc1_bias,
    dec_fc2,
    dec_cot,
):
    core = lax.axis_index("section")
    slots = keep_index.shape[1]
    shards = lax.axis_size("tensor")
    enc_heads, dec_heads = HE // shards, HD // shards
    enc_width, dec_width = bridge_w.shape
    enc_low = pick(enc_in, core)
    keep = pick(keep_index, core)
    cot = pick(dec_cot, core)
    count = pick(image_count, core)
    live = (lax.broadcasted_iota(jnp.int32, (slots, 1), 0) < count).astype(FULL)
    live_enc = jnp.repeat(live, VIS, axis=0)
    live_dec = jnp.repeat(live, PATCHES, axis=0)
    dec_rows = dec_vec[2:]

    enc_x = full(enc_low)
    part, enc_saved = attention_part(
        enc_x, enc_vec, enc_qkv, enc_qv_bias, enc_out_w, enc_heads, VIS
    )
    enc_middle = enc_x + pair(part, swap(part, "tensor")) + enc_vec[2]
    part, enc_two = hidden_part(enc_middle, enc_vec, enc_fc1, enc_fc1_bias, enc_fc2)
    encoded = enc_middle + pair(part, swap(part, "tensor")) + enc_vec[5]
    enc_out = low(encoded * live_enc)
    enc_out_both = ordered(core, enc_out, swap(enc_out, "section"))

    lifted = matmul(enc_out, bridge_w) + dec_vec[0]
    selector = (
        keep[:, None, :] == lax.broadcasted_iota(jnp.int32, (slots, PATCHES, VIS), 1)
    ).astype(FULL)
    placed = jnp.einsum(
        "npj,njd->npd",
        selector,
        lifted.reshape(slots, VIS, dec_width),
        precision=lax.Precision.HIGHEST,
    )
    hidden_patch = 1.0 - jnp.sum(selector, axis=2, keepdims=True)
    starting = (placed + hidden_patch * dec_vec[1] + dec_pos).reshape(slots * PATCHES, dec_width)
    part, dec_saved = attention_part(
        starting, dec_rows, dec_qkv, dec_qv_bias, dec_out_w, dec_heads, PATCHES
    )
    dec_middle = starting + pair(part, swap(part, "tensor")) + dec_rows[2]
    part_out, dec_two = hidden_part(dec_middle, dec_rows, dec_fc1, dec_fc1_bias, dec_fc2)

    dec_gain = full(dec_rows)
    out_low = low(full(cot) * live_dec)
    part, up_grad = hidden_back(out_low, dec_two[3], dec_fc1, dec_fc2)
    two_grad = pair(part, swap(part, "tensor"))
    decoded = dec_middle + pair(part_out, swap(part_out, "tensor")) + dec_rows[5]
    dec_out = low(decoded * live_dec)[None]
    g_dec_fc2 = grand_total(left_product(dec_two[4], out_low))
    g_dec_fc1 = grand_total(left_product(dec_two[2], up_grad))
    middle_grad = full(out_low) + norm_back(two_grad, dec_gain[3], dec_two[0], dec_two[1])
    middle_low = low(middle_grad)
    part, stacked = attention_back(middle_low, dec_saved, dec_qkv, dec_out_w, dec_heads, PATCHES)
    one_grad = pair(part, swap(part, "tensor"))
    g_dec_out_w = grand_total(left_product(dec_saved[7], middle_low))
    g_dec_qkv = grand_total(left_product(dec_saved[2], stacked))
    starting_grad = middle_grad + norm_back(one_grad, dec_gain[0], dec_saved[0], dec_saved[1])
    grad_three = starting_grad.reshape(slots, PATCHES, dec_width)
    lifted_grad = low(
        jnp.einsum(
            "npj,npd->njd", selector, grad_three, precision=lax.Precision.HIGHEST
        ).reshape(slots * VIS, dec_width)
    )
    enc_cot = low(right_product(lifted_grad, bridge_w) * live_enc)
    dec_small = jnp.concatenate(
        [
            jnp.sum(grad_three, axis=0),
            column_sum(lifted_grad)[None],
            jnp.sum(hidden_patch * grad_three, axis=(0, 1))[None],
            column_sum(one_grad * dec_saved[0])[None],
            column_sum(one_grad)[None],
            column_sum(middle_grad)[None],
            column_sum(two_grad * dec_two[0])[None],
            column_sum(two_grad)[None],
            column_sum(out_low)[None],
            column_sum(up_grad).reshape(-1, dec_width),
            column_sum(stacked).reshape(3, -1)[::2].reshape(-1, dec_width),
        ],
        axis=0,
    )
    dec_small_rows = dec_small.shape[0]
    dec_small = grand_total(jnp.pad(dec_small, ((0, -dec_small_rows % 4), (0, 0))))
    g_bridge = grand_total(left_product(enc_out, lifted_grad))

    enc_gain = full(enc_vec)
    part, enc_up_grad = hidden_back(enc_cot, enc_two[3], enc_fc1, enc_fc2)
    two_grad = pair(part, swap(part, "tensor"))
    g_enc_fc2 = grand_total(left_product(enc_two[4], enc_cot))
    g_enc_fc1 = grand_total(left_product(enc_two[2], enc_up_grad))
    middle_grad = full(enc_cot) + norm_back(two_grad, enc_gain[3], enc_two[0], enc_two[1])
    middle_low = low(middle_grad)
    part, enc_stacked = attention_back(middle_low, enc_saved, enc_qkv, enc_out_w, enc_heads, VIS)
    one_grad = pair(part, swap(part, "tensor"))
    g_enc_out_w = grand_total(left_product(enc_saved[7], middle_low))
    g_enc_qkv = grand_total(left_product(enc_saved[2], enc_stacked))
    grad_in = (middle_grad + norm_back(one_grad, enc_gain[0], enc_saved[0], enc_saved[1]))[None]
    enc_small = jnp.concatenate(
        [
            column_sum(one_grad * enc_saved[0])[None],
            column_sum(one_grad)[None],
            column_sum(middle_grad)[None],
            column_sum(two_grad * enc_two[0])[None],
            column_sum(two_grad)[None],
            column_sum(enc_cot)[None],
            column_sum(enc_up_grad).reshape(-1, enc_width),
            column_sum(enc_stacked).reshape(3, -1)[::2].reshape(-1, enc_width),
        ],
        axis=0,
    )
    enc_small_rows = enc_small.shape[0]
    enc_small = grand_total(jnp.pad(enc_small, ((0, -enc_small_rows % 4), (0, 0))))

    hidden_rows = enc_fc1.shape[1] // enc_width
    g_enc_vec = enc_small[:6]
    g_enc_fc1_bias = enc_small[6 : 6 + hidden_rows].reshape(-1)
    g_enc_qv_bias = enc_small[6 + hidden_rows : enc_small_rows].reshape(2, -1)
    hidden_rows = dec_fc1.shape[1] // dec_width
    g_dec_pos = dec_small[:PATCHES]
    g_dec_vec = dec_small[PATCHES : PATCHES + 8]
    g_dec_fc1_bias = dec_small[PATCHES + 8 : PATCHES + 8 + hidden_rows].reshape(-1)
    g_dec_qv_bias = dec_small[PATCHES + 8 + hidden_rows : dec_small_rows].reshape(2, -1)
    return (
        enc_out_both,
        dec_out,
        grad_in,
        g_enc_vec,
        g_enc_qkv.reshape(enc_qkv.shape),
        g_enc_qv_bias,
        g_enc_out_w,
        g_enc_fc1,
        g_enc_fc1_bias,
        g_enc_fc2,
        g_bridge,
        g_dec_vec,
        g_dec_pos,
        g_dec_qkv.reshape(dec_qkv.shape),
        g_dec_qv_bias,
        g_dec_out_w,
        g_dec_fc1,
        g_dec_fc1_bias,
        g_dec_fc2,
    )


def solution(mesh):
    return jax.shard_map(
        body,
        mesh=mesh,
        in_specs=(
            P(None, "dp", None),
            P(None, "dp", None),
            P(None, "dp"),
            P(),
            P(None, None, "tensor"),
            P(None, "tensor"),
            P("tensor", None),
            P(None, "tensor"),
            P("tensor"),
            P("tensor", None),
            P(),
            P(),
            P(),
            P(None, None, "tensor"),
            P(None, "tensor"),
            P("tensor", None),
            P(None, "tensor"),
            P("tensor"),
            P("tensor", None),
            P(None, "dp", None),
        ),
        out_specs=(
            P(None, "dp", None),
            P("section", "dp", None),
            P("section", "dp", None),
            P(),
            P(None, None, "tensor"),
            P(None, "tensor"),
            P("tensor", None),
            P(None, "tensor"),
            P("tensor"),
            P("tensor", None),
            P(),
            P(),
            P(),
            P(None, None, "tensor"),
            P(None, "tensor"),
            P("tensor", None),
            P(None, "tensor"),
            P("tensor"),
            P("tensor", None),
        ),
        check_vma=False,
    )
```

```python
import functools
import math

import jax
import jax.numpy as jnp
from jax import lax
from jax.experimental import pallas as pl
from jax.experimental.pallas import tpu as pltpu
from jax.sharding import PartitionSpec as P

HE = 12
HD = 16
PATCHES = 196
VIS = 49
PAD_E = 64
PAD_D = 208
LANES = 128
EPSILON = 1e-06
LOW = jnp.bfloat16
FULL = jnp.float32
MIB = 2**20


def low(values):
    return values.astype(LOW)


def full(values):
    return values.astype(FULL)


def matmul(left, right):
    return jnp.dot(left, right, preferred_element_type=FULL)


def left_product(left, right):
    return lax.dot_general(left, right, (((0,), (0,)), ((), ())), preferred_element_type=FULL)


def right_product(left, right):
    return lax.dot_general(left, right, (((1,), (1,)), ((), ())), preferred_element_type=FULL)


def pair(first, second):
    return full(first) + full(second)


def swap(value, axis):
    return lax.ppermute(value, axis, [(i, i ^ 1) for i in range(lax.axis_size(axis))])


def normalize(values):
    center = values - jnp.mean(values, axis=-1, keepdims=True)
    scale = lax.rsqrt(jnp.mean(center * center, axis=-1, keepdims=True) + EPSILON)
    return center * scale, scale


def norm_back(grad, gain, xhat, scale):
    inner = grad * gain
    return scale * (
        inner
        - jnp.mean(inner, axis=-1, keepdims=True)
        - xhat * jnp.mean(inner * xhat, axis=-1, keepdims=True)
    )


def column_sum(values):
    return jnp.sum(full(values), axis=0, keepdims=True)


def one_hot_rows(padded, length, images, packed_first=False):
    shape = (images * length, images * padded) if packed_first else (images * padded, images * length)
    first = lax.broadcasted_iota(jnp.int32, shape, 0)
    second = lax.broadcasted_iota(jnp.int32, shape, 1)
    packed, wide = (first, second) if packed_first else (second, first)
    hit = None
    for image in range(images):
        here = (
            (packed >= image * length)
            & (packed < (image + 1) * length)
            & (wide - image * padded == packed - image * length)
        )
        hit = here if hit is None else hit | here
    return low(jnp.where(hit, 1.0, 0.0))


def head_masks(head_size):
    lane = lax.broadcasted_iota(jnp.int32, (1, LANES), 1)
    return [
        jnp.where((lane >= j * head_size) & (lane < (j + 1) * head_size), 1.0, 0.0)
        for j in range(LANES // head_size)
    ]


def spread_heads(values, masks):
    wide = full(values)
    return jnp.concatenate([low(wide * mask) for mask in masks], axis=0)


def gather_heads(stacked, masks):
    rows = stacked.shape[0] // len(masks)
    total = None
    for j, mask in enumerate(masks):
        term = stacked[j * rows : (j + 1) * rows] * mask
        total = term if total is None else total + term
    return total


def attend(queries, key_rows, value_rows, masks, allowed, factor):
    scores = right_product(spread_heads(queries, masks), key_rows) * factor
    scores = jnp.where(allowed, scores, -1e30)
    exponent = jnp.exp(scores - jnp.max(scores, axis=-1, keepdims=True))
    weights_low = low(exponent * (1.0 / jnp.sum(exponent, axis=-1, keepdims=True)))
    return weights_low, low(gather_heads(matmul(weights_low, value_rows), masks))


def attend_back(queries, key_rows, value_rows, weights_low, upstream, masks, factor):
    spread_up = spread_heads(upstream, masks)
    weight_grad = right_product(spread_up, value_rows)
    weights = full(weights_low)
    product = weights * weight_grad
    score_grad = low(product - weights * jnp.sum(product, axis=-1, keepdims=True))
    query_grad = gather_heads(matmul(score_grad, key_rows), masks) * factor
    key_grad = left_product(score_grad, spread_heads(queries, masks)) * factor
    value_grad = left_product(weights_low, spread_up)
    return low(query_grad), low(key_grad), low(value_grad)


def same_image(heads, images, padded, length):
    shape = (heads * images * padded, images * padded)
    row = lax.broadcasted_iota(jnp.int32, shape, 0)
    key = lax.broadcasted_iota(jnp.int32, shape, 1)
    hit = None
    for head in range(heads):
        for image in range(images):
            start = (head * images + image) * padded
            here = (
                (row >= start)
                & (row < start + padded)
                & (key >= image * padded)
                & (key < image * padded + length)
            )
            hit = here if hit is None else hit | here
    return hit


def live_rows(count, rows, padded):
    row = lax.broadcasted_iota(jnp.int32, (rows, 1), 0)
    return jnp.where(row < count * padded, 1.0, 0.0)


def kernel_call(kernel, outs, *arguments, scalars=0, flops=0, name=None):
    specs = [pl.BlockSpec(memory_space=pltpu.SMEM)] * scalars
    specs += [pl.BlockSpec(memory_space=pltpu.VMEM)] * (len(arguments) - scalars)
    moved = sum(math.prod(x.shape) * x.dtype.itemsize for x in (*arguments, *outs))
    return pl.pallas_call(
        kernel,
        out_shape=[jax.ShapeDtypeStruct(x.shape, x.dtype) for x in outs],
        in_specs=specs,
        out_specs=[pl.BlockSpec(memory_space=pltpu.VMEM)] * len(outs),
        compiler_params=pltpu.CompilerParams(vmem_limit_bytes=40 * MIB),
        cost_estimate=pl.CostEstimate(flops=flops, bytes_accessed=moved, transcendentals=0),
        name=name,
    )(*arguments)


def shaped(shape, dtype=LOW):
    return jax.ShapeDtypeStruct(shape, dtype)


def project_heads(normed, qkv_ref, bias, proj_ref, width):
    queries = low(matmul(normed, qkv_ref[0]) + bias[0:1])
    key_rows = low(matmul(normed, qkv_ref[1]))
    value_rows = low(matmul(normed, qkv_ref[2]) + bias[1:2])
    proj_ref[0] = queries
    proj_ref[1] = key_rows
    proj_ref[2] = value_rows


def enc_attend_kernel(
    images, head_size, x_ref, vec_ref, qkv_ref, bias_ref, out_w_ref,
    part_ref, x_out_ref, normed_ref, proj_ref, weights_ref, mix_ref,
):
    width = qkv_ref.shape[2]
    x = matmul(one_hot_rows(PAD_E, VIS, images), x_ref[...])
    x_out_ref[...] = low(x)
    vec = full(vec_ref[...])
    xhat, _ = normalize(x)
    normed = low(xhat * vec[0:1] + vec[1:2])
    normed_ref[...] = normed
    project_heads(normed, qkv_ref, full(bias_ref[...]), proj_ref, width)
    masks = head_masks(head_size)
    allowed = same_image(len(masks), images, PAD_E, VIS)
    for group in range(width // LANES):
        lanes = slice(group * LANES, (group + 1) * LANES)
        weights_low, mixture = attend(
            proj_ref[0, :, lanes],
            proj_ref[1, :, lanes],
            proj_ref[2, :, lanes],
            masks,
            allowed,
            1.0 / math.sqrt(head_size),
        )
        weights_ref[group] = weights_low
        mix_ref[:, lanes] = mixture
    part_ref[...] = low(matmul(mix_ref[...], out_w_ref[...]))


def mlp_forward(middle, gain, shift, fc1_ref, bias_ref, fc2_ref, normed_ref, hidden_ref, slope_ref):
    xhat, _ = normalize(middle)
    normed = low(xhat * gain + shift)
    normed_ref[...] = normed
    pre = matmul(normed, fc1_ref[...]) + full(bias_ref[...])
    share = 0.5 + 0.5 * lax.erf(pre * math.sqrt(0.5))
    hidden = low(pre * share)
    hidden_ref[...] = hidden
    slope = share + pre * jnp.exp(-0.5 * pre * pre) * (1.0 / math.sqrt(2.0 * math.pi))
    if slope_ref is not None:
        slope_ref[...] = low(slope)
    return low(matmul(hidden, fc2_ref[...])), slope


def enc_hidden_kernel(
    x_ref, vec_ref, part_ref, other_ref, fc1_ref, bias_ref, fc2_ref,
    part_two_ref, middle_ref, normed_ref, hidden_ref, slope_ref,
):
    vec = full(vec_ref[...])
    middle = full(x_ref[...]) + pair(part_ref[...], other_ref[...]) + vec[2:3]
    middle_ref[...] = middle
    part, _ = mlp_forward(
        middle, vec[3:4], vec[4:5], fc1_ref, bias_ref, fc2_ref, normed_ref, hidden_ref, slope_ref
    )
    part_two_ref[...] = part


def selector(keep_ref, image):
    patch = lax.broadcasted_iota(jnp.int32, (PAD_D, PAD_E), 0)
    return jnp.where(patch == keep_ref[image : image + 1, :], 1.0, 0.0)


def dec_attend_kernel(
    images, head_size, count_ref, keep_ref, middle_ref, part_ref, other_ref, enc_vec_ref, bridge_ref,
    vec_ref, pos_ref, qkv_ref, bias_ref, out_w_ref,
    part_out_ref, enc_out_ref, enc_pad_ref, starting_ref, normed_ref, proj_ref, weights_ref, mix_ref,
):
    width = qkv_ref.shape[2]
    vec = full(vec_ref[...])
    encoded = middle_ref[...] + pair(part_ref[...], other_ref[...]) + full(enc_vec_ref[...])[5:6]
    enc_pad = low(encoded * live_rows(count_ref[0], images * PAD_E, PAD_E))
    enc_pad_ref[...] = enc_pad
    enc_out_ref[...] = low(matmul(one_hot_rows(PAD_E, VIS, images, True), enc_pad))
    lifted = matmul(enc_pad, bridge_ref[...]) + vec[0:1]
    lifted_high = low(lifted)
    lifted_rest = low(lifted - full(lifted_high))
    pos = matmul(one_hot_rows(PAD_D, PATCHES, 1), pos_ref[...])
    for image in range(images):
        chosen = selector(keep_ref, image)
        rows = slice(image * PAD_E, (image + 1) * PAD_E)
        placed = matmul(low(chosen), lifted_high[rows]) + matmul(low(chosen), lifted_rest[rows])
        hidden_patch = 1.0 - jnp.sum(chosen, axis=1, keepdims=True)
        starting_ref[image * PAD_D : (image + 1) * PAD_D, :] = placed + hidden_patch * vec[1:2] + pos
    xhat, _ = normalize(starting_ref[...])
    normed = low(xhat * vec[2:3] + vec[3:4])
    normed_ref[...] = normed
    project_heads(normed, qkv_ref, full(bias_ref[...]), proj_ref, width)
    masks = head_masks(head_size)
    allowed = lax.broadcasted_iota(jnp.int32, (1, PAD_D), 1) < PATCHES
    groups = width // LANES
    for image in range(images):
        rows = slice(image * PAD_D, (image + 1) * PAD_D)
        for group in range(groups):
            lanes = slice(group * LANES, (group + 1) * LANES)
            weights_low, mixture = attend(
                proj_ref[0, rows, lanes],
                proj_ref[1, rows, lanes],
                proj_ref[2, rows, lanes],
                masks,
                allowed,
                1.0 / math.sqrt(head_size),
            )
            weights_ref[image * groups + group] = weights_low
            mix_ref[rows, lanes] = mixture
    part_out_ref[...] = low(matmul(mix_ref[...], out_w_ref[...]))


def dec_hidden_kernel(
    images, count_ref, starting_ref, part_ref, other_ref, vec_ref, fc1_ref, bias_ref, fc2_ref, cot_ref,
    part_back_ref, part_two_ref, middle_ref, normed_ref, hidden_ref, out_low_ref, up_ref,
    up_sum_ref, out_sum_ref,
):
    vec = full(vec_ref[...])
    middle = starting_ref[...] + pair(part_ref[...], other_ref[...]) + vec[4:5]
    middle_ref[...] = middle
    part, slope = mlp_forward(
        middle, vec[5:6], vec[6:7], fc1_ref, bias_ref, fc2_ref, normed_ref, hidden_ref, None
    )
    part_two_ref[...] = part
    spread = matmul(one_hot_rows(PAD_D, PATCHES, images), cot_ref[...])
    out_low = low(spread * live_rows(count_ref[0], images * PAD_D, PAD_D))
    out_low_ref[...] = out_low
    up_grad = low(slope * right_product(out_low, fc2_ref[...]))
    up_ref[...] = up_grad
    part_back_ref[...] = low(right_product(up_grad, fc1_ref[...]))
    up_sum_ref[...] = column_sum(up_grad)
    out_sum_ref[...] = column_sum(out_low)


def dec_out_kernel(images, count_ref, middle_ref, part_ref, other_ref, vec_ref, out_ref):
    decoded = middle_ref[...] + pair(part_ref[...], other_ref[...]) + full(vec_ref[...])[7:8]
    decoded = low(decoded * live_rows(count_ref[0], images * PAD_D, PAD_D))
    out_ref[...] = low(matmul(one_hot_rows(PAD_D, PATCHES, images, True), decoded))


def attention_back(
    images, padded, together, head_size, middle, out_grad, two_grad, gain, proj_ref, weights_ref,
    qkv_ref, out_w_ref, part_ref, middle_grad_ref, middle_low_ref, stacked_ref,
):
    width = qkv_ref.shape[2]
    xhat, scale = normalize(middle)
    middle_grad = out_grad + norm_back(two_grad, gain, xhat, scale)
    middle_grad_ref[...] = middle_grad
    middle_low = low(middle_grad)
    middle_low_ref[...] = middle_low
    mixture_grad = low(right_product(middle_low, out_w_ref[...]))
    masks = head_masks(head_size)
    groups = width // LANES
    step = images if together else 1
    for first in range(0, images, step):
        rows = slice(first * padded, (first + step) * padded)
        for group in range(groups):
            lanes = slice(group * LANES, (group + 1) * LANES)
            grads = attend_back(
                proj_ref[0, rows, lanes],
                proj_ref[1, rows, lanes],
                proj_ref[2, rows, lanes],
                weights_ref[first // step * groups + group],
                mixture_grad[rows, lanes],
                masks,
                1.0 / math.sqrt(head_size),
            )
            for j in range(3):
                stacked_ref[j, rows, lanes] = grads[j]
    total = right_product(stacked_ref[0], qkv_ref[0])
    for j in (1, 2):
        total = total + right_product(stacked_ref[j], qkv_ref[j])
    part_ref[...] = low(total)
    return xhat, middle_grad


def dec_attend_back_kernel(
    images, head_size, middle_ref, out_low_ref, part_in_ref, other_ref, vec_ref, proj_ref, weights_ref,
    qkv_ref, out_w_ref,
    part_ref, middle_grad_ref, middle_low_ref, stacked_ref, sums_ref, bias_sum_ref,
):
    vec = full(vec_ref[...])
    two_grad = pair(part_in_ref[...], other_ref[...])
    xhat, middle_grad = attention_back(
        images, PAD_D, False, head_size, middle_ref[...], full(out_low_ref[...]), two_grad, vec[5:6],
        proj_ref, weights_ref, qkv_ref, out_w_ref, part_ref, middle_grad_ref, middle_low_ref, stacked_ref,
    )
    sums_ref[0:1] = column_sum(middle_grad)
    sums_ref[1:2] = column_sum(two_grad * xhat)
    sums_ref[2:3] = column_sum(two_grad)
    bias_sum_ref[0:1] = column_sum(stacked_ref[0])
    bias_sum_ref[1:2] = column_sum(stacked_ref[2])


def dec_start_back_kernel(
    images, count_ref, keep_ref, starting_ref, part_ref, other_ref, vec_ref, middle_grad_ref, bridge_ref,
    enc_cot_ref, lifted_ref, pos_ref, sums_ref,
):
    vec = full(vec_ref[...])
    one_grad = pair(part_ref[...], other_ref[...])
    xhat, scale = normalize(starting_ref[...])
    starting_grad = middle_grad_ref[...] + norm_back(one_grad, vec[2:3], xhat, scale)
    sums_ref[2:3] = column_sum(one_grad * xhat)
    sums_ref[3:4] = column_sum(one_grad)
    token = None
    total = None
    for image in range(images):
        grad = starting_grad[image * PAD_D : (image + 1) * PAD_D]
        chosen = selector(keep_ref, image)
        hidden_patch = 1.0 - jnp.sum(chosen, axis=1, keepdims=True)
        term = column_sum(hidden_patch * grad)
        token = term if token is None else token + term
        total = grad if total is None else total + grad
        lifted_ref[image * PAD_E : (image + 1) * PAD_E, :] = low(left_product(low(chosen), low(grad)))
    pos_ref[...] = total
    lifted_grad = lifted_ref[...]
    sums_ref[0:1] = column_sum(lifted_grad)
    sums_ref[1:2] = token
    handed = right_product(lifted_grad, bridge_ref[...])
    enc_cot_ref[...] = low(handed * live_rows(count_ref[0], images * PAD_E, PAD_E))


def enc_hidden_back_kernel(cot_ref, slope_ref, fc1_ref, fc2_ref, part_ref, up_ref):
    up_grad = low(full(slope_ref[...]) * right_product(cot_ref[...], fc2_ref[...]))
    up_ref[...] = up_grad
    part_ref[...] = low(right_product(up_grad, fc1_ref[...]))


def enc_attend_back_kernel(
    images, head_size, middle_ref, cot_ref, part_in_ref, other_ref, vec_ref, proj_ref, weights_ref,
    qkv_ref, out_w_ref, up_ref,
    part_ref, middle_grad_ref, middle_low_ref, stacked_ref, sums_ref, bias_sum_ref, up_sum_ref,
):
    vec = full(vec_ref[...])
    cot = full(cot_ref[...])
    two_grad = pair(part_in_ref[...], other_ref[...])
    xhat, middle_grad = attention_back(
        images, PAD_E, True, head_size, middle_ref[...], cot, two_grad, vec[3:4],
        proj_ref, weights_ref, qkv_ref, out_w_ref, part_ref, middle_grad_ref, middle_low_ref, stacked_ref,
    )
    sums_ref[0:1] = column_sum(middle_grad)
    sums_ref[1:2] = column_sum(two_grad * xhat)
    sums_ref[2:3] = column_sum(two_grad)
    sums_ref[3:4] = column_sum(cot)
    bias_sum_ref[0:1] = column_sum(stacked_ref[0])
    bias_sum_ref[1:2] = column_sum(stacked_ref[2])
    up_sum_ref[...] = column_sum(up_ref[...])


def enc_start_back_kernel(
    images, x_ref, part_ref, other_ref, vec_ref, middle_grad_ref, grad_in_ref, sums_ref,
):
    vec = full(vec_ref[...])
    one_grad = pair(part_ref[...], other_ref[...])
    xhat, scale = normalize(full(x_ref[...]))
    grad = middle_grad_ref[...] + norm_back(one_grad, vec[0:1], xhat, scale)
    take = full(one_hot_rows(PAD_E, VIS, images, True))
    grad_in_ref[...] = jnp.dot(take, grad, preferred_element_type=FULL, precision=lax.Precision.HIGHEST)
    sums_ref[0:1] = column_sum(one_grad * xhat)
    sums_ref[1:2] = column_sum(one_grad)


def chunk(index, size):
    return pl.ds(pl.multiple_of(index * size, LANES), size)


def dec_hidden_weights_kernel(place_ref, hidden_ref, out_low_ref, normed_ref, up_ref, keep_ref, send_ref):
    core = place_ref[0]
    rows, cols = hidden_ref.shape[1] // 2, out_low_ref.shape[1]
    half = normed_ref.shape[1] // 2
    for ref, index in ((send_ref, 1 - core), (keep_ref, core)):
        ref[0] = low(left_product(hidden_ref[:, chunk(index, rows)], out_low_ref[...]))
        up = low(left_product(normed_ref[:, chunk(index, half)], up_ref[...]))
        ref[1, :half] = up[:, :cols]
        ref[1, half:] = up[:, cols:]


def head_blocks(normed, stacked, mix, middle_low, core, side):
    half = normed[0].shape[1] // 2
    wide = middle_low[0].shape[1] // 2
    left = jnp.concatenate([ref[:, chunk(core, half)] for ref in normed], axis=0)

    def across(j):
        return jnp.concatenate([ref[j] for ref in stacked], axis=0)

    if side == 0:
        return low(left_product(left, across(0))), low(left_product(left, across(1)))
    out = left_product(
        jnp.concatenate([ref[...] for ref in mix], axis=0),
        jnp.concatenate([ref[:, chunk(core, wide)] for ref in middle_low], axis=0),
    )
    return low(left_product(left, across(2))), low(out)


def dec_head_weights_kernel(
    place_ref, normed_ref, stacked_ref, mix_ref, middle_low_ref, keep_ref, send_ref
):
    core = place_ref[0]
    width = mix_ref.shape[1]
    for ref, index in ((send_ref, 1 - core), (keep_ref, core)):
        for side in range(2):
            first, second = head_blocks(
                [normed_ref], [stacked_ref], [mix_ref], [middle_low_ref], index, side
            )
            ref[side, :, :width] = first
            ref[side, :, width:] = second


def dec_bridge_weights_kernel(
    place_ref, enc_pad_ref, lifted_ref, pos_ref, sums_ref, middle_sums_ref, out_sum_ref, up_sum_ref,
    bias_sum_ref, keep_ref, send_ref, small_ref,
):
    core = place_ref[0]
    cols = lifted_ref.shape[1]
    bridge = low(left_product(enc_pad_ref[...], lifted_ref[...]))
    quarter = bridge.shape[0] // 4
    small_ref[...] = jnp.zeros_like(small_ref)
    small_ref[0:PAD_D] = pos_ref[...]
    row = PAD_D
    for ref, count in ((sums_ref, 4), (middle_sums_ref, 3), (out_sum_ref, 1)):
        small_ref[row : row + count] = ref[...]
        row += count
    for piece in range(up_sum_ref.shape[1] // cols):
        small_ref[row : row + 1] = up_sum_ref[:, piece * cols : (piece + 1) * cols]
        row += 1
    per_row = cols // bias_sum_ref.shape[1]
    for piece in range(2):
        place = piece % per_row * bias_sum_ref.shape[1]
        small_ref[row + piece // per_row : row + piece // per_row + 1, place : place + bias_sum_ref.shape[1]] = (
            bias_sum_ref[piece : piece + 1]
        )
    few = small_ref.shape[0] // 4
    for side in range(2):
        low_part = bridge[side * quarter : (side + 1) * quarter]
        high_part = bridge[(2 + side) * quarter : (3 + side) * quarter]
        low_small = low(small_ref[side * few : (side + 1) * few])
        high_small = low(small_ref[(2 + side) * few : (3 + side) * few])
        first = core == 0
        keep_ref[side, :quarter] = jnp.where(first, low_part, high_part)
        send_ref[side, :quarter] = jnp.where(first, high_part, low_part)
        keep_ref[side, quarter:] = jnp.where(first, low_small, high_small)
        send_ref[side, quarter:] = jnp.where(first, high_small, low_small)


def enc_hidden_weights_kernel(
    place_ref, hidden_a, hidden_b, cot_a, cot_b, normed_a, normed_b, up_a, up_b, keep_ref, send_ref
):
    core, side = place_ref[0], place_ref[1]
    half = hidden_a.shape[1] // 2

    def both(first, second, lanes=slice(None)):
        return jnp.concatenate([first[:, lanes], second[:, lanes]], axis=0)

    @pl.when(side == 0)
    def _():
        for ref, index in ((send_ref, 1 - core), (keep_ref, core)):
            ref[...] = low(left_product(both(hidden_a, hidden_b, chunk(index, half)), both(cot_a, cot_b)))

    @pl.when(side == 1)
    def _():
        for ref, index in ((send_ref, 1 - core), (keep_ref, core)):
            ref[...] = low(left_product(both(normed_a, normed_b), both(up_a, up_b, chunk(index, half))))


def enc_head_weights_kernel(
    place_ref, normed_a, normed_b, stacked_a, stacked_b, mix_a, mix_b, middle_a, middle_b, keep_ref, send_ref
):
    core = place_ref[0]
    width = mix_a.shape[1]
    for wanted in range(2):

        @pl.when(place_ref[1] == wanted)
        def _(wanted=wanted):
            for ref, index in ((send_ref, 1 - core), (keep_ref, core)):
                first, second = head_blocks(
                    [normed_a, normed_b], [stacked_a, stacked_b], [mix_a, mix_b], [middle_a, middle_b],
                    index, wanted,
                )
                ref[:, :width] = first
                ref[:, width:] = second


def fold_kernel(place_ref, keep_ref, other_ref, mine_ref, theirs_ref):
    side = place_ref[1]
    mine_ref[...] = low(pair(keep_ref[side], other_ref[side]))
    theirs_ref[...] = low(pair(keep_ref[1 - side], other_ref[1 - side]))


def blocks_of(place_ref, refs, rows=slice(None), lanes=slice(None)):
    core, side = place_ref[0], place_ref[1]
    mine, across, over, over_across = (full(ref[rows, lanes]) for ref in refs)
    here = [jnp.where(side == 0, mine, across), jnp.where(side == 0, across, mine)]
    there = [jnp.where(side == 0, over, over_across), jnp.where(side == 0, over_across, over)]
    return [
        [jnp.where(core == 0, here[d], there[d]) for d in range(2)],
        [jnp.where(core == 0, there[d], here[d]) for d in range(2)],
    ]


def dec_hidden_whole_kernel(place_ref, *refs):
    fc1_ref, fc2_ref = refs[4:]
    found = blocks_of(place_ref, refs[:4])
    rows, cols = found[0][0].shape
    half = fc1_ref.shape[0] // 2
    for core in range(2):
        fc2_ref[core * rows : (core + 1) * rows] = found[core][0]
        fc1_ref[core * half : (core + 1) * half, :cols] = found[core][1][:half]
        fc1_ref[core * half : (core + 1) * half, cols:] = found[core][1][half:]


def head_whole_kernel(place_ref, *refs):
    qkv_ref, out_w_ref = refs[4:]
    found = blocks_of(place_ref, refs[:4])
    rows = qkv_ref.shape[1] // 2
    width = qkv_ref.shape[2]
    wide = out_w_ref.shape[1] // 2
    for core in range(2):
        here = slice(core * rows, (core + 1) * rows)
        qkv_ref[0, here] = found[core][0][:, :width]
        qkv_ref[1, here] = found[core][0][:, width:]
        qkv_ref[2, here] = found[core][1][:, :width]
        out_w_ref[:, core * wide : (core + 1) * wide] = found[core][1][:, width:]


def dec_bridge_whole_kernel(place_ref, *refs):
    bridge_ref, small_ref = refs[4:]
    found = blocks_of(place_ref, refs[:4])
    quarter, few = bridge_ref.shape[0] // 4, small_ref.shape[0] // 4
    for core in range(2):
        for side in range(2):
            index = 2 * core + side
            bridge_ref[index * quarter : (index + 1) * quarter] = found[core][side][:quarter]
            small_ref[index * few : (index + 1) * few] = found[core][side][quarter:]


def enc_hidden_whole_kernel(place_ref, *refs):
    fc1_ref, fc2_ref = refs[-2:]
    half = fc1_ref.shape[0]
    row = 0
    for part in range(len(refs[:-2]) // 4):
        found = blocks_of(place_ref, refs[4 * part : 4 * part + 4])
        rows = found[0][0].shape[0]
        for core in range(2):
            fc2_ref[core * half + row : core * half + row + rows] = found[core][0]
            fc1_ref[row : row + rows, core * half : (core + 1) * half] = found[core][1]
        row += rows


def line_sum(value, length):
    if length == 4:
        inward = [(0, 2), (1, 3), (6, 4), (7, 5)]
        middle = [(2, 4), (4, 2), (3, 5), (5, 3)]
        outward = [(2, 0), (3, 1), (4, 6), (5, 7)]
        place = lax.axis_index("dp") // 2
        inner = (place == 1) | (place == 2)
        value = low(pair(value, lax.ppermute(value, "dp", inward)))
        value = low(pair(value, lax.ppermute(value, "dp", middle)))
        return jnp.where(inner, value, lax.ppermute(value, "dp", outward))
    step = 1
    while step < length:
        partner = [(i, i ^ (2 * step)) for i in range(2 * length)]
        value = low(pair(value, lax.ppermute(value, "dp", partner)))
        step *= 2
    return value


def spread_block(block):
    across = swap(block, "dp")
    return block, across, swap(block, "section"), swap(across, "section")


def small_total(value):
    value = low(value)
    groups = lax.axis_size("dp")
    value = low(pair(value, swap(value, "section")))
    step = 1
    while step < groups:
        partner = [(i, i ^ step) for i in range(groups)]
        value = low(pair(value, lax.ppermute(value, "dp", partner)))
        step *= 2
    return full(value)


def pick(stacked, index):
    return lax.dynamic_index_in_dim(stacked, index, 0, keepdims=False)


def body(
    enc_in, keep_index, image_count, enc_vec, enc_qkv, enc_qv_bias, enc_out_w, enc_fc1, enc_fc1_bias, enc_fc2,
    bridge_w, dec_vec, dec_pos, dec_qkv, dec_qv_bias, dec_out_w, dec_fc1, dec_fc1_bias, dec_fc2, dec_cot,
):
    core = lax.axis_index("section")
    groups = lax.axis_size("dp")
    place = jnp.stack([core, lax.axis_index("dp") % 2]).astype(jnp.int32)
    images = keep_index.shape[1]
    enc_width, dec_width = bridge_w.shape
    enc_local, dec_local = enc_qkv.shape[2], dec_qkv.shape[2]
    enc_size, dec_size = enc_width // HE, dec_width // HD
    enc_mlp, dec_mlp = enc_fc1.shape[1], dec_fc1.shape[1]
    rows_e, rows_d = images * PAD_E, images * PAD_D
    enc_groups, dec_groups = enc_local // LANES, dec_local // LANES
    enc_heads, dec_heads = LANES // enc_size, LANES // dec_size
    enc_qkv, dec_qkv = jnp.transpose(enc_qkv, (1, 0, 2)), jnp.transpose(dec_qkv, (1, 0, 2))
    enc_fc1_bias, dec_fc1_bias = enc_fc1_bias[None], dec_fc1_bias[None]
    own_in = pick(enc_in, core)
    keep = jnp.pad(pick(keep_index, core), ((0, 0), (0, PAD_E - VIS)), constant_values=-1)
    cot = pick(dec_cot, core)
    count = pick(image_count, core)
    dec_rows = images * PATCHES

    def enc_attend(rows):
        return kernel_call(
            functools.partial(enc_attend_kernel, images, enc_size),
            [
                shaped((rows_e, enc_width)),
                shaped((rows_e, enc_width)),
                shaped((rows_e, enc_width)),
                shaped((3, rows_e, enc_local)),
                shaped((enc_groups, enc_heads * rows_e, rows_e)),
                shaped((rows_e, enc_local)),
            ],
            rows, enc_vec, enc_qkv, enc_qv_bias, enc_out_w,
            name="enc_attend",
        )

    def enc_hidden(x, part):
        return kernel_call(
            enc_hidden_kernel,
            [
                shaped((rows_e, enc_width)),
                shaped((rows_e, enc_width), FULL),
                shaped((rows_e, enc_width)),
                shaped((rows_e, enc_mlp)),
                shaped((rows_e, enc_mlp)),
            ],
            x, enc_vec, part, swap(part, "tensor"), enc_fc1, enc_fc1_bias, enc_fc2,
            name="enc_hidden",
        )

    side_in = swap(own_in, "dp")
    first = enc_attend(own_in)
    second = enc_hidden(first[1], first[0])
    other_first = enc_attend(side_in)
    other_second = enc_hidden(other_first[1], other_first[0])

    dec_a = kernel_call(
        functools.partial(dec_attend_kernel, images, dec_size),
        [
            shaped((rows_d, dec_width)),
            shaped((images * VIS, enc_width)),
            shaped((rows_e, enc_width)),
            shaped((rows_d, dec_width), FULL),
            shaped((rows_d, dec_width)),
            shaped((3, rows_d, dec_local)),
            shaped((images * dec_groups, dec_heads * PAD_D, PAD_D)),
            shaped((rows_d, dec_local)),
        ],
        count, keep, second[1], second[0], swap(second[0], "tensor"), enc_vec, bridge_w,
        dec_vec, dec_pos, dec_qkv, dec_qv_bias, dec_out_w,
        scalars=1, name="dec_attend",
    )
    dec_part, enc_out, enc_pad, starting, dec_normed, dec_proj, dec_weights, dec_mix = dec_a
    enc_out_over = swap(enc_out, "section")
    enc_out_both = jnp.stack(
        [jnp.where(core == 0, enc_out, enc_out_over), jnp.where(core == 0, enc_out_over, enc_out)]
    )
    dec_b = kernel_call(
        functools.partial(dec_hidden_kernel, images),
        [
            shaped((rows_d, dec_width)),
            shaped((rows_d, dec_width)),
            shaped((rows_d, dec_width), FULL),
            shaped((rows_d, dec_width)),
            shaped((rows_d, dec_mlp)),
            shaped((rows_d, dec_width)),
            shaped((rows_d, dec_mlp)),
            shaped((1, dec_mlp), FULL),
            shaped((1, dec_width), FULL),
        ],
        count, starting, dec_part, swap(dec_part, "tensor"), dec_vec, dec_fc1, dec_fc1_bias, dec_fc2, cot,
        scalars=1, name="dec_hidden",
    )
    part_back, part_two, dec_middle, dec_normed_two, dec_hid, out_low, dec_up, up_sum, out_sum = dec_b

    part_back_other = swap(part_back, "tensor")
    part_two_other = swap(part_two, "tensor")
    d1 = kernel_call(
        dec_hidden_weights_kernel,
        [shaped((2, dec_mlp // 2, dec_width))] * 2,
        place, dec_hid, out_low, dec_normed_two, dec_up,
        scalars=1, name="dec_hidden_weights",
    )
    dec_c = kernel_call(
        functools.partial(dec_attend_back_kernel, images, dec_size),
        [
            shaped((rows_d, dec_width)),
            shaped((rows_d, dec_width), FULL),
            shaped((rows_d, dec_width)),
            shaped((3, rows_d, dec_local)),
            shaped((3, dec_width), FULL),
            shaped((2, dec_local), FULL),
        ],
        dec_middle, out_low, part_back, part_back_other, dec_vec, dec_proj, dec_weights, dec_qkv, dec_out_w,
        name="dec_attend_back",
    )
    dec_part_one, dec_middle_grad, dec_middle_low, dec_stacked, middle_sums, dec_bias_sum = dec_c
    dec_part_one_other = swap(dec_part_one, "tensor")
    d2 = kernel_call(
        dec_head_weights_kernel,
        [shaped((2, dec_width // 2, 2 * dec_local))] * 2,
        place, dec_normed, dec_stacked, dec_mix, dec_middle_low,
        scalars=1, name="dec_head_weights",
    )
    dec_d = kernel_call(
        functools.partial(dec_start_back_kernel, images),
        [
            shaped((rows_e, enc_width)),
            shaped((rows_e, dec_width)),
            shaped((PAD_D, dec_width), FULL),
            shaped((4, dec_width), FULL),
        ],
        count, keep, starting, dec_part_one, dec_part_one_other, dec_vec, dec_middle_grad, bridge_w,
        scalars=1, name="dec_start_back",
    )
    enc_cot, lifted_grad, pos_grad, start_sums = dec_d
    side_cot = swap(enc_cot, "dp")
    small_rows = 256

    def enc_hidden_back(rows, slope):
        return kernel_call(
            enc_hidden_back_kernel,
            [shaped((rows_e, enc_width)), shaped((rows_e, enc_mlp))],
            rows, slope, enc_fc1, enc_fc2,
            name="enc_hidden_back",
        )

    def enc_attend_back(rows, part, up, kept, kept_two):
        return kernel_call(
            functools.partial(enc_attend_back_kernel, images, enc_size),
            [
                shaped((rows_e, enc_width)),
                shaped((rows_e, enc_width), FULL),
                shaped((rows_e, enc_width)),
                shaped((3, rows_e, enc_local)),
                shaped((4, enc_width), FULL),
                shaped((2, enc_local), FULL),
                shaped((1, enc_mlp), FULL),
            ],
            kept_two[1], rows, part, swap(part, "tensor"), enc_vec, kept[3], kept[4], enc_qkv, enc_out_w, up,
            name="enc_attend_back",
        )

    part, up = enc_hidden_back(enc_cot, second[4])
    d3 = pl.pallas_call(
        dec_bridge_weights_kernel,
        out_shape=[jax.ShapeDtypeStruct((2, enc_width // 4 + small_rows // 4, dec_width), LOW)] * 2,
        in_specs=[pl.BlockSpec(memory_space=pltpu.SMEM)] + [pl.BlockSpec(memory_space=pltpu.VMEM)] * 8,
        out_specs=[pl.BlockSpec(memory_space=pltpu.VMEM)] * 2,
        scratch_shapes=[pltpu.VMEM((small_rows, dec_width), FULL)],
        compiler_params=pltpu.CompilerParams(vmem_limit_bytes=40 * MIB),
        name="dec_bridge_weights",
    )(place, enc_pad, lifted_grad, pos_grad, start_sums, middle_sums, out_sum, up_sum, dec_bias_sum)
    other_part, other_up = enc_hidden_back(side_cot, other_second[4])
    back = enc_attend_back(enc_cot, part, up, first, second)
    other_back = enc_attend_back(side_cot, other_part, other_up, other_first, other_second)
    e1 = kernel_call(
        enc_hidden_weights_kernel,
        [shaped((enc_mlp // 2, enc_width))] * 2,
        place, second[3], other_second[3], enc_cot, side_cot, second[2], other_second[2], up, other_up,
        scalars=1, name="enc_hidden_weights",
    )
    e2 = kernel_call(
        enc_head_weights_kernel,
        [shaped((enc_width // 2, 2 * enc_local))] * 2,
        place, first[2], other_first[2], back[3], other_back[3], first[5], other_first[5], back[2], other_back[2],
        scalars=1, name="enc_head_weights",
    )
    grad_in, enc_sums = kernel_call(
        functools.partial(enc_start_back_kernel, images),
        [shaped((images * VIS, enc_width), FULL), shaped((2, enc_width), FULL)],
        first[1], back[0], swap(back[0], "tensor"), enc_vec, back[1],
        name="enc_start_back",
    )
    enc_small = jnp.concatenate(
        [
            enc_sums,
            back[4],
            back[6].reshape(-1, enc_width),
            back[5].reshape(-1, enc_width),
        ],
        axis=0,
    )
    enc_small_rows = enc_small.shape[0]
    enc_small = small_total(jnp.pad(enc_small, ((0, -enc_small_rows % 16), (0, 0))))

    def dec_sum(keep_send):
        mine, theirs = kernel_call(
            fold_kernel,
            [shaped(keep_send[0].shape[1:])] * 2,
            place, keep_send[0], swap(keep_send[1], "section"),
            scalars=1, name="fold",
        )
        return line_sum(low(pair(mine, swap(theirs, "dp"))), groups // 2)

    def enc_sum(keep_send, pieces):
        total = low(pair(keep_send[0], swap(keep_send[1], "section")))
        rows = total.shape[0] // pieces
        return [line_sum(total[i * rows : (i + 1) * rows], groups // 2) for i in range(pieces)]

    g_dec_fc1, g_dec_fc2 = kernel_call(
        dec_hidden_whole_kernel,
        [shaped(dec_fc1.shape, FULL), shaped(dec_fc2.shape, FULL)],
        place, *spread_block(dec_sum(d1)), scalars=1, name="dec_hidden_whole",
    )
    g_dec_qkv, g_dec_out_w = kernel_call(
        head_whole_kernel,
        [shaped(dec_qkv.shape, FULL), shaped(dec_out_w.shape, FULL)],
        place, *spread_block(dec_sum(d2)), scalars=1, name="dec_head_whole",
    )
    g_bridge, dec_small = kernel_call(
        dec_bridge_whole_kernel,
        [shaped(bridge_w.shape, FULL), shaped((small_rows, dec_width), FULL)],
        place, *spread_block(dec_sum(d3)), scalars=1, name="dec_bridge_whole",
    )
    pieces = []
    for piece in enc_sum(e1, 4):
        pieces += spread_block(piece)
    g_enc_fc1, g_enc_fc2 = kernel_call(
        enc_hidden_whole_kernel,
        [shaped(enc_fc1.shape, FULL), shaped(enc_fc2.shape, FULL)],
        place, *pieces, scalars=1, name="enc_hidden_whole",
    )
    g_enc_qkv, g_enc_out_w = kernel_call(
        head_whole_kernel,
        [shaped(enc_qkv.shape, FULL), shaped(enc_out_w.shape, FULL)],
        place, *spread_block(enc_sum(e2, 1)[0]), scalars=1, name="enc_head_whole",
    )
    (dec_out,) = kernel_call(
        functools.partial(dec_out_kernel, images),
        [shaped((dec_rows, dec_width))],
        count, dec_middle, part_two, part_two_other, dec_vec,
        scalars=1, name="dec_out",
    )

    g_enc_vec = enc_small[:6]
    bias_rows = enc_mlp // enc_width
    g_enc_fc1_bias = enc_small[6 : 6 + bias_rows].reshape(-1)
    g_enc_qv_bias = enc_small[6 + bias_rows : enc_small_rows].reshape(2, -1)
    g_dec_pos = dec_small[:PATCHES]
    base = PAD_D
    g_dec_vec = dec_small[base : base + 8]
    bias_rows = dec_mlp // dec_width
    g_dec_fc1_bias = dec_small[base + 8 : base + 8 + bias_rows].reshape(-1)
    qv_rows = 2 * dec_local // dec_width
    g_dec_qv_bias = dec_small[base + 8 + bias_rows : base + 8 + bias_rows + qv_rows].reshape(2, -1)
    return (
        enc_out_both,
        dec_out[None],
        grad_in[None],
        g_enc_vec,
        jnp.transpose(g_enc_qkv, (1, 0, 2)),
        g_enc_qv_bias,
        g_enc_out_w,
        g_enc_fc1,
        g_enc_fc1_bias,
        g_enc_fc2,
        g_bridge,
        g_dec_vec,
        g_dec_pos,
        jnp.transpose(g_dec_qkv, (1, 0, 2)),
        g_dec_qv_bias,
        g_dec_out_w,
        g_dec_fc1,
        g_dec_fc1_bias,
        g_dec_fc2,
    )


def solution(mesh):
    return jax.shard_map(
        body,
        mesh=mesh,
        in_specs=(
            P(None, "dp", None),
            P(None, "dp", None),
            P(None, "dp"),
            P(),
            P(None, None, "tensor"),
            P(None, "tensor"),
            P("tensor", None),
            P(None, "tensor"),
            P("tensor"),
            P("tensor", None),
            P(),
            P(),
            P(),
            P(None, None, "tensor"),
            P(None, "tensor"),
            P("tensor", None),
            P(None, "tensor"),
            P("tensor"),
            P("tensor", None),
            P(None, "dp", None),
        ),
        out_specs=(
            P(None, "dp", None),
            P("section", "dp", None),
            P("section", "dp", None),
            P(),
            P(None, None, "tensor"),
            P(None, "tensor"),
            P("tensor", None),
            P(None, "tensor"),
            P("tensor"),
            P("tensor", None),
            P(),
            P(),
            P(),
            P(None, None, "tensor"),
            P(None, "tensor"),
            P("tensor", None),
            P(None, "tensor"),
            P("tensor"),
            P("tensor", None),
        ),
        check_vma=False,
    )
```

```python
import functools
import math

import jax
import jax.numpy as jnp
from jax import lax
from jax.experimental import pallas as pl
from jax.experimental.pallas import tpu as pltpu
from jax.sharding import PartitionSpec as P

HE = 12
HD = 16
PATCHES = 196
VIS = 49
PAD_E = 64
PAD_D = 208
LANES = 128
EPSILON = 1e-06
LOW = jnp.bfloat16
FULL = jnp.float32
MIB = 2**20


def low(values):
    return values.astype(LOW)


def full(values):
    return values.astype(FULL)


def matmul(left, right):
    return jnp.dot(left, right, preferred_element_type=FULL)


def left_product(left, right):
    return lax.dot_general(left, right, (((0,), (0,)), ((), ())), preferred_element_type=FULL)


def right_product(left, right):
    return lax.dot_general(left, right, (((1,), (1,)), ((), ())), preferred_element_type=FULL)


def pair(first, second):
    return full(first) + full(second)


def swap(value, axis):
    return lax.ppermute(value, axis, [(i, i ^ 1) for i in range(lax.axis_size(axis))])


def normalize(values):
    center = values - jnp.mean(values, axis=-1, keepdims=True)
    scale = lax.rsqrt(jnp.mean(center * center, axis=-1, keepdims=True) + EPSILON)
    return center * scale, scale


def norm_back(grad, gain, xhat, scale):
    inner = grad * gain
    return scale * (
        inner
        - jnp.mean(inner, axis=-1, keepdims=True)
        - xhat * jnp.mean(inner * xhat, axis=-1, keepdims=True)
    )


def column_sum(values):
    return jnp.sum(full(values), axis=0, keepdims=True)


def one_hot_rows(padded, length, images, packed_first=False):
    shape = (images * length, images * padded) if packed_first else (images * padded, images * length)
    first = lax.broadcasted_iota(jnp.int32, shape, 0)
    second = lax.broadcasted_iota(jnp.int32, shape, 1)
    packed, wide = (first, second) if packed_first else (second, first)
    hit = None
    for image in range(images):
        here = (
            (packed >= image * length)
            & (packed < (image + 1) * length)
            & (wide - image * padded == packed - image * length)
        )
        hit = here if hit is None else hit | here
    return low(jnp.where(hit, 1.0, 0.0))


def head_masks(head_size):
    lane = lax.broadcasted_iota(jnp.int32, (1, LANES), 1)
    return [
        jnp.where((lane >= j * head_size) & (lane < (j + 1) * head_size), 1.0, 0.0)
        for j in range(LANES // head_size)
    ]


def spread_heads(values, masks):
    wide = full(values)
    return jnp.concatenate([low(wide * mask) for mask in masks], axis=0)


def gather_heads(stacked, masks):
    rows = stacked.shape[0] // len(masks)
    total = None
    for j, mask in enumerate(masks):
        term = stacked[j * rows : (j + 1) * rows] * mask
        total = term if total is None else total + term
    return total


def attend(queries, key_rows, value_rows, masks, allowed, factor):
    scores = right_product(spread_heads(queries, masks), key_rows) * factor
    scores = jnp.where(allowed, scores, -1e30)
    exponent = jnp.exp(scores - jnp.max(scores, axis=-1, keepdims=True))
    weights_low = low(exponent * (1.0 / jnp.sum(exponent, axis=-1, keepdims=True)))
    return weights_low, low(gather_heads(matmul(weights_low, value_rows), masks))


def attend_back(queries, key_rows, value_rows, weights_low, upstream, masks, factor):
    spread_up = spread_heads(upstream, masks)
    weight_grad = right_product(spread_up, value_rows)
    weights = full(weights_low)
    product = weights * weight_grad
    score_grad = low(product - weights * jnp.sum(product, axis=-1, keepdims=True))
    query_grad = gather_heads(matmul(score_grad, key_rows), masks) * factor
    key_grad = left_product(score_grad, spread_heads(queries, masks)) * factor
    value_grad = left_product(weights_low, spread_up)
    return low(query_grad), low(key_grad), low(value_grad)


def same_image(heads, images, padded, length):
    shape = (heads * images * padded, images * padded)
    row = lax.broadcasted_iota(jnp.int32, shape, 0)
    key = lax.broadcasted_iota(jnp.int32, shape, 1)
    hit = None
    for head in range(heads):
        for image in range(images):
            start = (head * images + image) * padded
            here = (
                (row >= start)
                & (row < start + padded)
                & (key >= image * padded)
                & (key < image * padded + length)
            )
            hit = here if hit is None else hit | here
    return hit


def live_rows(count, rows, padded):
    row = lax.broadcasted_iota(jnp.int32, (rows, 1), 0)
    return jnp.where(row < count * padded, 1.0, 0.0)


def kernel_call(order, kernel, outs, *arguments, scalars=0, scratch=(), name=None):
    count = len(arguments)
    before = order[-1:]

    def run(*refs):
        mark = count + len(before) + len(outs)
        refs[mark][...] = jnp.zeros((8, LANES), FULL)
        kernel(*refs[:count], *refs[count + len(before) : mark], *refs[mark + 1 :])

    specs = [pl.BlockSpec(memory_space=pltpu.SMEM)] * scalars
    specs += [pl.BlockSpec(memory_space=pltpu.VMEM)] * (count - scalars)
    specs += [pl.BlockSpec(memory_space=pl.ANY)] * len(before)
    results = pl.pallas_call(
        run,
        out_shape=[jax.ShapeDtypeStruct(x.shape, x.dtype) for x in outs] + [shaped((8, LANES), FULL)],
        in_specs=specs,
        out_specs=[pl.BlockSpec(memory_space=pltpu.VMEM)] * (len(outs) + 1),
        scratch_shapes=scratch,
        compiler_params=pltpu.CompilerParams(vmem_limit_bytes=24 * MIB),
        cost_estimate=pl.CostEstimate(flops=2 * 10**11, bytes_accessed=1, transcendentals=0),
        name=name,
    )(*arguments, *before)
    order.append(results[-1])
    return results[:-1]


def shaped(shape, dtype=LOW):
    return jax.ShapeDtypeStruct(shape, dtype)


def project_heads(normed, qkv_ref, bias, proj_ref, width):
    queries = low(matmul(normed, qkv_ref[0]) + bias[0:1])
    key_rows = low(matmul(normed, qkv_ref[1]))
    value_rows = low(matmul(normed, qkv_ref[2]) + bias[1:2])
    proj_ref[0] = queries
    proj_ref[1] = key_rows
    proj_ref[2] = value_rows


def enc_attend_kernel(
    images, head_size, place_ref, x_ref, vec_ref, qkv_ref, bias_ref, out_w_ref,
    part_ref, x_out_ref, normed_ref, proj_ref, weights_ref, mix_ref,
):
    width = qkv_ref.shape[2]
    if len(x_ref.shape) == 2:
        rows = x_ref[...]
    else:
        rows = low(jnp.where(place_ref[0] == 0, full(x_ref[:, 0, :]), full(x_ref[:, 1, :])))
    x = matmul(one_hot_rows(PAD_E, VIS, images), rows)
    x_out_ref[...] = low(x)
    vec = full(vec_ref[...])
    xhat, _ = normalize(x)
    normed = low(xhat * vec[0:1] + vec[1:2])
    normed_ref[...] = normed
    project_heads(normed, qkv_ref, full(bias_ref[...]), proj_ref, width)
    masks = head_masks(head_size)
    allowed = same_image(len(masks), images, PAD_E, VIS)
    for group in range(width // LANES):
        lanes = slice(group * LANES, (group + 1) * LANES)
        weights_low, mixture = attend(
            proj_ref[0, :, lanes],
            proj_ref[1, :, lanes],
            proj_ref[2, :, lanes],
            masks,
            allowed,
            1.0 / math.sqrt(head_size),
        )
        weights_ref[group] = weights_low
        mix_ref[:, lanes] = mixture
    part_ref[...] = low(matmul(mix_ref[...], out_w_ref[...]))


def mlp_forward(middle, gain, shift, fc1_ref, bias_ref, fc2_ref, normed_ref, hidden_ref, slope_ref):
    xhat, _ = normalize(middle)
    normed = low(xhat * gain + shift)
    normed_ref[...] = normed
    pre = matmul(normed, fc1_ref[...]) + full(bias_ref[...])
    share = 0.5 + 0.5 * lax.erf(pre * math.sqrt(0.5))
    hidden = low(pre * share)
    hidden_ref[...] = hidden
    slope = share + pre * jnp.exp(-0.5 * pre * pre) * (1.0 / math.sqrt(2.0 * math.pi))
    if slope_ref is not None:
        slope_ref[...] = low(slope)
    return None if fc2_ref is None else low(matmul(hidden, fc2_ref[...])), slope


def enc_hidden_kernel(
    x_ref, vec_ref, part_ref, other_ref, fc1_ref, bias_ref, fc2_ref,
    part_two_ref, middle_ref, normed_ref, hidden_ref, slope_ref,
):
    vec = full(vec_ref[...])
    middle = full(x_ref[...]) + pair(part_ref[...], other_ref[...]) + vec[2:3]
    middle_ref[...] = middle
    part, _ = mlp_forward(
        middle, vec[3:4], vec[4:5], fc1_ref, bias_ref, fc2_ref, normed_ref, hidden_ref, slope_ref
    )
    part_two_ref[...] = part


def enc_side_hidden_kernel(
    x_ref, vec_ref, part_ref, other_ref, fc1_ref, bias_ref,
    middle_ref, normed_ref, hidden_ref, slope_ref,
):
    vec = full(vec_ref[...])
    middle = full(x_ref[...]) + pair(part_ref[...], other_ref[...]) + vec[2:3]
    middle_ref[...] = middle
    mlp_forward(middle, vec[3:4], vec[4:5], fc1_ref, bias_ref, None, normed_ref, hidden_ref, slope_ref)


def both_cores_kernel(place_ref, own_ref, over_ref, both_ref):
    first = place_ref[0] == 0
    own, over = full(own_ref[...]), full(over_ref[...])
    both_ref[:, 0, :] = low(jnp.where(first, own, over))
    both_ref[:, 1, :] = low(jnp.where(first, over, own))


def selector(keep_ref, image):
    patch = lax.broadcasted_iota(jnp.int32, (PAD_D, PAD_E), 0)
    return jnp.where(patch == keep_ref[image : image + 1, :], 1.0, 0.0)


def dec_attend_kernel(
    images, head_size, count_ref, keep_ref, middle_ref, part_ref, other_ref, enc_vec_ref, bridge_ref,
    vec_ref, pos_ref, qkv_ref, bias_ref, out_w_ref,
    part_out_ref, enc_out_ref, enc_pad_ref, starting_ref, normed_ref, proj_ref, weights_ref, mix_ref,
):
    width = qkv_ref.shape[2]
    vec = full(vec_ref[...])
    encoded = middle_ref[...] + pair(part_ref[...], other_ref[...]) + full(enc_vec_ref[...])[5:6]
    enc_pad = low(encoded * live_rows(count_ref[0], images * PAD_E, PAD_E))
    enc_pad_ref[...] = enc_pad
    enc_out_ref[...] = low(matmul(one_hot_rows(PAD_E, VIS, images, True), enc_pad))
    lifted = matmul(enc_pad, bridge_ref[...]) + vec[0:1]
    lifted_high = low(lifted)
    lifted_rest = low(lifted - full(lifted_high))
    pos = matmul(one_hot_rows(PAD_D, PATCHES, 1), pos_ref[...])
    for image in range(images):
        chosen = selector(keep_ref, image)
        rows = slice(image * PAD_E, (image + 1) * PAD_E)
        placed = matmul(low(chosen), lifted_high[rows]) + matmul(low(chosen), lifted_rest[rows])
        hidden_patch = 1.0 - jnp.sum(chosen, axis=1, keepdims=True)
        starting_ref[image * PAD_D : (image + 1) * PAD_D, :] = placed + hidden_patch * vec[1:2] + pos
    xhat, _ = normalize(starting_ref[...])
    normed = low(xhat * vec[2:3] + vec[3:4])
    normed_ref[...] = normed
    project_heads(normed, qkv_ref, full(bias_ref[...]), proj_ref, width)
    masks = head_masks(head_size)
    allowed = lax.broadcasted_iota(jnp.int32, (1, PAD_D), 1) < PATCHES
    groups = width // LANES
    for image in range(images):
        rows = slice(image * PAD_D, (image + 1) * PAD_D)
        for group in range(groups):
            lanes = slice(group * LANES, (group + 1) * LANES)
            weights_low, mixture = attend(
                proj_ref[0, rows, lanes],
                proj_ref[1, rows, lanes],
                proj_ref[2, rows, lanes],
                masks,
                allowed,
                1.0 / math.sqrt(head_size),
            )
            weights_ref[image * groups + group] = weights_low
            mix_ref[rows, lanes] = mixture
    part_out_ref[...] = low(matmul(mix_ref[...], out_w_ref[...]))


def dec_hidden_kernel(
    images, count_ref, starting_ref, part_ref, other_ref, vec_ref, fc1_ref, bias_ref, fc2_ref, cot_ref,
    part_back_ref, part_two_ref, middle_ref, normed_ref, hidden_ref, out_low_ref, up_ref,
    up_sum_ref, out_sum_ref,
):
    vec = full(vec_ref[...])
    middle = starting_ref[...] + pair(part_ref[...], other_ref[...]) + vec[4:5]
    middle_ref[...] = middle
    part, slope = mlp_forward(
        middle, vec[5:6], vec[6:7], fc1_ref, bias_ref, fc2_ref, normed_ref, hidden_ref, None
    )
    part_two_ref[...] = part
    spread = matmul(one_hot_rows(PAD_D, PATCHES, images), cot_ref[...])
    out_low = low(spread * live_rows(count_ref[0], images * PAD_D, PAD_D))
    out_low_ref[...] = out_low
    up_grad = low(slope * right_product(out_low, fc2_ref[...]))
    up_ref[...] = up_grad
    part_back_ref[...] = low(right_product(up_grad, fc1_ref[...]))
    up_sum_ref[...] = column_sum(up_grad)
    out_sum_ref[...] = column_sum(out_low)


def dec_out_kernel(images, count_ref, middle_ref, part_ref, other_ref, vec_ref, out_ref):
    decoded = middle_ref[...] + pair(part_ref[...], other_ref[...]) + full(vec_ref[...])[7:8]
    decoded = low(decoded * live_rows(count_ref[0], images * PAD_D, PAD_D))
    out_ref[...] = low(matmul(one_hot_rows(PAD_D, PATCHES, images, True), decoded))


def attention_back(
    first_row, images, padded, together, head_size, mixture_grad, proj_ref, weights_ref, stacked_ref
):
    masks = head_masks(head_size)
    groups = proj_ref.shape[2] // LANES
    step = images if together else 1
    for first in range(0, images, step):
        rows = slice(first * padded, (first + step) * padded)
        out_rows = slice(first_row + first * padded, first_row + (first + step) * padded)
        for group in range(groups):
            lanes = slice(group * LANES, (group + 1) * LANES)
            grads = attend_back(
                proj_ref[0, rows, lanes],
                proj_ref[1, rows, lanes],
                proj_ref[2, rows, lanes],
                weights_ref[first // step * groups + group],
                mixture_grad[out_rows, lanes],
                masks,
                1.0 / math.sqrt(head_size),
            )
            for j in range(3):
                stacked_ref[j, out_rows, lanes] = grads[j]


def normed_back(stacked_ref, qkv_ref):
    total = right_product(stacked_ref[0], qkv_ref[0])
    for j in (1, 2):
        total = total + right_product(stacked_ref[j], qkv_ref[j])
    return low(total)


def dec_attend_back_kernel(
    images, head_size, middle_ref, out_low_ref, part_in_ref, other_ref, vec_ref, proj_ref, weights_ref,
    qkv_ref, out_w_ref,
    part_ref, middle_grad_ref, middle_low_ref, stacked_ref, sums_ref, bias_sum_ref,
):
    vec = full(vec_ref[...])
    two_grad = pair(part_in_ref[...], other_ref[...])
    xhat, scale = normalize(middle_ref[...])
    middle_grad = full(out_low_ref[...]) + norm_back(two_grad, vec[5:6], xhat, scale)
    middle_grad_ref[...] = middle_grad
    middle_low = low(middle_grad)
    middle_low_ref[...] = middle_low
    mixture_grad = low(right_product(middle_low, out_w_ref[...]))
    attention_back(0, images, PAD_D, False, head_size, mixture_grad, proj_ref, weights_ref, stacked_ref)
    part_ref[...] = normed_back(stacked_ref, qkv_ref)
    sums_ref[0:1] = column_sum(middle_grad)
    sums_ref[1:2] = column_sum(two_grad * xhat)
    sums_ref[2:3] = column_sum(two_grad)
    bias_sum_ref[0:1] = column_sum(stacked_ref[0])
    bias_sum_ref[1:2] = column_sum(stacked_ref[2])


def dec_start_back_kernel(
    images, count_ref, keep_ref, starting_ref, part_ref, other_ref, vec_ref, middle_grad_ref, bridge_ref,
    enc_cot_ref, lifted_ref, pos_ref, sums_ref,
):
    vec = full(vec_ref[...])
    one_grad = pair(part_ref[...], other_ref[...])
    xhat, scale = normalize(starting_ref[...])
    starting_grad = middle_grad_ref[...] + norm_back(one_grad, vec[2:3], xhat, scale)
    sums_ref[2:3] = column_sum(one_grad * xhat)
    sums_ref[3:4] = column_sum(one_grad)
    token = None
    total = None
    for image in range(images):
        grad = starting_grad[image * PAD_D : (image + 1) * PAD_D]
        chosen = selector(keep_ref, image)
        hidden_patch = 1.0 - jnp.sum(chosen, axis=1, keepdims=True)
        term = column_sum(hidden_patch * grad)
        token = term if token is None else token + term
        total = grad if total is None else total + grad
        lifted_ref[image * PAD_E : (image + 1) * PAD_E, :] = low(left_product(low(chosen), low(grad)))
    pos_ref[...] = total
    lifted_grad = lifted_ref[...]
    sums_ref[0:1] = column_sum(lifted_grad)
    sums_ref[1:2] = token
    handed = right_product(lifted_grad, bridge_ref[...])
    enc_cot_ref[...] = low(handed * live_rows(count_ref[0], images * PAD_E, PAD_E))


def enc_hidden_back_kernel(cot_a, cot_b, slope_a, slope_b, fc1_ref, fc2_ref, part_ref, up_ref):
    slope = jnp.concatenate([slope_a[...], slope_b[...]], axis=0)
    up_grad = low(full(slope) * right_product(stacked_rows(cot_a, cot_b), fc2_ref[...]))
    up_ref[...] = up_grad
    part_ref[...] = low(right_product(up_grad, fc1_ref[...]))


def enc_attend_back_kernel(
    images, head_size, middle_a, middle_b, cot_a, cot_b, part_in_ref, other_ref, vec_ref, proj_a, proj_b,
    weights_a, weights_b, qkv_ref, out_w_ref, up_ref,
    part_ref, middle_grad_ref, middle_low_ref, stacked_ref, sums_ref, bias_sum_ref, up_sum_ref,
):
    vec = full(vec_ref[...])
    own = middle_a.shape[0]
    cot = full(stacked_rows(cot_a, cot_b))
    two_grad = pair(part_in_ref[...], other_ref[...])
    xhat, scale = normalize(stacked_rows(middle_a, middle_b))
    middle_grad = cot + norm_back(two_grad, vec[3:4], xhat, scale)
    middle_grad_ref[...] = middle_grad
    middle_low = low(middle_grad)
    middle_low_ref[...] = middle_low
    mixture_grad = low(right_product(middle_low, out_w_ref[...]))
    attention_back(0, images, PAD_E, True, head_size, mixture_grad, proj_a, weights_a, stacked_ref)
    attention_back(own, images, PAD_E, True, head_size, mixture_grad, proj_b, weights_b, stacked_ref)
    part_ref[...] = normed_back(stacked_ref, qkv_ref)
    sums_ref[0:1] = column_sum(middle_grad)
    sums_ref[1:2] = column_sum(two_grad * xhat)
    sums_ref[2:3] = column_sum(two_grad)
    sums_ref[3:4] = column_sum(cot)
    bias_sum_ref[0:1] = column_sum(stacked_ref[0])
    bias_sum_ref[1:2] = column_sum(stacked_ref[2])
    up_sum_ref[...] = column_sum(up_ref[...])


def enc_start_back_kernel(
    images, x_a, x_b, part_ref, other_ref, vec_ref, middle_grad_ref, sums_ref, up_sum_ref, bias_sum_ref,
    grad_in_ref, small_ref, rows_ref,
):
    vec = full(vec_ref[...])
    own = x_a.shape[0]
    one_grad = pair(part_ref[...], other_ref[...])
    xhat, scale = normalize(full(stacked_rows(x_a, x_b)))
    grad = middle_grad_ref[:own] + norm_back(one_grad[:own], vec[0:1], xhat[:own], scale[:own])
    take = full(one_hot_rows(PAD_E, VIS, images, True))
    grad_in_ref[:, 0, :] = jnp.dot(
        take, grad, preferred_element_type=FULL, precision=lax.Precision.HIGHEST
    )
    rows_ref[...] = jnp.zeros_like(rows_ref)
    rows_ref[0:1] = column_sum(one_grad * xhat)
    rows_ref[1:2] = column_sum(one_grad)
    rows_ref[2:6] = sums_ref[...]
    put_rows(rows_ref, 6, up_sum_ref, bias_sum_ref)
    small_ref[...] = low(rows_ref[...])


def chunk(index, size):
    return pl.ds(pl.multiple_of(index * size, LANES), size)


def dec_hidden_weights_kernel(place_ref, hidden_ref, out_low_ref, normed_ref, up_ref, keep_ref, send_ref):
    core = place_ref[0]
    rows, cols = hidden_ref.shape[1] // 2, out_low_ref.shape[1]
    half = normed_ref.shape[1] // 2
    for ref, index in ((send_ref, 1 - core), (keep_ref, core)):
        down = low(left_product(hidden_ref[:, chunk(index, rows)], out_low_ref[...]))
        up = low(left_product(normed_ref[:, chunk(index, half)], up_ref[...]))
        for part in range(2):
            ref[0, part] = down[part * rows // 2 : (part + 1) * rows // 2]
            ref[1, part] = up[:, part * cols : (part + 1) * cols]


def head_blocks(normed, stacked_ref, mix, middle_low_ref, core, side):
    half = normed[0].shape[1] // 2
    wide = middle_low_ref.shape[1] // 2
    left = jnp.concatenate([ref[:, chunk(core, half)] for ref in normed], axis=0)
    if side == 0:
        return low(left_product(left, stacked_ref[0])), low(left_product(left, stacked_ref[1]))
    out = left_product(
        jnp.concatenate([ref[...] for ref in mix], axis=0), middle_low_ref[:, chunk(core, wide)]
    )
    return low(left_product(left, stacked_ref[2])), low(out)


def dec_head_weights_kernel(
    place_ref, normed_ref, stacked_ref, mix_ref, middle_low_ref, keep_ref, send_ref
):
    core = place_ref[0]
    width = mix_ref.shape[1]
    for ref, index in ((send_ref, 1 - core), (keep_ref, core)):
        for side in range(2):
            first, second = head_blocks(
                [normed_ref], stacked_ref, [mix_ref], middle_low_ref, index, side
            )
            rows = first.shape[0] // 2
            for part in range(2):
                ref[side, part, :, :width] = first[part * rows : (part + 1) * rows]
                ref[side, part, :, width:] = second[part * rows : (part + 1) * rows]


def put_rows(rows_ref, row, up_sum_ref, bias_sum_ref):
    cols = rows_ref.shape[1]
    for piece in range(up_sum_ref.shape[1] // cols):
        rows_ref[row : row + 1] = up_sum_ref[:, piece * cols : (piece + 1) * cols]
        row += 1
    width = bias_sum_ref.shape[1]
    for piece in range(2):
        here, lane = row + piece * width // cols, piece * width % cols
        rows_ref[here : here + 1, lane : lane + width] = bias_sum_ref[piece : piece + 1]


def take_rows(rows_ref, row, up_sum_ref, bias_sum_ref):
    cols = rows_ref.shape[1]
    for piece in range(up_sum_ref.shape[1] // cols):
        up_sum_ref[:, piece * cols : (piece + 1) * cols] = rows_ref[row : row + 1]
        row += 1
    width = bias_sum_ref.shape[1]
    for piece in range(2):
        here, lane = row + piece * width // cols, piece * width % cols
        bias_sum_ref[piece : piece + 1] = rows_ref[here : here + 1, lane : lane + width]


def dec_bridge_weights_kernel(
    place_ref, enc_pad_ref, lifted_ref, pos_ref, sums_ref, middle_sums_ref, out_sum_ref, up_sum_ref,
    bias_sum_ref, keep_ref, send_ref, small_ref,
):
    core = place_ref[0]
    cols = lifted_ref.shape[1]
    bridge = low(left_product(enc_pad_ref[...], lifted_ref[...]))
    quarter = bridge.shape[0] // 4
    small_ref[...] = jnp.zeros_like(small_ref)
    small_ref[0:PAD_D] = pos_ref[...]
    row = PAD_D
    for ref, count in ((sums_ref, 4), (middle_sums_ref, 3), (out_sum_ref, 1)):
        small_ref[row : row + count] = ref[...]
        row += count
    put_rows(small_ref, row, up_sum_ref, bias_sum_ref)
    few = small_ref.shape[0] // 4
    first = core == 0

    def block(index):
        return jnp.concatenate(
            [bridge[index * quarter : (index + 1) * quarter], low(small_ref[index * few : (index + 1) * few])],
            axis=0,
        )

    for side in range(2):
        zero, one = block(side), block(2 + side)
        half = zero.shape[0] // 2
        for part in range(2):
            rows = slice(part * half, (part + 1) * half)
            keep_ref[side, part] = jnp.where(first, zero[rows], one[rows])
            send_ref[side, part] = jnp.where(first, one[rows], zero[rows])


def stacked_rows(first, second, lanes=slice(None)):
    return jnp.concatenate([first[:, lanes], second[:, lanes]], axis=0)


def enc_down_weights_kernel(place_ref, hidden_a, hidden_b, cot_a, cot_b, keep_ref, send_ref):
    core, side = place_ref[0], place_ref[1]
    cot = stacked_rows(cot_a, cot_b)
    half = keep_ref.shape[1]
    for ref, index in ((send_ref, 1 - core), (keep_ref, core)):
        block = low(left_product(stacked_rows(hidden_a, hidden_b, chunk(2 * index + side, 2 * half)), cot))
        ref[0] = block[:half]
        ref[1] = block[half:]


def enc_up_weights_kernel(place_ref, normed_a, normed_b, up_ref, keep_ref, send_ref):
    core, side = place_ref[0], place_ref[1]
    normed = stacked_rows(normed_a, normed_b)
    half, cols = keep_ref.shape[1:]
    for ref, index in ((send_ref, 1 - core), (keep_ref, core)):
        block = low(left_product(normed, up_ref[:, chunk(2 * index + side, cols)]))
        ref[0] = block[:half]
        ref[1] = block[half:]


def enc_head_weights_kernel(
    place_ref, normed_a, normed_b, stacked_ref, mix_a, mix_b, middle_low_ref, small_ref, keep_ref, send_ref
):
    core = place_ref[0]
    width = mix_a.shape[1]
    for wanted in range(2):

        @pl.when(place_ref[1] == wanted)
        def _(wanted=wanted):
            for ref, index in ((send_ref, 1 - core), (keep_ref, core)):
                first, second = head_blocks(
                    [normed_a, normed_b], stacked_ref, [mix_a, mix_b], middle_low_ref, index, wanted
                )
                rows = first.shape[0] // 2
                few = small_ref.shape[0] // 2
                for part in range(2):
                    ref[part, :rows, :width] = first[part * rows : (part + 1) * rows]
                    ref[part, :rows, width:] = second[part * rows : (part + 1) * rows]
                    ref[part, rows:] = small_ref[part * few : (part + 1) * few]


def fold_kernel(axis, place_ref, *refs):
    index = place_ref[axis]
    mine_ref, theirs_ref = refs[-2:]
    rows = 0
    for keep_ref, other_ref in zip(refs[:-2:2], refs[1:-2:2]):
        here = (slice(None),) * (len(keep_ref.shape) - 3) + (slice(rows, rows + keep_ref.shape[-2]),)
        rows += keep_ref.shape[-2]
        mine_ref[here] = low(pair(keep_ref[index], other_ref[index]))
        theirs_ref[here] = low(pair(keep_ref[1 - index], other_ref[1 - index]))


def add_kernel(first_ref, second_ref, sum_ref):
    sum_ref[...] = low(pair(first_ref[...], second_ref[...]))


def fold(order, place, axis, *arrays):
    shape = arrays[0].shape[1:-2] + (sum(x.shape[-2] for x in arrays[::2]), arrays[0].shape[-1])
    return kernel_call(
        order, functools.partial(fold_kernel, axis), [shaped(shape)] * 2, place, *arrays, scalars=1, name="fold"
    )


def add(order, first, second):
    return kernel_call(order, add_kernel, [shaped(first.shape)], first, second, name="add")[0]


def flip(value, step):
    return lax.ppermute(value, "dp", [(i, i ^ step) for i in range(lax.axis_size("dp"))])


def cross_start(value):
    return flip(value, 4) if lax.axis_size("dp") > 4 else jnp.zeros_like(value)


def cross_end(order, value, arrived):
    value = add(order, value, arrived)
    step = 8
    while step < lax.axis_size("dp"):
        value = add(order, value, flip(value, step))
        step *= 2
    return value


def pack_kernel(place_ref, mine_ref, other_ref, across_ref, there_ref, packed_ref):
    side, half = place_ref[1], place_ref[2]
    packed_ref[side, half] = mine_ref[...]
    packed_ref[side, 1 - half] = other_ref[...]
    packed_ref[1 - side, half] = across_ref[...]
    packed_ref[1 - side, 1 - half] = there_ref[...]


def pieces_of(place_ref, own_ref, over_ref):
    core = place_ref[0]
    return [
        (ref.at[side, half], index, side, half)
        for ref, index in ((own_ref, core), (over_ref, 1 - core))
        for side in range(2)
        for half in range(2)
    ]


def aligned(index, size):
    return pl.ds(pl.multiple_of(index * size, size), size)


def dec_hidden_whole_kernel(place_ref, own_ref, over_ref, fc1_ref, fc2_ref):
    for ref, core, side, half in pieces_of(place_ref, own_ref, over_ref):
        rows, cols = ref.shape
        if side == 0:
            fc2_ref[aligned(2 * core + half, rows), :] = full(ref[...])
        else:
            fc1_ref[aligned(core, rows), half * cols : (half + 1) * cols] = full(ref[...])


def put_heads(ref, rows, core, side, half, qkv_ref, out_w_ref):
    width = qkv_ref.shape[2]
    here = aligned(2 * core + half, rows)
    if side == 0:
        qkv_ref[0, here, :] = full(ref[:rows, :width])
        qkv_ref[1, here, :] = full(ref[:rows, width:])
    else:
        qkv_ref[2, here, :] = full(ref[:rows, :width])
        out_w_ref[half * rows : (half + 1) * rows, aligned(core, width)] = full(ref[:rows, width:])


def enc_head_whole_kernel(
    place_ref, own_ref, over_ref, qkv_ref, out_w_ref, vec_ref, up_sum_ref, bias_sum_ref, rows_ref
):
    few = rows_ref.shape[0] // 2
    rows = own_ref.shape[2] - few
    for ref, core, side, half in pieces_of(place_ref, own_ref, over_ref):
        put_heads(ref, rows, core, side, half, qkv_ref, out_w_ref)
    for half in range(2):
        rows_ref[half * few : (half + 1) * few] = full(own_ref[0, half, rows:])
    vec_ref[...] = rows_ref[0:6]
    take_rows(rows_ref, 6, up_sum_ref, bias_sum_ref)


def dec_rest_whole_kernel(
    place_ref, own_ref, over_ref, qkv_ref, out_w_ref, bridge_ref, pos_ref, vec_ref, up_sum_ref, bias_sum_ref,
    small_ref,
):
    quarter, few = bridge_ref.shape[0] // 4, small_ref.shape[0] // 4
    rows = qkv_ref.shape[1] // 4
    more = own_ref.shape[2] - rows
    for ref, core, side, half in pieces_of(place_ref, own_ref, over_ref):
        put_heads(ref, rows, core, side, half, qkv_ref, out_w_ref)
        index = 2 * core + side
        start = pl.multiple_of(index * quarter, 8)
        if half == 0:
            bridge_ref[pl.ds(start, more), :] = full(ref[rows:])
        else:
            left = quarter - more
            bridge_ref[pl.ds(start + more, left), :] = full(ref[rows : rows + left])
            small_ref[aligned(index, few), :] = full(ref[rows + left :])
    pos_ref[...] = small_ref[0:PATCHES]
    vec_ref[...] = small_ref[PAD_D : PAD_D + 8]
    take_rows(small_ref, PAD_D + 8, up_sum_ref, bias_sum_ref)


def enc_down_whole_kernel(place_ref, own_ref, over_ref, fc2_ref):
    for ref, core, side, half in pieces_of(place_ref, own_ref, over_ref):
        fc2_ref[aligned(4 * core + 2 * side + half, ref.shape[0]), :] = full(ref[...])


def enc_up_whole_kernel(place_ref, own_ref, over_ref, fc1_ref):
    for ref, core, side, half in pieces_of(place_ref, own_ref, over_ref):
        rows, cols = ref.shape
        fc1_ref[half * rows : (half + 1) * rows, aligned(2 * core + side, cols)] = full(ref[...])


def spread(piece):
    other = flip(piece, 2)
    return piece, other, flip(piece, 1), flip(other, 1)


def pack(order, place, pieces):
    (packed,) = kernel_call(
        order, pack_kernel, [shaped((2, 2) + pieces[0].shape)], place, *pieces, scalars=1, name="pack"
    )
    return packed, swap(packed, "section")


def pick(stacked, index):
    return lax.dynamic_index_in_dim(stacked, index, 0, keepdims=False)


def body(
    enc_in, keep_index, image_count, enc_vec, enc_qkv, enc_qv_bias, enc_out_w, enc_fc1, enc_fc1_bias, enc_fc2,
    bridge_w, dec_vec, dec_pos, dec_qkv, dec_qv_bias, dec_out_w, dec_fc1, dec_fc1_bias, dec_fc2, dec_cot,
):
    core = lax.axis_index("section")
    group = lax.axis_index("dp")
    place = jnp.stack([core, group % 2, group // 2 % 2]).astype(jnp.int32)
    images = keep_index.shape[1]
    enc_width, dec_width = bridge_w.shape
    enc_local, dec_local = enc_qkv.shape[2], dec_qkv.shape[2]
    enc_size, dec_size = enc_width // HE, dec_width // HD
    enc_mlp, dec_mlp = enc_fc1.shape[1], dec_fc1.shape[1]
    rows_e, rows_d = images * PAD_E, images * PAD_D
    enc_groups, dec_groups = enc_local // LANES, dec_local // LANES
    enc_heads, dec_heads = LANES // enc_size, LANES // dec_size
    enc_qkv, dec_qkv = jnp.transpose(enc_qkv, (1, 0, 2)), jnp.transpose(dec_qkv, (1, 0, 2))
    enc_fc1_bias, dec_fc1_bias = enc_fc1_bias[None], dec_fc1_bias[None]
    own_in = pick(enc_in, core)
    enc_in = jnp.transpose(enc_in, (1, 0, 2))
    keep = jnp.pad(pick(keep_index, core), ((0, 0), (0, PAD_E - VIS)), constant_values=-1)
    cot = pick(dec_cot, core)
    count = pick(image_count, core)
    dec_rows = images * PATCHES

    order = []
    call = functools.partial(kernel_call, order)

    def enc_attend(rows):
        return call(
            functools.partial(enc_attend_kernel, images, enc_size),
            [
                shaped((rows_e, enc_width)),
                shaped((rows_e, enc_width)),
                shaped((rows_e, enc_width)),
                shaped((3, rows_e, enc_local)),
                shaped((enc_groups, enc_heads * rows_e, rows_e)),
                shaped((rows_e, enc_local)),
            ],
            place, rows, enc_vec, enc_qkv, enc_qv_bias, enc_out_w,
            scalars=1, name="enc_attend",
        )

    side_in = flip(own_in, 1)
    part, x, normed, proj, weights, mix = enc_attend(enc_in)
    part_other = swap(part, "tensor")
    side_part, side_x, side_normed, side_proj, side_weights, side_mix = enc_attend(side_in)
    part_two, middle, normed_two, hidden, slope = call(
        enc_hidden_kernel,
        [
            shaped((rows_e, enc_width)),
            shaped((rows_e, enc_width), FULL),
            shaped((rows_e, enc_width)),
            shaped((rows_e, enc_mlp)),
            shaped((rows_e, enc_mlp)),
        ],
        x, enc_vec, part, part_other, enc_fc1, enc_fc1_bias, enc_fc2,
        name="enc_hidden",
    )
    part_two_other = swap(part_two, "tensor")
    side_part_other = swap(side_part, "tensor")

    (
        dec_part, enc_out, enc_pad, starting, dec_normed, dec_proj, dec_weights, dec_mix,
    ) = call(
        functools.partial(dec_attend_kernel, images, dec_size),
        [
            shaped((rows_d, dec_width)),
            shaped((images * VIS, enc_width)),
            shaped((rows_e, enc_width)),
            shaped((rows_d, dec_width), FULL),
            shaped((rows_d, dec_width)),
            shaped((3, rows_d, dec_local)),
            shaped((images * dec_groups, dec_heads * PAD_D, PAD_D)),
            shaped((rows_d, dec_local)),
        ],
        count, keep, middle, part_two, part_two_other, enc_vec, bridge_w,
        dec_vec, dec_pos, dec_qkv, dec_qv_bias, dec_out_w,
        scalars=1, name="dec_attend",
    )
    dec_part_other = swap(dec_part, "tensor")
    (enc_out_both,) = call(
        both_cores_kernel, [shaped((images * VIS, 2, enc_width))],
        place, enc_out, swap(enc_out, "section"), scalars=1, name="enc_out_both",
    )
    side_middle, side_normed_two, side_hidden, side_slope = call(
        enc_side_hidden_kernel,
        [
            shaped((rows_e, enc_width), FULL),
            shaped((rows_e, enc_width)),
            shaped((rows_e, enc_mlp)),
            shaped((rows_e, enc_mlp)),
        ],
        side_x, enc_vec, side_part, side_part_other, enc_fc1, enc_fc1_bias,
        name="enc_side_hidden",
    )
    (
        dec_part_back, dec_part_two, dec_middle, dec_normed_two, dec_hid, out_low, dec_up, up_sum, out_sum,
    ) = call(
        functools.partial(dec_hidden_kernel, images),
        [
            shaped((rows_d, dec_width)),
            shaped((rows_d, dec_width)),
            shaped((rows_d, dec_width), FULL),
            shaped((rows_d, dec_width)),
            shaped((rows_d, dec_mlp)),
            shaped((rows_d, dec_width)),
            shaped((rows_d, dec_mlp)),
            shaped((1, dec_mlp), FULL),
            shaped((1, dec_width), FULL),
        ],
        count, starting, dec_part, dec_part_other, dec_vec, dec_fc1, dec_fc1_bias, dec_fc2, cot,
        scalars=1, name="dec_hidden",
    )

    dec_part_back_other = swap(dec_part_back, "tensor")
    d1_keep, d1_send = call(
        dec_hidden_weights_kernel,
        [shaped((2, 2, dec_mlp // 4, dec_width))] * 2,
        place, dec_hid, out_low, dec_normed_two, dec_up,
        scalars=1, name="dec_hidden_weights",
    )
    d1_mine, d1_theirs = fold(order, place, 1, d1_keep, swap(d1_send, "section"))
    d1_arrived = flip(d1_theirs, 1)
    dec_part_one, dec_middle_grad, dec_middle_low, dec_stacked, middle_sums, dec_bias_sum = call(
        functools.partial(dec_attend_back_kernel, images, dec_size),
        [
            shaped((rows_d, dec_width)),
            shaped((rows_d, dec_width), FULL),
            shaped((rows_d, dec_width)),
            shaped((3, rows_d, dec_local)),
            shaped((3, dec_width), FULL),
            shaped((2, dec_local), FULL),
        ],
        dec_middle, out_low, dec_part_back, dec_part_back_other, dec_vec, dec_proj, dec_weights, dec_qkv, dec_out_w,
        name="dec_attend_back",
    )
    dec_part_one_other = swap(dec_part_one, "tensor")
    d1_mine, d1_theirs = fold(order, place, 2, d1_mine, d1_arrived)
    d1_arrived = flip(d1_theirs, 2)
    d2_keep, d2_send = call(
        dec_head_weights_kernel,
        [shaped((2, 2, dec_width // 4, 2 * dec_local))] * 2,
        place, dec_normed, dec_stacked, dec_mix, dec_middle_low,
        scalars=1, name="dec_head_weights",
    )
    d2_other = swap(d2_send, "section")
    d1 = add(order, d1_mine, d1_arrived)
    d1_arrived = cross_start(d1)
    enc_cot, lifted_grad, pos_grad, start_sums = call(
        functools.partial(dec_start_back_kernel, images),
        [
            shaped((rows_e, enc_width)),
            shaped((rows_e, dec_width)),
            shaped((PAD_D, dec_width), FULL),
            shaped((4, dec_width), FULL),
        ],
        count, keep, starting, dec_part_one, dec_part_one_other, dec_vec, dec_middle_grad, bridge_w,
        scalars=1, name="dec_start_back",
    )
    side_cot = flip(enc_cot, 1)
    small_rows = 256
    d3_keep, d3_send = call(
        dec_bridge_weights_kernel,
        [shaped((2, 2, enc_width // 8 + small_rows // 8, dec_width))] * 2,
        place, enc_pad, lifted_grad, pos_grad, start_sums, middle_sums, out_sum, up_sum, dec_bias_sum,
        scalars=1, scratch=[pltpu.VMEM((small_rows, dec_width), FULL)], name="dec_bridge_weights",
    )
    d3_other = swap(d3_send, "section")

    e1_keep, e1_send = call(
        enc_down_weights_kernel,
        [shaped((2, enc_mlp // 8, enc_width))] * 2,
        place, hidden, side_hidden, enc_cot, side_cot,
        scalars=1, name="enc_down_weights",
    )
    e1_other = swap(e1_send, "section")
    part, up = call(
        enc_hidden_back_kernel,
        [shaped((2 * rows_e, enc_width)), shaped((2 * rows_e, enc_mlp))],
        enc_cot, side_cot, slope, side_slope, enc_fc1, enc_fc2,
        name="enc_hidden_back",
    )
    part_other = swap(part, "tensor")
    e1_mine, e1_theirs = fold(order, place, 2, e1_keep, e1_other)
    e1_arrived = flip(e1_theirs, 2)
    d1 = cross_end(order, d1, d1_arrived)
    d1_spread = spread(d1)
    d2_mine, d2_theirs = fold(order, place, 1, d2_keep, d2_other, d3_keep, d3_other)
    d2_arrived = flip(d2_theirs, 1)
    e1 = add(order, e1_mine, e1_arrived)
    e1_arrived = cross_start(e1)
    back_part, middle_grad, middle_low, stacked, middle_two_sums, bias_sum, enc_up_sum = call(
        functools.partial(enc_attend_back_kernel, images, enc_size),
        [
            shaped((2 * rows_e, enc_width)),
            shaped((2 * rows_e, enc_width), FULL),
            shaped((2 * rows_e, enc_width)),
            shaped((3, 2 * rows_e, enc_local)),
            shaped((4, enc_width), FULL),
            shaped((2, enc_local), FULL),
            shaped((1, enc_mlp), FULL),
        ],
        middle, side_middle, enc_cot, side_cot, part, part_other, enc_vec, proj, side_proj,
        weights, side_weights, enc_qkv, enc_out_w, up,
        name="enc_attend_back",
    )
    back_part_other = swap(back_part, "tensor")
    d1_packed = pack(order, place, d1_spread)
    e2_keep, e2_send = call(
        enc_up_weights_kernel,
        [shaped((2, enc_width // 2, enc_mlp // 4))] * 2,
        place, normed_two, side_normed_two, up,
        scalars=1, name="enc_up_weights",
    )
    e2_other = swap(e2_send, "section")
    d2_mine, d2_theirs = fold(order, place, 2, d2_mine, d2_arrived)
    d2_arrived = flip(d2_theirs, 2)
    e2_mine, e2_theirs = fold(order, place, 2, e2_keep, e2_other)
    e2_arrived = flip(e2_theirs, 2)
    few = 32
    grad_in, small = call(
        functools.partial(enc_start_back_kernel, images),
        [shaped((images * VIS, 1, enc_width), FULL), shaped((few, enc_width))],
        x, side_x, back_part, back_part_other, enc_vec, middle_grad, middle_two_sums, enc_up_sum, bias_sum,
        scratch=[pltpu.VMEM((few, enc_width), FULL)], name="enc_start_back",
    )
    e3_keep, e3_send = call(
        enc_head_weights_kernel,
        [shaped((2, enc_width // 4 + few // 2, 2 * enc_local))] * 2,
        place, normed, side_normed, stacked, mix, side_mix, middle_low, small,
        scalars=1, name="enc_head_weights",
    )
    e3_other = swap(e3_send, "section")
    e1 = cross_end(order, e1, e1_arrived)
    e1_spread = spread(e1)
    e2 = add(order, e2_mine, e2_arrived)
    e2_arrived = cross_start(e2)
    e3_mine, e3_theirs = fold(order, place, 2, e3_keep, e3_other)
    e3_arrived = flip(e3_theirs, 2)
    g_dec_fc1, g_dec_fc2 = call(
        dec_hidden_whole_kernel,
        [shaped(dec_fc1.shape, FULL), shaped(dec_fc2.shape, FULL)],
        place, *d1_packed, scalars=1, name="dec_hidden_whole",
    )
    d2 = add(order, d2_mine, d2_arrived)
    d2_arrived = cross_start(d2)
    e1_packed = pack(order, place, e1_spread)
    e2 = cross_end(order, e2, e2_arrived)
    e2_spread = spread(e2)
    (g_enc_fc2,) = call(
        enc_down_whole_kernel, [shaped(enc_fc2.shape, FULL)],
        place, *e1_packed, scalars=1, name="enc_down_whole",
    )
    e3 = add(order, e3_mine, e3_arrived)
    e3_arrived = cross_start(e3)
    d2 = cross_end(order, d2, d2_arrived)
    d2_spread = spread(d2)
    e2_packed = pack(order, place, e2_spread)
    dec_part_two, e2_own = lax.optimization_barrier((dec_part_two, e2_packed[0]))
    dec_part_two_other = swap(dec_part_two, "tensor")
    (g_enc_fc1,) = call(
        enc_up_whole_kernel, [shaped(enc_fc1.shape, FULL)],
        place, e2_own, e2_packed[1], scalars=1, name="enc_up_whole",
    )
    e3 = cross_end(order, e3, e3_arrived)
    e3_spread = spread(e3)
    d2_packed = pack(order, place, d2_spread)
    (dec_out,) = call(
        functools.partial(dec_out_kernel, images),
        [shaped((dec_rows, dec_width))],
        count, dec_middle, dec_part_two, dec_part_two_other, dec_vec,
        scalars=1, name="dec_out",
    )
    g_dec_qkv, g_dec_out_w, g_bridge, g_dec_pos, g_dec_vec, g_dec_fc1_bias, g_dec_qv_bias = call(
        dec_rest_whole_kernel,
        [
            shaped(x.shape, FULL)
            for x in (dec_qkv, dec_out_w, bridge_w, dec_pos, dec_vec, dec_fc1_bias, dec_qv_bias)
        ],
        place, *d2_packed, scalars=1, scratch=[pltpu.VMEM((small_rows, dec_width), FULL)], name="dec_rest_whole",
    )
    e3_packed = pack(order, place, e3_spread)
    g_enc_qkv, g_enc_out_w, g_enc_vec, g_enc_fc1_bias, g_enc_qv_bias = call(
        enc_head_whole_kernel,
        [shaped(x.shape, FULL) for x in (enc_qkv, enc_out_w, enc_vec, enc_fc1_bias, enc_qv_bias)],
        place, *e3_packed, scalars=1, scratch=[pltpu.VMEM((few, enc_width), FULL)], name="enc_head_whole",
    )

    return (
        jnp.transpose(enc_out_both, (1, 0, 2)),
        dec_out[None],
        jnp.transpose(grad_in, (1, 0, 2)),
        g_enc_vec,
        jnp.transpose(g_enc_qkv, (1, 0, 2)),
        g_enc_qv_bias,
        g_enc_out_w,
        g_enc_fc1,
        g_enc_fc1_bias.reshape(-1),
        g_enc_fc2,
        g_bridge,
        g_dec_vec,
        g_dec_pos,
        jnp.transpose(g_dec_qkv, (1, 0, 2)),
        g_dec_qv_bias,
        g_dec_out_w,
        g_dec_fc1,
        g_dec_fc1_bias.reshape(-1),
        g_dec_fc2,
    )


def solution(mesh):
    return jax.shard_map(
        body,
        mesh=mesh,
        in_specs=(
            P(None, "dp", None),
            P(None, "dp", None),
            P(None, "dp"),
            P(),
            P(None, None, "tensor"),
            P(None, "tensor"),
            P("tensor", None),
            P(None, "tensor"),
            P("tensor"),
            P("tensor", None),
            P(),
            P(),
            P(),
            P(None, None, "tensor"),
            P(None, "tensor"),
            P("tensor", None),
            P(None, "tensor"),
            P("tensor"),
            P("tensor", None),
            P(None, "dp", None),
        ),
        out_specs=(
            P(None, "dp", None),
            P("section", "dp", None),
            P("section", "dp", None),
            P(),
            P(None, None, "tensor"),
            P(None, "tensor"),
            P("tensor", None),
            P(None, "tensor"),
            P("tensor"),
            P("tensor", None),
            P(),
            P(),
            P(),
            P(None, None, "tensor"),
            P(None, "tensor"),
            P("tensor", None),
            P(None, "tensor"),
            P("tensor"),
            P("tensor", None),
        ),
        check_vma=False,
    )
```

```python
import functools
import math

import jax
import jax.numpy as jnp
from jax import lax
from jax.experimental import pallas as pl
from jax.experimental.pallas import tpu as pltpu
from jax.sharding import PartitionSpec as P

HE = 12
HD = 16
PATCHES = 196
VIS = 49
PAD_E = 64
PAD_D = 208
LANES = 128
EPSILON = 1e-06
LOW = jnp.bfloat16
FULL = jnp.float32
MIB = 2**20


def low(values):
    return values.astype(LOW)


def full(values):
    return values.astype(FULL)


def matmul(left, right):
    return jnp.dot(left, right, preferred_element_type=FULL)


def left_product(left, right):
    return lax.dot_general(left, right, (((0,), (0,)), ((), ())), preferred_element_type=FULL)


def right_product(left, right):
    return lax.dot_general(left, right, (((1,), (1,)), ((), ())), preferred_element_type=FULL)


def pair(first, second):
    return full(first) + full(second)


def swap(value, axis):
    return lax.ppermute(value, axis, [(i, i ^ 1) for i in range(lax.axis_size(axis))])


def normalize(values):
    center = values - jnp.mean(values, axis=-1, keepdims=True)
    scale = lax.rsqrt(jnp.mean(center * center, axis=-1, keepdims=True) + EPSILON)
    return center * scale, scale


def norm_back(grad, gain, xhat, scale):
    inner = grad * gain
    return scale * (
        inner
        - jnp.mean(inner, axis=-1, keepdims=True)
        - xhat * jnp.mean(inner * xhat, axis=-1, keepdims=True)
    )


def column_sum(values):
    return jnp.sum(full(values), axis=0, keepdims=True)


def one_hot_rows(padded, length, images, packed_first=False):
    shape = (images * length, images * padded) if packed_first else (images * padded, images * length)
    first = lax.broadcasted_iota(jnp.int32, shape, 0)
    second = lax.broadcasted_iota(jnp.int32, shape, 1)
    packed, wide = (first, second) if packed_first else (second, first)
    hit = None
    for image in range(images):
        here = (
            (packed >= image * length)
            & (packed < (image + 1) * length)
            & (wide - image * padded == packed - image * length)
        )
        hit = here if hit is None else hit | here
    return low(jnp.where(hit, 1.0, 0.0))


def head_masks(head_size):
    lane = lax.broadcasted_iota(jnp.int32, (1, LANES), 1)
    return [
        jnp.where((lane >= j * head_size) & (lane < (j + 1) * head_size), 1.0, 0.0)
        for j in range(LANES // head_size)
    ]


def spread_heads(values, masks):
    wide = full(values)
    return jnp.concatenate([low(wide * mask) for mask in masks], axis=0)


def gather_heads(stacked, masks):
    rows = stacked.shape[0] // len(masks)
    total = None
    for j, mask in enumerate(masks):
        term = stacked[j * rows : (j + 1) * rows] * mask
        total = term if total is None else total + term
    return total


def attend(queries, key_rows, value_rows, masks, allowed, factor):
    scores = right_product(spread_heads(queries, masks), key_rows) * factor
    scores = jnp.where(allowed, scores, -1e30)
    exponent = jnp.exp(scores - jnp.max(scores, axis=-1, keepdims=True))
    weights_low = low(exponent * (1.0 / jnp.sum(exponent, axis=-1, keepdims=True)))
    return weights_low, low(gather_heads(matmul(weights_low, value_rows), masks))


def attend_back(queries, key_rows, value_rows, weights_low, upstream, masks, factor):
    spread_up = spread_heads(upstream, masks)
    weight_grad = right_product(spread_up, value_rows)
    weights = full(weights_low)
    product = weights * weight_grad
    score_grad = low(product - weights * jnp.sum(product, axis=-1, keepdims=True))
    query_grad = gather_heads(matmul(score_grad, key_rows), masks) * factor
    key_grad = left_product(score_grad, spread_heads(queries, masks)) * factor
    value_grad = left_product(weights_low, spread_up)
    return low(query_grad), low(key_grad), low(value_grad)


def same_image(heads, images, padded, length):
    shape = (heads * images * padded, images * padded)
    row = lax.broadcasted_iota(jnp.int32, shape, 0)
    key = lax.broadcasted_iota(jnp.int32, shape, 1)
    hit = None
    for head in range(heads):
        for image in range(images):
            start = (head * images + image) * padded
            here = (
                (row >= start)
                & (row < start + padded)
                & (key >= image * padded)
                & (key < image * padded + length)
            )
            hit = here if hit is None else hit | here
    return hit


def live_rows(count, rows, padded):
    row = lax.broadcasted_iota(jnp.int32, (rows, 1), 0)
    return jnp.where(row < count * padded, 1.0, 0.0)


def kernel_call(order, kernel, outs, *arguments, scalars=0, scratch=(), after=(), memory=24, name=None):
    count = len(arguments)
    before = order[-1:] + list(after)

    def run(*refs):
        mark = count + len(before) + len(outs)
        refs[mark][...] = jnp.zeros((8, LANES), FULL)
        kernel(*refs[:count], *refs[count + len(before) : mark], *refs[mark + 1 :])

    specs = [pl.BlockSpec(memory_space=pltpu.SMEM)] * scalars
    specs += [pl.BlockSpec(memory_space=pltpu.VMEM)] * (count - scalars)
    specs += [pl.BlockSpec(memory_space=pl.ANY)] * len(before)
    results = pl.pallas_call(
        run,
        out_shape=[jax.ShapeDtypeStruct(x.shape, x.dtype) for x in outs] + [shaped((8, LANES), FULL)],
        in_specs=specs,
        out_specs=[pl.BlockSpec(memory_space=pltpu.VMEM)] * (len(outs) + 1),
        scratch_shapes=scratch,
        compiler_params=pltpu.CompilerParams(vmem_limit_bytes=memory * MIB),
        cost_estimate=pl.CostEstimate(flops=2 * 10**11, bytes_accessed=1, transcendentals=0),
        name=name,
    )(*arguments, *before)
    order.append(results[-1])
    return results[:-1]


def chunk(index, size):
    return pl.ds(pl.multiple_of(index * size, LANES), size)


def shaped(shape, dtype=LOW):
    return jax.ShapeDtypeStruct(shape, dtype)


def project_heads(normed, qkv_ref, bias, proj_ref, width):
    queries = low(matmul(normed, qkv_ref[0]) + bias[0:1])
    key_rows = low(matmul(normed, qkv_ref[1]))
    value_rows = low(matmul(normed, qkv_ref[2]) + bias[1:2])
    proj_ref[0] = queries
    proj_ref[1] = key_rows
    proj_ref[2] = value_rows


def enc_attend_kernel(
    images, head_size, place_ref, x_ref, vec_ref, qkv_ref, bias_ref, out_w_ref,
    part_ref, x_out_ref, normed_ref, proj_ref, weights_ref, mix_ref,
):
    width = qkv_ref.shape[2]
    if len(x_ref.shape) == 2:
        rows = x_ref[...]
    else:
        rows = low(jnp.where(place_ref[0] == 0, full(x_ref[:, 0, :]), full(x_ref[:, 1, :])))
    x = matmul(one_hot_rows(PAD_E, VIS, images), rows)
    x_out_ref[...] = low(x)
    vec = full(vec_ref[...])
    xhat, _ = normalize(x)
    normed = low(xhat * vec[0:1] + vec[1:2])
    normed_ref[...] = normed
    project_heads(normed, qkv_ref, full(bias_ref[...]), proj_ref, width)
    masks = head_masks(head_size)
    allowed = same_image(len(masks), images, PAD_E, VIS)
    for group in range(width // LANES):
        lanes = slice(group * LANES, (group + 1) * LANES)
        weights_low, mixture = attend(
            proj_ref[0, :, lanes],
            proj_ref[1, :, lanes],
            proj_ref[2, :, lanes],
            masks,
            allowed,
            1.0 / math.sqrt(head_size),
        )
        weights_ref[group] = weights_low
        mix_ref[:, lanes] = mixture
    part_ref[...] = low(matmul(mix_ref[...], out_w_ref[...]))


def mlp_forward(middle, gain, shift, fc1_ref, bias_ref, fc2_ref, normed_ref, hidden_ref, slope_ref):
    xhat, _ = normalize(middle)
    normed = low(xhat * gain + shift)
    normed_ref[...] = normed
    pre = matmul(normed, fc1_ref[...]) + full(bias_ref[...])
    share = 0.5 + 0.5 * lax.erf(pre * math.sqrt(0.5))
    hidden = low(pre * share)
    hidden_ref[...] = hidden
    slope = share + pre * jnp.exp(-0.5 * pre * pre) * (1.0 / math.sqrt(2.0 * math.pi))
    if slope_ref is not None:
        slope_ref[...] = low(slope)
    return None if fc2_ref is None else low(matmul(hidden, fc2_ref[...])), slope


def enc_forward_send(place_ref, first_normed_ref, mix_ref, normed_ref, hidden_ref, send_ref):
    core, side = 1 - place_ref[0], place_ref[1]
    width, wide = normed_ref.shape[1], hidden_ref.shape[1] // 4
    half = width // 2
    send_ref[:, :wide] = hidden_ref[:, chunk(2 * core + side, wide)]
    send_ref[:, wide : wide + width] = normed_ref[...]
    send_ref[:, wide + width : wide + width + half] = first_normed_ref[:, chunk(core, half)]
    send_ref[:, wide + width + half :] = mix_ref[...]


def enc_hidden_kernel(
    place_ref, x_ref, vec_ref, part_ref, other_ref, fc1_ref, bias_ref, first_normed_ref, mix_ref, fc2_ref,
    part_two_ref, middle_ref, normed_ref, hidden_ref, slope_ref, send_ref,
):
    vec = full(vec_ref[...])
    middle = full(x_ref[...]) + pair(part_ref[...], other_ref[...]) + vec[2:3]
    middle_ref[...] = middle
    part, _ = mlp_forward(
        middle, vec[3:4], vec[4:5], fc1_ref, bias_ref, fc2_ref, normed_ref, hidden_ref, slope_ref
    )
    part_two_ref[...] = part
    enc_forward_send(place_ref, first_normed_ref, mix_ref, normed_ref, hidden_ref, send_ref)


def enc_side_hidden_kernel(
    place_ref, x_ref, vec_ref, part_ref, other_ref, fc1_ref, bias_ref, first_normed_ref, mix_ref,
    middle_ref, normed_ref, hidden_ref, slope_ref, send_ref,
):
    vec = full(vec_ref[...])
    middle = full(x_ref[...]) + pair(part_ref[...], other_ref[...]) + vec[2:3]
    middle_ref[...] = middle
    mlp_forward(middle, vec[3:4], vec[4:5], fc1_ref, bias_ref, None, normed_ref, hidden_ref, slope_ref)
    enc_forward_send(place_ref, first_normed_ref, mix_ref, normed_ref, hidden_ref, send_ref)


def both_cores_kernel(place_ref, own_ref, over_ref, both_ref):
    first = place_ref[0] == 0
    own, over = full(own_ref[...]), full(over_ref[...])
    both_ref[:, 0, :] = low(jnp.where(first, own, over))
    both_ref[:, 1, :] = low(jnp.where(first, over, own))


def selector(keep_ref, image):
    patch = lax.broadcasted_iota(jnp.int32, (PAD_D, PAD_E), 0)
    return jnp.where(patch == keep_ref[image : image + 1, :], 1.0, 0.0)


def dec_attend_kernel(
    images, head_size, count_ref, keep_ref, middle_ref, part_ref, other_ref, enc_vec_ref, bridge_ref,
    vec_ref, pos_ref, qkv_ref, bias_ref, out_w_ref,
    part_out_ref, enc_out_ref, enc_pad_ref, starting_ref, normed_ref, proj_ref, weights_ref, mix_ref,
):
    width = qkv_ref.shape[2]
    vec = full(vec_ref[...])
    encoded = middle_ref[...] + pair(part_ref[...], other_ref[...]) + full(enc_vec_ref[...])[5:6]
    enc_pad = low(encoded * live_rows(count_ref[0], images * PAD_E, PAD_E))
    enc_pad_ref[...] = enc_pad
    enc_out_ref[...] = low(matmul(one_hot_rows(PAD_E, VIS, images, True), enc_pad))
    lifted = matmul(enc_pad, bridge_ref[...]) + vec[0:1]
    lifted_high = low(lifted)
    lifted_rest = low(lifted - full(lifted_high))
    pos = matmul(one_hot_rows(PAD_D, PATCHES, 1), pos_ref[...])
    for image in range(images):
        chosen = selector(keep_ref, image)
        rows = slice(image * PAD_E, (image + 1) * PAD_E)
        placed = matmul(low(chosen), lifted_high[rows]) + matmul(low(chosen), lifted_rest[rows])
        hidden_patch = 1.0 - jnp.sum(chosen, axis=1, keepdims=True)
        starting_ref[image * PAD_D : (image + 1) * PAD_D, :] = placed + hidden_patch * vec[1:2] + pos
    xhat, _ = normalize(starting_ref[...])
    normed = low(xhat * vec[2:3] + vec[3:4])
    normed_ref[...] = normed
    project_heads(normed, qkv_ref, full(bias_ref[...]), proj_ref, width)
    masks = head_masks(head_size)
    allowed = lax.broadcasted_iota(jnp.int32, (1, PAD_D), 1) < PATCHES
    groups = width // LANES
    for image in range(images):
        rows = slice(image * PAD_D, (image + 1) * PAD_D)
        for group in range(groups):
            lanes = slice(group * LANES, (group + 1) * LANES)
            weights_low, mixture = attend(
                proj_ref[0, rows, lanes],
                proj_ref[1, rows, lanes],
                proj_ref[2, rows, lanes],
                masks,
                allowed,
                1.0 / math.sqrt(head_size),
            )
            weights_ref[image * groups + group] = weights_low
            mix_ref[rows, lanes] = mixture
    part_out_ref[...] = low(matmul(mix_ref[...], out_w_ref[...]))


def dec_hidden_kernel(
    images, count_ref, place_ref, starting_ref, part_ref, other_ref, vec_ref, fc1_ref, bias_ref, fc2_ref, cot_ref,
    part_back_ref, part_two_ref, middle_ref, normed_ref, hidden_ref, out_low_ref, up_ref,
    up_sum_ref, out_sum_ref, send_ref,
):
    vec = full(vec_ref[...])
    middle = starting_ref[...] + pair(part_ref[...], other_ref[...]) + vec[4:5]
    middle_ref[...] = middle
    part, slope = mlp_forward(
        middle, vec[5:6], vec[6:7], fc1_ref, bias_ref, fc2_ref, normed_ref, hidden_ref, None
    )
    part_two_ref[...] = part
    spread = matmul(one_hot_rows(PAD_D, PATCHES, images), cot_ref[...])
    out_low = low(spread * live_rows(count_ref[0], images * PAD_D, PAD_D))
    out_low_ref[...] = out_low
    up_grad = low(slope * right_product(out_low, fc2_ref[...]))
    up_ref[...] = up_grad
    part_back_ref[...] = low(right_product(up_grad, fc1_ref[...]))
    up_sum_ref[...] = column_sum(up_grad)
    out_sum_ref[...] = column_sum(out_low)
    core = 1 - place_ref[0]
    width, wide = out_low.shape[1], up_grad.shape[1]
    half = width // 2
    send_ref[:, : wide // 2] = hidden_ref[:, chunk(core, wide // 2)]
    send_ref[:, wide // 2 : wide // 2 + half] = normed_ref[:, chunk(core, half)]
    send_ref[:, wide // 2 + half : wide // 2 + half + wide] = up_grad
    send_ref[:, wide // 2 + half + wide :] = out_low


def dec_out_kernel(images, count_ref, middle_ref, part_ref, other_ref, vec_ref, out_ref):
    decoded = middle_ref[...] + pair(part_ref[...], other_ref[...]) + full(vec_ref[...])[7:8]
    decoded = low(decoded * live_rows(count_ref[0], images * PAD_D, PAD_D))
    out_ref[...] = low(matmul(one_hot_rows(PAD_D, PATCHES, images, True), decoded))


def attention_back(
    first_row, images, padded, together, head_size, mixture_grad, proj_ref, weights_ref, stacked_ref
):
    masks = head_masks(head_size)
    groups = proj_ref.shape[2] // LANES
    step = images if together else 1
    for first in range(0, images, step):
        rows = slice(first * padded, (first + step) * padded)
        out_rows = slice(first_row + first * padded, first_row + (first + step) * padded)
        for group in range(groups):
            lanes = slice(group * LANES, (group + 1) * LANES)
            grads = attend_back(
                proj_ref[0, rows, lanes],
                proj_ref[1, rows, lanes],
                proj_ref[2, rows, lanes],
                weights_ref[first // step * groups + group],
                mixture_grad[out_rows, lanes],
                masks,
                1.0 / math.sqrt(head_size),
            )
            for j in range(3):
                stacked_ref[j, out_rows, lanes] = grads[j]


def normed_back(stacked_ref, qkv_ref):
    total = right_product(stacked_ref[0], qkv_ref[0])
    for j in (1, 2):
        total = total + right_product(stacked_ref[j], qkv_ref[j])
    return low(total)


def dec_attend_back_kernel(
    images, head_size, place_ref, middle_ref, out_low_ref, part_in_ref, other_ref, vec_ref, proj_ref, weights_ref,
    qkv_ref, out_w_ref, normed_ref, mix_ref,
    part_ref, middle_grad_ref, middle_low_ref, stacked_ref, sums_ref, bias_sum_ref, send_ref,
):
    vec = full(vec_ref[...])
    two_grad = pair(part_in_ref[...], other_ref[...])
    xhat, scale = normalize(middle_ref[...])
    middle_grad = full(out_low_ref[...]) + norm_back(two_grad, vec[5:6], xhat, scale)
    middle_grad_ref[...] = middle_grad
    middle_low = low(middle_grad)
    middle_low_ref[...] = middle_low
    mixture_grad = low(right_product(middle_low, out_w_ref[...]))
    attention_back(0, images, PAD_D, False, head_size, mixture_grad, proj_ref, weights_ref, stacked_ref)
    part_ref[...] = normed_back(stacked_ref, qkv_ref)
    core = 1 - place_ref[0]
    width = mix_ref.shape[1]
    half = middle_low.shape[1] // 2
    for j in range(3):
        send_ref[:, j * width : (j + 1) * width] = stacked_ref[j]
    send_ref[:, 3 * width : 4 * width] = mix_ref[...]
    send_ref[:, 4 * width : 4 * width + half] = normed_ref[:, chunk(core, half)]
    send_ref[:, 4 * width + half :] = middle_low_ref[:, chunk(core, half)]
    sums_ref[0:1] = column_sum(middle_grad)
    sums_ref[1:2] = column_sum(two_grad * xhat)
    sums_ref[2:3] = column_sum(two_grad)
    bias_sum_ref[0:1] = column_sum(stacked_ref[0])
    bias_sum_ref[1:2] = column_sum(stacked_ref[2])


def dec_start_back_kernel(
    images, count_ref, keep_ref, starting_ref, part_ref, other_ref, vec_ref, middle_grad_ref, bridge_ref,
    enc_cot_ref, lifted_ref, pos_ref, sums_ref,
):
    vec = full(vec_ref[...])
    one_grad = pair(part_ref[...], other_ref[...])
    xhat, scale = normalize(starting_ref[...])
    starting_grad = middle_grad_ref[...] + norm_back(one_grad, vec[2:3], xhat, scale)
    sums_ref[2:3] = column_sum(one_grad * xhat)
    sums_ref[3:4] = column_sum(one_grad)
    token = None
    total = None
    for image in range(images):
        grad = starting_grad[image * PAD_D : (image + 1) * PAD_D]
        chosen = selector(keep_ref, image)
        hidden_patch = 1.0 - jnp.sum(chosen, axis=1, keepdims=True)
        term = column_sum(hidden_patch * grad)
        token = term if token is None else token + term
        total = grad if total is None else total + grad
        lifted_ref[image * PAD_E : (image + 1) * PAD_E, :] = low(left_product(low(chosen), low(grad)))
    pos_ref[...] = total
    lifted_grad = lifted_ref[...]
    sums_ref[0:1] = column_sum(lifted_grad)
    sums_ref[1:2] = token
    handed = right_product(lifted_grad, bridge_ref[...])
    enc_cot_ref[...] = low(handed * live_rows(count_ref[0], images * PAD_E, PAD_E))


def enc_hidden_back_kernel(
    place_ref, cot_a, cot_b, slope_a, slope_b, fc1_ref, fc2_ref, part_ref, up_ref, send_ref
):
    slope = jnp.concatenate([slope_a[...], slope_b[...]], axis=0)
    up_grad = low(full(slope) * right_product(stacked_rows(cot_a, cot_b), fc2_ref[...]))
    up_ref[...] = up_grad
    part_ref[...] = low(right_product(up_grad, fc1_ref[...]))
    send_ref[...] = up_ref[:, chunk(2 * (1 - place_ref[0]) + place_ref[1], send_ref.shape[1])]


def enc_attend_back_kernel(
    images, head_size, place_ref, middle_a, middle_b, cot_a, cot_b, part_in_ref, other_ref, vec_ref, proj_a, proj_b,
    weights_a, weights_b, qkv_ref, out_w_ref, up_ref,
    part_ref, middle_grad_ref, middle_low_ref, stacked_ref, sums_ref, bias_sum_ref, up_sum_ref, send_ref,
):
    vec = full(vec_ref[...])
    own = middle_a.shape[0]
    cot = full(stacked_rows(cot_a, cot_b))
    two_grad = pair(part_in_ref[...], other_ref[...])
    xhat, scale = normalize(stacked_rows(middle_a, middle_b))
    middle_grad = cot + norm_back(two_grad, vec[3:4], xhat, scale)
    middle_grad_ref[...] = middle_grad
    middle_low = low(middle_grad)
    middle_low_ref[...] = middle_low
    mixture_grad = low(right_product(middle_low, out_w_ref[...]))
    attention_back(0, images, PAD_E, True, head_size, mixture_grad, proj_a, weights_a, stacked_ref)
    attention_back(own, images, PAD_E, True, head_size, mixture_grad, proj_b, weights_b, stacked_ref)
    part_ref[...] = normed_back(stacked_ref, qkv_ref)
    width = qkv_ref.shape[2]

    @pl.when(place_ref[1] == 0)
    def _():
        send_ref[:, :width] = stacked_ref[0]
        send_ref[:, width:] = stacked_ref[1]

    @pl.when(place_ref[1] == 1)
    def _():
        send_ref[:, :width] = stacked_ref[2]
        send_ref[:, width:] = middle_low_ref[:, chunk(1 - place_ref[0], width)]

    sums_ref[0:1] = column_sum(middle_grad)
    sums_ref[1:2] = column_sum(two_grad * xhat)
    sums_ref[2:3] = column_sum(two_grad)
    sums_ref[3:4] = column_sum(cot)
    bias_sum_ref[0:1] = column_sum(stacked_ref[0])
    bias_sum_ref[1:2] = column_sum(stacked_ref[2])
    up_sum_ref[...] = column_sum(up_ref[...])


def enc_start_back_kernel(
    images, x_a, x_b, part_ref, other_ref, vec_ref, middle_grad_ref, sums_ref, up_sum_ref, bias_sum_ref,
    grad_in_ref, small_ref, rows_ref,
):
    vec = full(vec_ref[...])
    own = x_a.shape[0]
    one_grad = pair(part_ref[...], other_ref[...])
    xhat, scale = normalize(full(stacked_rows(x_a, x_b)))
    grad = middle_grad_ref[:own] + norm_back(one_grad[:own], vec[0:1], xhat[:own], scale[:own])
    take = full(one_hot_rows(PAD_E, VIS, images, True))
    grad_in_ref[:, 0, :] = jnp.dot(
        take, grad, preferred_element_type=FULL, precision=lax.Precision.HIGHEST
    )
    rows_ref[...] = jnp.zeros_like(rows_ref)
    rows_ref[0:1] = column_sum(one_grad * xhat)
    rows_ref[1:2] = column_sum(one_grad)
    rows_ref[2:6] = sums_ref[...]
    put_rows(rows_ref, 6, up_sum_ref, bias_sum_ref)
    small_ref[...] = low(rows_ref[...])


def tall(*parts):
    return jnp.concatenate(parts, axis=0)


def by_side(place_ref, mine_ref, theirs_ref, blocks):
    first = place_ref[1] == 0
    rows = mine_ref.shape[1]
    for part in range(2):
        zero, one = (low(block[part * rows : (part + 1) * rows]) for block in blocks)
        mine_ref[part] = jnp.where(first, zero, one)
        theirs_ref[part] = jnp.where(first, one, zero)


def dec_hidden_weights_kernel(
    place_ref, hidden_ref, out_low_ref, normed_ref, up_ref, over_ref, mine_ref, theirs_ref
):
    core = place_ref[0]
    width, wide = out_low_ref.shape[1], up_ref.shape[1]
    half = width // 2
    over_up = over_ref[:, wide // 2 + half : wide // 2 + half + wide]
    over_out = over_ref[:, wide // 2 + half + wide :]
    down = left_product(
        tall(hidden_ref[:, chunk(core, wide // 2)], over_ref[:, : wide // 2]), tall(out_low_ref[...], over_out)
    )
    up = left_product(
        tall(normed_ref[:, chunk(core, half)], over_ref[:, wide // 2 : wide // 2 + half]),
        tall(up_ref[...], over_up),
    )
    by_side(place_ref, mine_ref, theirs_ref, (down, tall(up[:, :width], up[:, width:])))


def dec_head_weights_kernel(
    place_ref, normed_ref, stacked_ref, mix_ref, middle_low_ref, over_ref, mine_ref, theirs_ref
):
    core = place_ref[0]
    width = mix_ref.shape[1]
    half = normed_ref.shape[1] // 2
    left = tall(normed_ref[:, chunk(core, half)], over_ref[:, 4 * width : 4 * width + half])
    grads = [
        left_product(left, tall(stacked_ref[j], over_ref[:, j * width : (j + 1) * width])) for j in range(3)
    ]
    out = left_product(
        tall(mix_ref[...], over_ref[:, 3 * width : 4 * width]),
        tall(middle_low_ref[:, chunk(core, half)], over_ref[:, 4 * width + half :]),
    )
    by_side(
        place_ref, mine_ref, theirs_ref,
        (jnp.concatenate(grads[:2], axis=1), jnp.concatenate([grads[2], out], axis=1)),
    )


def put_rows(rows_ref, row, up_sum_ref, bias_sum_ref):
    cols = rows_ref.shape[1]
    for piece in range(up_sum_ref.shape[1] // cols):
        rows_ref[row : row + 1] = up_sum_ref[:, piece * cols : (piece + 1) * cols]
        row += 1
    width = bias_sum_ref.shape[1]
    for piece in range(2):
        here, lane = row + piece * width // cols, piece * width % cols
        rows_ref[here : here + 1, lane : lane + width] = bias_sum_ref[piece : piece + 1]


def take_rows(rows_ref, row, up_sum_ref, bias_sum_ref):
    cols = rows_ref.shape[1]
    for piece in range(up_sum_ref.shape[1] // cols):
        up_sum_ref[:, piece * cols : (piece + 1) * cols] = rows_ref[row : row + 1]
        row += 1
    width = bias_sum_ref.shape[1]
    for piece in range(2):
        here, lane = row + piece * width // cols, piece * width % cols
        bias_sum_ref[piece : piece + 1] = rows_ref[here : here + 1, lane : lane + width]


def dec_bridge_weights_kernel(
    place_ref, enc_pad_ref, lifted_ref, pos_ref, sums_ref, middle_sums_ref, out_sum_ref, up_sum_ref,
    bias_sum_ref, keep_ref, send_ref, small_ref,
):
    core = place_ref[0]
    cols = lifted_ref.shape[1]
    bridge = low(left_product(enc_pad_ref[...], lifted_ref[...]))
    quarter = bridge.shape[0] // 4
    small_ref[...] = jnp.zeros_like(small_ref)
    small_ref[0:PAD_D] = pos_ref[...]
    row = PAD_D
    for ref, count in ((sums_ref, 4), (middle_sums_ref, 3), (out_sum_ref, 1)):
        small_ref[row : row + count] = ref[...]
        row += count
    put_rows(small_ref, row, up_sum_ref, bias_sum_ref)
    few = small_ref.shape[0] // 4
    first = core == 0

    def block(index):
        return jnp.concatenate(
            [bridge[index * quarter : (index + 1) * quarter], low(small_ref[index * few : (index + 1) * few])],
            axis=0,
        )

    for side in range(2):
        zero, one = block(side), block(2 + side)
        half = zero.shape[0] // 2
        for part in range(2):
            rows = slice(part * half, (part + 1) * half)
            keep_ref[side, part] = jnp.where(first, zero[rows], one[rows])
            send_ref[side, part] = jnp.where(first, one[rows], zero[rows])


def stacked_rows(first, second, lanes=slice(None)):
    return jnp.concatenate([first[:, lanes], second[:, lanes]], axis=0)


def enc_hidden_weights_kernel(
    place_ref, hidden_a, hidden_b, cot_a, cot_b, normed_a, normed_b, up_ref,
    forward_a, forward_b, over_cot_a, over_cot_b, over_up, mine_ref, theirs_ref,
):
    core, side, half = place_ref[0], place_ref[1], place_ref[2]
    rows = mine_ref.shape[0] // 2
    width = 2 * rows
    features = cot_a.shape[1]
    lanes = chunk(2 * core + side, width)
    down = low(
        left_product(
            tall(hidden_a[:, lanes], hidden_b[:, lanes], forward_a[:, :width], forward_b[:, :width]),
            tall(cot_a[...], cot_b[...], over_cot_a[...], over_cot_b[...]),
        )
    )
    here = slice(width, width + features)
    up = low(
        left_product(
            tall(normed_a[...], normed_b[...], forward_a[:, here], forward_b[:, here]),
            tall(up_ref[:, lanes], over_up[...]),
        )
    )
    for part in range(2):
        block = (
            down[part * rows : (part + 1) * rows],
            up[2 * part * rows : (2 * part + 1) * rows],
            up[(2 * part + 1) * rows : (2 * part + 2) * rows],
        )
        for ref, index in ((mine_ref, half), (theirs_ref, 1 - half)):

            @pl.when(index == part)
            def _(ref=ref, block=block):
                ref[:rows] = block[0]
                ref[rows:, :width] = block[1]
                ref[rows:, width:] = block[2]


def last_weights_kernel(
    place_ref, normed_a, normed_b, stacked_ref, mix_a, mix_b, middle_low_ref, forward_a, forward_b, over_ref,
    small_ref, rest_mine, rest_other, mine_ref, theirs_ref,
):
    core, half = place_ref[0], place_ref[2]
    width = mix_a.shape[1]
    half_width = normed_a.shape[1] // 2
    lanes = chunk(core, half_width)
    start = forward_a.shape[1] - half_width - width
    left = tall(
        normed_a[:, lanes], normed_b[:, lanes],
        forward_a[:, start : start + half_width], forward_b[:, start : start + half_width],
    )
    few = small_ref.shape[0] // 2
    columns = mine_ref.shape[1]

    def put(first, second):
        rows = first.shape[0] // 2
        for part in range(2):
            here = slice(part * rows, (part + 1) * rows)
            block = jnp.concatenate([first[here], second[here]], axis=1)
            block = tall(low(block), small_ref[part * few : (part + 1) * few])
            for ref, index in ((mine_ref, half), (theirs_ref, 1 - half)):

                @pl.when(index == part)
                def _(ref=ref, block=block):
                    for i in range(block.shape[1] // columns):
                        ref[i * block.shape[0] : (i + 1) * block.shape[0]] = block[
                            :, i * columns : (i + 1) * columns
                        ]

    @pl.when(place_ref[1] == 0)
    def _():
        put(
            left_product(left, tall(stacked_ref[0], over_ref[:, :width])),
            left_product(left, tall(stacked_ref[1], over_ref[:, width:])),
        )

    @pl.when(place_ref[1] == 1)
    def _():
        put(
            left_product(left, tall(stacked_ref[2], over_ref[:, :width])),
            left_product(
                tall(mix_a[...], mix_b[...], forward_a[:, start + half_width :], forward_b[:, start + half_width :]),
                tall(middle_low_ref[:, lanes], over_ref[:, width:]),
            ),
        )

    for ref, index in ((mine_ref, half), (theirs_ref, 1 - half)):
        total = low(pair(rest_mine[index], rest_other[index]))
        count = total.shape[0]
        row = ref.shape[0] - count * (total.shape[1] // columns)
        for i in range(total.shape[1] // columns):
            ref[row + i * count : row + (i + 1) * count] = total[:, i * columns : (i + 1) * columns]


def fold_kernel(axis, place_ref, *refs):
    index = place_ref[axis]
    mine_ref, theirs_ref = refs[-2:]
    rows = 0
    for keep_ref, other_ref in zip(refs[:-2:2], refs[1:-2:2]):
        here = (slice(None),) * (len(keep_ref.shape) - 3) + (slice(rows, rows + keep_ref.shape[-2]),)
        rows += keep_ref.shape[-2]
        mine_ref[here] = low(pair(keep_ref[index], other_ref[index]))
        theirs_ref[here] = low(pair(keep_ref[1 - index], other_ref[1 - index]))


def fold_more_kernel(place_ref, keep_ref, other_ref, before_mine, before_theirs, mine_ref, theirs_ref):
    index = place_ref[2]
    rows = before_mine.shape[0]
    mine_ref[:rows] = before_mine[...]
    theirs_ref[:rows] = before_theirs[...]
    mine_ref[rows:] = low(pair(keep_ref[index], other_ref[index]))
    theirs_ref[rows:] = low(pair(keep_ref[1 - index], other_ref[1 - index]))


def add_kernel(first_ref, second_ref, sum_ref):
    sum_ref[...] = low(pair(first_ref[...], second_ref[...]))


def fold(order, place, axis, *arrays, after=()):
    shape = arrays[0].shape[1:-2] + (sum(x.shape[-2] for x in arrays[::2]), arrays[0].shape[-1])
    return kernel_call(
        order, functools.partial(fold_kernel, axis), [shaped(shape)] * 2, place, *arrays,
        scalars=1, after=after, name="fold",
    )


def add(order, first, second, after=()):
    return kernel_call(order, add_kernel, [shaped(first.shape)], first, second, after=after, name="add")[0]


def mark_kernel(out_ref):
    out_ref[...] = jnp.zeros_like(out_ref)


def mark(order, *values):
    kernel_call(order, mark_kernel, [shaped((8, LANES), FULL)], after=values, name="mark")


def flip(value, step):
    return lax.ppermute(value, "dp", [(i, i ^ step) for i in range(lax.axis_size("dp"))])


def cross_start(value):
    return flip(value, 4) if lax.axis_size("dp") > 4 else jnp.zeros_like(value)


def cross_end(order, value, arrived, after=()):
    value = add(order, value, arrived, after)
    step = 8
    while step < lax.axis_size("dp"):
        value = add(order, value, flip(value, step))
        step *= 2
    return value


def pack_kernel(place_ref, mine_ref, other_ref, across_ref, there_ref, packed_ref):
    side, half = place_ref[1], place_ref[2]
    packed_ref[side, half] = mine_ref[...]
    packed_ref[side, 1 - half] = other_ref[...]
    packed_ref[1 - side, half] = across_ref[...]
    packed_ref[1 - side, 1 - half] = there_ref[...]


def pieces_of(place_ref, own_ref, over_ref):
    core = place_ref[0]
    return [
        (ref.at[side, half], index, side, half)
        for ref, index in ((own_ref, core), (over_ref, 1 - core))
        for side in range(2)
        for half in range(2)
    ]


def aligned(index, size):
    return pl.ds(pl.multiple_of(index * size, size), size)


def put_heads(block, core, side, half, qkv_ref, out_w_ref):
    rows, width = block.shape[0], qkv_ref.shape[2]
    here = aligned(2 * core + half, rows)
    if side == 0:
        qkv_ref[0, here, :] = full(block[:, :width])
        qkv_ref[1, here, :] = full(block[:, width:])
    else:
        qkv_ref[2, here, :] = full(block[:, :width])
        out_w_ref[half * rows : (half + 1) * rows, aligned(core, width)] = full(block[:, width:])


def dec_whole_kernel(place_ref, own_ref, over_ref, fc1_ref, fc2_ref, qkv_ref, out_w_ref):
    rows, cols = fc1_ref.shape[0] // 2, fc1_ref.shape[1] // 2
    for ref, core, side, half in pieces_of(place_ref, own_ref, over_ref):
        if side == 0:
            fc2_ref[aligned(2 * core + half, rows), :] = full(ref[:rows])
        else:
            fc1_ref[aligned(core, rows), half * cols : (half + 1) * cols] = full(ref[:rows])
        put_heads(ref[rows:], core, side, half, qkv_ref, out_w_ref)


def last_whole_kernel(
    place_ref, own_ref, over_ref, qkv_ref, out_w_ref, vec_ref, up_sum_ref, bias_sum_ref,
    bridge_ref, pos_ref, dec_vec_ref, dec_up_sum_ref, dec_bias_sum_ref, rows_ref, small_ref,
):
    few = rows_ref.shape[0] // 2
    rows = qkv_ref.shape[1] // 4 + few
    width = own_ref.shape[3]
    wide, cols = 2 * qkv_ref.shape[2], bridge_ref.shape[1]
    rest = (own_ref.shape[2] - rows * (wide // width)) * width // cols
    quarter, part = bridge_ref.shape[0] // 4, small_ref.shape[0] // 4

    def take(ref, row, count, lanes):
        return jnp.concatenate(
            [ref[row + i * count : row + (i + 1) * count] for i in range(lanes // width)], axis=1
        )

    for ref, core, side, half in pieces_of(place_ref, own_ref, over_ref):
        heads = take(ref, 0, rows, wide)
        put_heads(heads[: rows - few], core, side, half, qkv_ref, out_w_ref)
        block = take(ref, rows * (wide // width), rest, cols)
        index = 2 * core + side
        start = pl.multiple_of(index * quarter, 8)
        if half == 0:
            bridge_ref[pl.ds(start, rest), :] = full(block)
        else:
            left = quarter - rest
            bridge_ref[pl.ds(start + rest, left), :] = full(block[:left])
            small_ref[aligned(index, part), :] = full(block[left:])
    for half in range(2):
        rows_ref[half * few : (half + 1) * few] = pair(
            take(own_ref.at[0, half], 0, rows, wide)[rows - few :],
            take(over_ref.at[0, half], 0, rows, wide)[rows - few :],
        )
    vec_ref[...] = rows_ref[0:6]
    take_rows(rows_ref, 6, up_sum_ref, bias_sum_ref)
    pos_ref[...] = small_ref[0:PATCHES]
    dec_vec_ref[...] = small_ref[PAD_D : PAD_D + 8]
    take_rows(small_ref, PAD_D + 8, dec_up_sum_ref, dec_bias_sum_ref)


def enc_hidden_whole_kernel(place_ref, own_ref, over_ref, fc1_ref, fc2_ref):
    for ref, core, side, half in pieces_of(place_ref, own_ref, over_ref):
        rows = ref.shape[0] // 2
        width = 2 * rows
        fc2_ref[aligned(4 * core + 2 * side + half, rows), :] = full(ref[:rows])
        lanes = aligned(2 * core + side, width)
        for part in range(2):
            fc1_ref[(2 * half + part) * rows : (2 * half + part + 1) * rows, lanes] = full(
                ref[rows:, part * width : (part + 1) * width]
            )


def spread(piece):
    other = flip(piece, 2)
    return piece, other, flip(piece, 1), flip(other, 1)


def pack(order, place, pieces, after=()):
    (packed,) = kernel_call(
        order, pack_kernel, [shaped((2, 2) + pieces[0].shape)], place, *pieces, scalars=1, after=after, name="pack"
    )
    return packed, swap(packed, "section")


def pick(stacked, index):
    return lax.dynamic_index_in_dim(stacked, index, 0, keepdims=False)


def body(
    enc_in, keep_index, image_count, enc_vec, enc_qkv, enc_qv_bias, enc_out_w, enc_fc1, enc_fc1_bias, enc_fc2,
    bridge_w, dec_vec, dec_pos, dec_qkv, dec_qv_bias, dec_out_w, dec_fc1, dec_fc1_bias, dec_fc2, dec_cot,
):
    core = lax.axis_index("section")
    group = lax.axis_index("dp")
    place = jnp.stack([core, group % 2, group // 2 % 2]).astype(jnp.int32)
    images = keep_index.shape[1]
    enc_width, dec_width = bridge_w.shape
    enc_local, dec_local = enc_qkv.shape[2], dec_qkv.shape[2]
    enc_size, dec_size = enc_width // HE, dec_width // HD
    enc_mlp, dec_mlp = enc_fc1.shape[1], dec_fc1.shape[1]
    rows_e, rows_d = images * PAD_E, images * PAD_D
    enc_groups, dec_groups = enc_local // LANES, dec_local // LANES
    enc_heads, dec_heads = LANES // enc_size, LANES // dec_size
    enc_qkv, dec_qkv = jnp.transpose(enc_qkv, (1, 0, 2)), jnp.transpose(dec_qkv, (1, 0, 2))
    enc_fc1_bias, dec_fc1_bias = enc_fc1_bias[None], dec_fc1_bias[None]
    own_in = pick(enc_in, core)
    enc_in = jnp.transpose(enc_in, (1, 0, 2))
    keep = jnp.pad(pick(keep_index, core), ((0, 0), (0, PAD_E - VIS)), constant_values=-1)
    cot = pick(dec_cot, core)
    count = pick(image_count, core)
    dec_rows = images * PATCHES

    order = []
    call = functools.partial(kernel_call, order)

    def enc_attend(rows, memory=24):
        return call(
            functools.partial(enc_attend_kernel, images, enc_size),
            [
                shaped((rows_e, enc_width)),
                shaped((rows_e, enc_width)),
                shaped((rows_e, enc_width)),
                shaped((3, rows_e, enc_local)),
                shaped((enc_groups, enc_heads * rows_e, rows_e)),
                shaped((rows_e, enc_local)),
            ],
            place, rows, enc_vec, enc_qkv, enc_qv_bias, enc_out_w,
            scalars=1, memory=memory, name="enc_attend",
        )

    part, x, normed, proj, weights, mix = enc_attend(enc_in, 60)
    part_other = swap(part, "tensor")
    own_in, x = lax.optimization_barrier((own_in, x))
    side_in = flip(own_in, 1)
    side_part, side_x, side_normed, side_proj, side_weights, side_mix = enc_attend(side_in)
    part_two, middle, normed_two, hidden, slope, forward_send = call(
        enc_hidden_kernel,
        [
            shaped((rows_e, enc_width)),
            shaped((rows_e, enc_width), FULL),
            shaped((rows_e, enc_width)),
            shaped((rows_e, enc_mlp)),
            shaped((rows_e, enc_mlp)),
            shaped((rows_e, enc_mlp // 4 + enc_width + enc_width // 2 + enc_local)),
        ],
        place, x, enc_vec, part, part_other, enc_fc1, enc_fc1_bias, normed, mix, enc_fc2,
        scalars=1, name="enc_hidden",
    )
    part_two_other = swap(part_two, "tensor")
    side_part_other = swap(side_part, "tensor")

    (
        dec_part, enc_out, enc_pad, starting, dec_normed, dec_proj, dec_weights, dec_mix,
    ) = call(
        functools.partial(dec_attend_kernel, images, dec_size),
        [
            shaped((rows_d, dec_width)),
            shaped((images * VIS, enc_width)),
            shaped((rows_e, enc_width)),
            shaped((rows_d, dec_width), FULL),
            shaped((rows_d, dec_width)),
            shaped((3, rows_d, dec_local)),
            shaped((images * dec_groups, dec_heads * PAD_D, PAD_D)),
            shaped((rows_d, dec_local)),
        ],
        count, keep, middle, part_two, part_two_other, enc_vec, bridge_w,
        dec_vec, dec_pos, dec_qkv, dec_qv_bias, dec_out_w,
        scalars=1, name="dec_attend",
    )
    dec_part_other = swap(dec_part, "tensor")
    enc_out_over = swap(enc_out, "section")
    forward_over = swap(forward_send, "section")
    side_middle, side_normed_two, side_hidden, side_slope, side_forward_send = call(
        enc_side_hidden_kernel,
        [
            shaped((rows_e, enc_width), FULL),
            shaped((rows_e, enc_width)),
            shaped((rows_e, enc_mlp)),
            shaped((rows_e, enc_mlp)),
            shaped((rows_e, enc_mlp // 4 + enc_width + enc_width // 2 + enc_local)),
        ],
        place, side_x, enc_vec, side_part, side_part_other, enc_fc1, enc_fc1_bias, side_normed, side_mix,
        scalars=1, name="enc_side_hidden",
    )
    (
        dec_part_back, dec_part_two, dec_middle, dec_normed_two, dec_hid, out_low, dec_up, up_sum, out_sum, d1_send,
    ) = call(
        functools.partial(dec_hidden_kernel, images),
        [
            shaped((rows_d, dec_width)),
            shaped((rows_d, dec_width)),
            shaped((rows_d, dec_width), FULL),
            shaped((rows_d, dec_width)),
            shaped((rows_d, dec_mlp)),
            shaped((rows_d, dec_width)),
            shaped((rows_d, dec_mlp)),
            shaped((1, dec_mlp), FULL),
            shaped((1, dec_width), FULL),
            shaped((rows_d, dec_mlp // 2 + dec_width // 2 + dec_mlp + dec_width)),
        ],
        count, place, starting, dec_part, dec_part_other, dec_vec, dec_fc1, dec_fc1_bias, dec_fc2, cot,
        scalars=2, after=[forward_over], name="dec_hidden",
    )

    side_forward_over = swap(side_forward_send, "section")
    d1_over = swap(d1_send, "section")
    dec_part_back_other = swap(dec_part_back, "tensor")
    (enc_out_both,) = call(
        both_cores_kernel, [shaped((images * VIS, 2, enc_width))],
        place, enc_out, enc_out_over, scalars=1, name="enc_out_both",
    )
    d1_mine, d1_theirs = call(
        dec_hidden_weights_kernel,
        [shaped((2, dec_mlp // 4, dec_width))] * 2,
        place, dec_hid, out_low, dec_normed_two, dec_up, d1_over,
        scalars=1, after=[side_forward_over], name="dec_hidden_weights",
    )
    d1_arrived = flip(d1_theirs, 1)
    dec_part_one, dec_middle_grad, dec_middle_low, dec_stacked, middle_sums, dec_bias_sum, d2_send = call(
        functools.partial(dec_attend_back_kernel, images, dec_size),
        [
            shaped((rows_d, dec_width)),
            shaped((rows_d, dec_width), FULL),
            shaped((rows_d, dec_width)),
            shaped((3, rows_d, dec_local)),
            shaped((3, dec_width), FULL),
            shaped((2, dec_local), FULL),
            shaped((rows_d, 4 * dec_local + dec_width)),
        ],
        place, dec_middle, out_low, dec_part_back, dec_part_back_other, dec_vec, dec_proj, dec_weights, dec_qkv, dec_out_w,
        dec_normed, dec_mix,
        scalars=1, name="dec_attend_back",
    )
    d2_over = swap(d2_send, "section")
    dec_part_one_other = swap(dec_part_one, "tensor")
    d1_mine, d1_theirs = fold(order, place, 2, d1_mine, d1_arrived)
    d2_mine, d2_theirs = call(
        dec_head_weights_kernel,
        [shaped((2, dec_width // 4, 2 * dec_local))] * 2,
        place, dec_normed, dec_stacked, dec_mix, dec_middle_low, d2_over,
        scalars=1, name="dec_head_weights",
    )
    d2_arrived = flip(d2_theirs, 1)
    enc_cot, lifted_grad, pos_grad, start_sums = call(
        functools.partial(dec_start_back_kernel, images),
        [
            shaped((rows_e, enc_width)),
            shaped((rows_e, dec_width)),
            shaped((PAD_D, dec_width), FULL),
            shaped((4, dec_width), FULL),
        ],
        count, keep, starting, dec_part_one, dec_part_one_other, dec_vec, dec_middle_grad, bridge_w,
        scalars=1, name="dec_start_back",
    )
    side_cot = flip(enc_cot, 1)
    over_cot = swap(enc_cot, "section")
    d1_mine, d1_theirs = call(
        fold_more_kernel,
        [shaped((dec_mlp // 4 + dec_width // 4, dec_width))] * 2,
        place, d2_mine, d2_arrived, d1_mine, d1_theirs,
        scalars=1, name="fold_more",
    )
    d1_arrived = flip(d1_theirs, 2)
    small_rows = 256
    d3_keep, d3_send = call(
        dec_bridge_weights_kernel,
        [shaped((2, 2, enc_width // 8 + small_rows // 8, dec_width))] * 2,
        place, enc_pad, lifted_grad, pos_grad, start_sums, middle_sums, out_sum, up_sum, dec_bias_sum,
        scalars=1, scratch=[pltpu.VMEM((small_rows, dec_width), FULL)], name="dec_bridge_weights",
    )
    d3_other = swap(d3_send, "section")
    side_cot, d3_keep = lax.optimization_barrier((side_cot, d3_keep))
    side_over_cot = swap(side_cot, "section")

    part, up, up_send = call(
        enc_hidden_back_kernel,
        [
            shaped((2 * rows_e, enc_width)),
            shaped((2 * rows_e, enc_mlp)),
            shaped((2 * rows_e, enc_mlp // 4)),
        ],
        place, enc_cot, side_cot, slope, side_slope, enc_fc1, enc_fc2,
        scalars=1, after=[over_cot], name="enc_hidden_back",
    )
    up_over = swap(up_send, "section")
    part_other = swap(part, "tensor")
    d3_mine, d3_theirs = fold(order, place, 1, d3_keep, d3_other, after=[side_over_cot])
    d3_arrived = flip(d3_theirs, 1)
    e1_mine, e1_theirs = call(
        enc_hidden_weights_kernel,
        [shaped((enc_mlp // 4, enc_width))] * 2,
        place, hidden, side_hidden, enc_cot, side_cot, normed_two, side_normed_two, up,
        forward_over, side_forward_over, over_cot, side_over_cot, up_over,
        scalars=1, name="enc_hidden_weights",
    )
    e1_arrived = flip(e1_theirs, 2)
    d1 = add(order, d1_mine, d1_arrived)
    d1_arrived = cross_start(d1)
    back_part, middle_grad, middle_low, stacked, middle_two_sums, bias_sum, enc_up_sum, e3_send = call(
        functools.partial(enc_attend_back_kernel, images, enc_size),
        [
            shaped((2 * rows_e, enc_width)),
            shaped((2 * rows_e, enc_width), FULL),
            shaped((2 * rows_e, enc_width)),
            shaped((3, 2 * rows_e, enc_local)),
            shaped((4, enc_width), FULL),
            shaped((2, enc_local), FULL),
            shaped((1, enc_mlp), FULL),
            shaped((2 * rows_e, 2 * enc_local)),
        ],
        place, middle, side_middle, enc_cot, side_cot, part, part_other, enc_vec, proj, side_proj,
        weights, side_weights, enc_qkv, enc_out_w, up,
        scalars=1, after=[d3_arrived], name="enc_attend_back",
    )
    e3_over = swap(e3_send, "section")
    back_part_other = swap(back_part, "tensor")
    d1 = cross_end(order, d1, d1_arrived)
    d1_spread = spread(d1)
    e1 = add(order, e1_mine, e1_arrived, [e3_over])
    dec_part_two, e1 = lax.optimization_barrier((dec_part_two, e1))
    dec_part_two_other = swap(dec_part_two, "tensor")
    e1_arrived = cross_start(e1)
    few = 32
    grad_in, small = call(
        functools.partial(enc_start_back_kernel, images),
        [shaped((images * VIS, 1, enc_width), FULL), shaped((few, enc_width))],
        x, side_x, back_part, back_part_other, enc_vec, middle_grad, middle_two_sums, enc_up_sum, bias_sum,
        scratch=[pltpu.VMEM((few, enc_width), FULL)], name="enc_start_back",
    )
    e3_mine, e3_theirs = call(
        last_weights_kernel,
        [
            shaped(
                (
                    ((enc_width // 4 + few // 2) * 2 * enc_local + (enc_width + small_rows) // 8 * dec_width)
                    // (dec_width // 2),
                    dec_width // 2,
                )
            )
        ] * 2,
        place, normed, side_normed, stacked, mix, side_mix, middle_low, forward_over, side_forward_over, e3_over,
        small, d3_mine, d3_arrived,
        scalars=1, after=[d1_spread[1]], name="last_weights",
    )
    e3_arrived = flip(e3_theirs, 2)
    d1_packed = pack(order, place, d1_spread)
    (dec_out,) = call(
        functools.partial(dec_out_kernel, images),
        [shaped((dec_rows, dec_width))],
        count, dec_middle, dec_part_two, dec_part_two_other, dec_vec,
        scalars=1, name="dec_out",
    )
    e1 = cross_end(order, e1, e1_arrived)
    e1_spread = spread(e1)
    e3 = add(order, e3_mine, e3_arrived)
    e3_arrived = cross_start(e3)
    g_dec_fc1, g_dec_fc2, g_dec_qkv, g_dec_out_w = call(
        dec_whole_kernel,
        [shaped(x.shape, FULL) for x in (dec_fc1, dec_fc2, dec_qkv, dec_out_w)],
        place, *d1_packed, scalars=1, name="dec_whole",
    )
    mark(order, e1_spread[1])
    e3 = cross_end(order, e3, e3_arrived)
    e3_spread = spread(e3)
    e1_packed = pack(order, place, e1_spread)
    mark(order, e3_spread[1])
    g_enc_fc1, g_enc_fc2 = call(
        enc_hidden_whole_kernel,
        [shaped(enc_fc1.shape, FULL), shaped(enc_fc2.shape, FULL)],
        place, *e1_packed, scalars=1, name="enc_hidden_whole",
    )
    e3_packed = pack(order, place, e3_spread)
    (
        g_enc_qkv, g_enc_out_w, g_enc_vec, g_enc_fc1_bias, g_enc_qv_bias,
        g_bridge, g_dec_pos, g_dec_vec, g_dec_fc1_bias, g_dec_qv_bias,
    ) = call(
        last_whole_kernel,
        [
            shaped(x.shape, FULL)
            for x in (
                enc_qkv, enc_out_w, enc_vec, enc_fc1_bias, enc_qv_bias,
                bridge_w, dec_pos, dec_vec, dec_fc1_bias, dec_qv_bias,
            )
        ],
        place, *e3_packed, scalars=1,
        scratch=[pltpu.VMEM((few, enc_width), FULL), pltpu.VMEM((small_rows, dec_width), FULL)],
        name="last_whole",
    )

    return (
        jnp.transpose(enc_out_both, (1, 0, 2)),
        dec_out[None],
        jnp.transpose(grad_in, (1, 0, 2)),
        g_enc_vec,
        jnp.transpose(g_enc_qkv, (1, 0, 2)),
        g_enc_qv_bias,
        g_enc_out_w,
        g_enc_fc1,
        g_enc_fc1_bias.reshape(-1),
        g_enc_fc2,
        g_bridge,
        g_dec_vec,
        g_dec_pos,
        jnp.transpose(g_dec_qkv, (1, 0, 2)),
        g_dec_qv_bias,
        g_dec_out_w,
        g_dec_fc1,
        g_dec_fc1_bias.reshape(-1),
        g_dec_fc2,
    )


def solution(mesh):
    return jax.shard_map(
        body,
        mesh=mesh,
        in_specs=(
            P(None, "dp", None),
            P(None, "dp", None),
            P(None, "dp"),
            P(),
            P(None, None, "tensor"),
            P(None, "tensor"),
            P("tensor", None),
            P(None, "tensor"),
            P("tensor"),
            P("tensor", None),
            P(),
            P(),
            P(),
            P(None, None, "tensor"),
            P(None, "tensor"),
            P("tensor", None),
            P(None, "tensor"),
            P("tensor"),
            P("tensor", None),
            P(None, "dp", None),
        ),
        out_specs=(
            P(None, "dp", None),
            P("section", "dp", None),
            P("section", "dp", None),
            P(),
            P(None, None, "tensor"),
            P(None, "tensor"),
            P("tensor", None),
            P(None, "tensor"),
            P("tensor"),
            P("tensor", None),
            P(),
            P(),
            P(),
            P(None, None, "tensor"),
            P(None, "tensor"),
            P("tensor", None),
            P(None, "tensor"),
            P("tensor"),
            P("tensor", None),
        ),
        check_vma=False,
    )
```

```python
import functools
import math

import jax
import jax.numpy as jnp
from jax import lax
from jax.experimental import pallas as pl
from jax.experimental.pallas import tpu as pltpu
from jax.sharding import PartitionSpec as P

HE = 12
HD = 16
PATCHES = 196
VIS = 49
PAD_E = 64
PAD_D = 208
LANES = 128
EPSILON = 1e-06
LOW = jnp.bfloat16
FULL = jnp.float32
MIB = 2**20


def low(values):
    return values.astype(LOW)


def full(values):
    return values.astype(FULL)


def matmul(left, right):
    return jnp.dot(left, right, preferred_element_type=FULL)


def left_product(left, right):
    return lax.dot_general(left, right, (((0,), (0,)), ((), ())), preferred_element_type=FULL)


def right_product(left, right):
    return lax.dot_general(left, right, (((1,), (1,)), ((), ())), preferred_element_type=FULL)


def pair(first, second):
    return full(first) + full(second)


def swap(value, axis):
    return lax.ppermute(value, axis, [(i, i ^ 1) for i in range(lax.axis_size(axis))])


def normalize(values):
    center = values - jnp.mean(values, axis=-1, keepdims=True)
    scale = lax.rsqrt(jnp.mean(center * center, axis=-1, keepdims=True) + EPSILON)
    return center * scale, scale


def norm_back(grad, gain, xhat, scale):
    inner = grad * gain
    return scale * (
        inner
        - jnp.mean(inner, axis=-1, keepdims=True)
        - xhat * jnp.mean(inner * xhat, axis=-1, keepdims=True)
    )


def column_sum(values):
    return jnp.sum(full(values), axis=0, keepdims=True)


def one_hot_rows(padded, length, images, packed_first=False):
    shape = (images * length, images * padded) if packed_first else (images * padded, images * length)
    first = lax.broadcasted_iota(jnp.int32, shape, 0)
    second = lax.broadcasted_iota(jnp.int32, shape, 1)
    packed, wide = (first, second) if packed_first else (second, first)
    hit = None
    for image in range(images):
        here = (
            (packed >= image * length)
            & (packed < (image + 1) * length)
            & (wide - image * padded == packed - image * length)
        )
        hit = here if hit is None else hit | here
    return low(jnp.where(hit, 1.0, 0.0))


def head_masks(head_size):
    lane = lax.broadcasted_iota(jnp.int32, (1, LANES), 1)
    return [
        jnp.where((lane >= j * head_size) & (lane < (j + 1) * head_size), 1.0, 0.0)
        for j in range(LANES // head_size)
    ]


def spread_heads(values, masks):
    wide = full(values)
    return jnp.concatenate([low(wide * mask) for mask in masks], axis=0)


def gather_heads(stacked, masks):
    rows = stacked.shape[0] // len(masks)
    total = None
    for j, mask in enumerate(masks):
        term = stacked[j * rows : (j + 1) * rows] * mask
        total = term if total is None else total + term
    return total


def attend(queries, key_rows, value_rows, masks, allowed, factor):
    scores = right_product(spread_heads(queries, masks), key_rows) * factor
    scores = jnp.where(allowed, scores, -1e30)
    exponent = jnp.exp(scores - jnp.max(scores, axis=-1, keepdims=True))
    weights_low = low(exponent * (1.0 / jnp.sum(exponent, axis=-1, keepdims=True)))
    return weights_low, low(gather_heads(matmul(weights_low, value_rows), masks))


def attend_back(queries, key_rows, value_rows, weights_low, upstream, masks, factor):
    spread_up = spread_heads(upstream, masks)
    weight_grad = right_product(spread_up, value_rows)
    weights = full(weights_low)
    product = weights * weight_grad
    score_grad = low(product - weights * jnp.sum(product, axis=-1, keepdims=True))
    query_grad = gather_heads(matmul(score_grad, key_rows), masks) * factor
    key_grad = left_product(score_grad, spread_heads(queries, masks)) * factor
    value_grad = left_product(weights_low, spread_up)
    return low(query_grad), low(key_grad), low(value_grad)


def same_image(heads, images, padded, length):
    shape = (heads * images * padded, images * padded)
    row = lax.broadcasted_iota(jnp.int32, shape, 0)
    key = lax.broadcasted_iota(jnp.int32, shape, 1)
    hit = None
    for head in range(heads):
        for image in range(images):
            start = (head * images + image) * padded
            here = (
                (row >= start)
                & (row < start + padded)
                & (key >= image * padded)
                & (key < image * padded + length)
            )
            hit = here if hit is None else hit | here
    return hit


def live_rows(count, rows, padded):
    row = lax.broadcasted_iota(jnp.int32, (rows, 1), 0)
    return jnp.where(row < count * padded, 1.0, 0.0)


def kernel_call(order, kernel, outs, *arguments, scalars=0, scratch=(), after=(), memory=24, name=None):
    count = len(arguments)
    before = order[-1:] + list(after)

    def run(*refs):
        mark = count + len(before) + len(outs)
        refs[mark][...] = jnp.zeros((8, LANES), FULL)
        kernel(*refs[:count], *refs[count + len(before) : mark], *refs[mark + 1 :])

    specs = [pl.BlockSpec(memory_space=pltpu.SMEM)] * scalars
    specs += [pl.BlockSpec(memory_space=pltpu.VMEM)] * (count - scalars)
    specs += [pl.BlockSpec(memory_space=pl.ANY)] * len(before)
    results = pl.pallas_call(
        run,
        out_shape=[jax.ShapeDtypeStruct(x.shape, x.dtype) for x in outs] + [shaped((8, LANES), FULL)],
        in_specs=specs,
        out_specs=[pl.BlockSpec(memory_space=pltpu.VMEM)] * (len(outs) + 1),
        scratch_shapes=scratch,
        compiler_params=pltpu.CompilerParams(vmem_limit_bytes=memory * MIB),
        cost_estimate=pl.CostEstimate(flops=30000000000, bytes_accessed=1, transcendentals=0),
        name=name,
    )(*arguments, *before)
    order.append(results[-1])
    return results[:-1]


def chunk(index, size):
    return pl.ds(pl.multiple_of(index * size, LANES), size)


def shaped(shape, dtype=LOW):
    return jax.ShapeDtypeStruct(shape, dtype)


def project_heads(normed, qkv_ref, bias, proj_ref, width):
    queries = low(matmul(normed, qkv_ref[0]) + bias[0:1])
    key_rows = low(matmul(normed, qkv_ref[1]))
    value_rows = low(matmul(normed, qkv_ref[2]) + bias[1:2])
    proj_ref[0] = queries
    proj_ref[1] = key_rows
    proj_ref[2] = value_rows


def enc_attend_kernel(
    images, head_size, place_ref, x_ref, vec_ref, qkv_ref, bias_ref, out_w_ref,
    part_ref, x_out_ref, normed_ref, proj_ref, weights_ref, mix_ref,
):
    width = qkv_ref.shape[2]
    if len(x_ref.shape) == 2:
        rows = x_ref[...]
    else:
        rows = low(jnp.where(place_ref[0] == 0, full(x_ref[:, 0, :]), full(x_ref[:, 1, :])))
    x = matmul(one_hot_rows(PAD_E, VIS, images), rows)
    x_out_ref[...] = low(x)
    vec = full(vec_ref[...])
    xhat, _ = normalize(x)
    normed = low(xhat * vec[0:1] + vec[1:2])
    normed_ref[...] = normed
    project_heads(normed, qkv_ref, full(bias_ref[...]), proj_ref, width)
    masks = head_masks(head_size)
    allowed = same_image(len(masks), images, PAD_E, VIS)
    for group in range(width // LANES):
        lanes = slice(group * LANES, (group + 1) * LANES)
        weights_low, mixture = attend(
            proj_ref[0, :, lanes],
            proj_ref[1, :, lanes],
            proj_ref[2, :, lanes],
            masks,
            allowed,
            1.0 / math.sqrt(head_size),
        )
        weights_ref[group] = weights_low
        mix_ref[:, lanes] = mixture
    part_ref[...] = low(matmul(mix_ref[...], out_w_ref[...]))


def mlp_forward(middle, gain, shift, fc1_ref, bias_ref, fc2_ref, normed_ref, hidden_ref, slope_ref):
    xhat, _ = normalize(middle)
    normed = low(xhat * gain + shift)
    normed_ref[...] = normed
    pre = matmul(normed, fc1_ref[...]) + full(bias_ref[...])
    share = 0.5 + 0.5 * lax.erf(pre * math.sqrt(0.5))
    hidden = low(pre * share)
    hidden_ref[...] = hidden
    slope = share + pre * jnp.exp(-0.5 * pre * pre) * (1.0 / math.sqrt(2.0 * math.pi))
    if slope_ref is not None:
        slope_ref[...] = low(slope)
    return None if fc2_ref is None else low(matmul(hidden, fc2_ref[...])), slope


def enc_forward_send(place_ref, first_normed_ref, mix_ref, normed_ref, hidden_ref, send_ref):
    core, side = 1 - place_ref[0], place_ref[1]
    width, wide = normed_ref.shape[1], hidden_ref.shape[1] // 4
    half = width // 2
    send_ref[:, :wide] = hidden_ref[:, chunk(2 * core + side, wide)]
    send_ref[:, wide : wide + width] = normed_ref[...]
    send_ref[:, wide + width : wide + width + half] = first_normed_ref[:, chunk(core, half)]
    send_ref[:, wide + width + half :] = mix_ref[...]


def enc_hidden_kernel(
    place_ref, x_ref, vec_ref, part_ref, other_ref, fc1_ref, bias_ref, first_normed_ref, mix_ref, fc2_ref,
    part_two_ref, middle_ref, normed_ref, hidden_ref, slope_ref, send_ref,
):
    vec = full(vec_ref[...])
    middle = full(x_ref[...]) + pair(part_ref[...], other_ref[...]) + vec[2:3]
    middle_ref[...] = middle
    part, _ = mlp_forward(
        middle, vec[3:4], vec[4:5], fc1_ref, bias_ref, fc2_ref, normed_ref, hidden_ref, slope_ref
    )
    part_two_ref[...] = part
    enc_forward_send(place_ref, first_normed_ref, mix_ref, normed_ref, hidden_ref, send_ref)


def enc_side_hidden_kernel(
    place_ref, x_ref, vec_ref, part_ref, other_ref, fc1_ref, bias_ref, first_normed_ref, mix_ref,
    middle_ref, normed_ref, hidden_ref, slope_ref, send_ref,
):
    vec = full(vec_ref[...])
    middle = full(x_ref[...]) + pair(part_ref[...], other_ref[...]) + vec[2:3]
    middle_ref[...] = middle
    mlp_forward(middle, vec[3:4], vec[4:5], fc1_ref, bias_ref, None, normed_ref, hidden_ref, slope_ref)
    enc_forward_send(place_ref, first_normed_ref, mix_ref, normed_ref, hidden_ref, send_ref)


def both_cores_kernel(place_ref, own_ref, over_ref, both_ref):
    first = place_ref[0] == 0
    own, over = full(own_ref[...]), full(over_ref[...])
    both_ref[:, 0, :] = low(jnp.where(first, own, over))
    both_ref[:, 1, :] = low(jnp.where(first, over, own))


def selector(keep_ref, image):
    patch = lax.broadcasted_iota(jnp.int32, (PAD_D, PAD_E), 0)
    return jnp.where(patch == keep_ref[image : image + 1, :], 1.0, 0.0)


def dec_attend_kernel(
    images, head_size, count_ref, keep_ref, middle_ref, part_ref, other_ref, enc_vec_ref, bridge_ref,
    vec_ref, pos_ref, qkv_ref, bias_ref, out_w_ref,
    part_out_ref, enc_out_ref, enc_pad_ref, starting_ref, normed_ref, proj_ref, weights_ref, mix_ref,
):
    width = qkv_ref.shape[2]
    vec = full(vec_ref[...])
    encoded = middle_ref[...] + pair(part_ref[...], other_ref[...]) + full(enc_vec_ref[...])[5:6]
    enc_pad = low(encoded * live_rows(count_ref[0], images * PAD_E, PAD_E))
    enc_pad_ref[...] = enc_pad
    enc_out_ref[...] = low(matmul(one_hot_rows(PAD_E, VIS, images, True), enc_pad))
    lifted = matmul(enc_pad, bridge_ref[...]) + vec[0:1]
    lifted_high = low(lifted)
    lifted_rest = low(lifted - full(lifted_high))
    pos = matmul(one_hot_rows(PAD_D, PATCHES, 1), pos_ref[...])
    for image in range(images):
        chosen = selector(keep_ref, image)
        rows = slice(image * PAD_E, (image + 1) * PAD_E)
        placed = matmul(low(chosen), lifted_high[rows]) + matmul(low(chosen), lifted_rest[rows])
        hidden_patch = 1.0 - jnp.sum(chosen, axis=1, keepdims=True)
        starting_ref[image * PAD_D : (image + 1) * PAD_D, :] = placed + hidden_patch * vec[1:2] + pos
    xhat, _ = normalize(starting_ref[...])
    normed = low(xhat * vec[2:3] + vec[3:4])
    normed_ref[...] = normed
    project_heads(normed, qkv_ref, full(bias_ref[...]), proj_ref, width)
    masks = head_masks(head_size)
    allowed = lax.broadcasted_iota(jnp.int32, (1, PAD_D), 1) < PATCHES
    groups = width // LANES
    for image in range(images):
        rows = slice(image * PAD_D, (image + 1) * PAD_D)
        for group in range(groups):
            lanes = slice(group * LANES, (group + 1) * LANES)
            weights_low, mixture = attend(
                proj_ref[0, rows, lanes],
                proj_ref[1, rows, lanes],
                proj_ref[2, rows, lanes],
                masks,
                allowed,
                1.0 / math.sqrt(head_size),
            )
            weights_ref[image * groups + group] = weights_low
            mix_ref[rows, lanes] = mixture
    part_out_ref[...] = low(matmul(mix_ref[...], out_w_ref[...]))


def dec_hidden_kernel(
    images, count_ref, place_ref, starting_ref, part_ref, other_ref, vec_ref, fc1_ref, bias_ref, fc2_ref, cot_ref,
    part_back_ref, part_two_ref, middle_ref, normed_ref, hidden_ref, out_low_ref, up_ref,
    up_sum_ref, out_sum_ref, send_ref,
):
    vec = full(vec_ref[...])
    middle = starting_ref[...] + pair(part_ref[...], other_ref[...]) + vec[4:5]
    middle_ref[...] = middle
    part, slope = mlp_forward(
        middle, vec[5:6], vec[6:7], fc1_ref, bias_ref, fc2_ref, normed_ref, hidden_ref, None
    )
    part_two_ref[...] = part
    spread = matmul(one_hot_rows(PAD_D, PATCHES, images), cot_ref[...])
    out_low = low(spread * live_rows(count_ref[0], images * PAD_D, PAD_D))
    out_low_ref[...] = out_low
    up_grad = low(slope * right_product(out_low, fc2_ref[...]))
    up_ref[...] = up_grad
    part_back_ref[...] = low(right_product(up_grad, fc1_ref[...]))
    up_sum_ref[...] = column_sum(up_grad)
    out_sum_ref[...] = column_sum(out_low)
    core = 1 - place_ref[0]
    width, wide = out_low.shape[1], up_grad.shape[1]
    half = width // 2
    send_ref[:, : wide // 2] = hidden_ref[:, chunk(core, wide // 2)]
    send_ref[:, wide // 2 : wide // 2 + half] = normed_ref[:, chunk(core, half)]
    send_ref[:, wide // 2 + half : wide // 2 + half + wide] = up_grad
    send_ref[:, wide // 2 + half + wide :] = out_low


def dec_out_kernel(images, count_ref, middle_ref, part_ref, other_ref, vec_ref, out_ref):
    decoded = middle_ref[...] + pair(part_ref[...], other_ref[...]) + full(vec_ref[...])[7:8]
    decoded = low(decoded * live_rows(count_ref[0], images * PAD_D, PAD_D))
    out_ref[...] = low(matmul(one_hot_rows(PAD_D, PATCHES, images, True), decoded))


def attention_back(
    first_row, images, padded, together, head_size, mixture_grad, proj_ref, weights_ref, stacked_ref
):
    masks = head_masks(head_size)
    groups = proj_ref.shape[2] // LANES
    step = images if together else 1
    for first in range(0, images, step):
        rows = slice(first * padded, (first + step) * padded)
        out_rows = slice(first_row + first * padded, first_row + (first + step) * padded)
        for group in range(groups):
            lanes = slice(group * LANES, (group + 1) * LANES)
            grads = attend_back(
                proj_ref[0, rows, lanes],
                proj_ref[1, rows, lanes],
                proj_ref[2, rows, lanes],
                weights_ref[first // step * groups + group],
                mixture_grad[out_rows, lanes],
                masks,
                1.0 / math.sqrt(head_size),
            )
            for j in range(3):
                stacked_ref[j, out_rows, lanes] = grads[j]


def normed_back(stacked_ref, qkv_ref):
    total = right_product(stacked_ref[0], qkv_ref[0])
    for j in (1, 2):
        total = total + right_product(stacked_ref[j], qkv_ref[j])
    return low(total)


def dec_attend_back_kernel(
    images, head_size, place_ref, middle_ref, out_low_ref, part_in_ref, other_ref, vec_ref, proj_ref, weights_ref,
    qkv_ref, out_w_ref, normed_ref, mix_ref,
    part_ref, middle_grad_ref, middle_low_ref, stacked_ref, sums_ref, bias_sum_ref, send_ref,
):
    vec = full(vec_ref[...])
    two_grad = pair(part_in_ref[...], other_ref[...])
    xhat, scale = normalize(middle_ref[...])
    middle_grad = full(out_low_ref[...]) + norm_back(two_grad, vec[5:6], xhat, scale)
    middle_grad_ref[...] = middle_grad
    middle_low = low(middle_grad)
    middle_low_ref[...] = middle_low
    mixture_grad = low(right_product(middle_low, out_w_ref[...]))
    attention_back(0, images, PAD_D, False, head_size, mixture_grad, proj_ref, weights_ref, stacked_ref)
    part_ref[...] = normed_back(stacked_ref, qkv_ref)
    core = 1 - place_ref[0]
    width = mix_ref.shape[1]
    half = middle_low.shape[1] // 2
    for j in range(3):
        send_ref[:, j * width : (j + 1) * width] = stacked_ref[j]
    send_ref[:, 3 * width : 4 * width] = mix_ref[...]
    send_ref[:, 4 * width : 4 * width + half] = normed_ref[:, chunk(core, half)]
    send_ref[:, 4 * width + half :] = middle_low_ref[:, chunk(core, half)]
    sums_ref[0:1] = column_sum(middle_grad)
    sums_ref[1:2] = column_sum(two_grad * xhat)
    sums_ref[2:3] = column_sum(two_grad)
    bias_sum_ref[0:1] = column_sum(stacked_ref[0])
    bias_sum_ref[1:2] = column_sum(stacked_ref[2])


def dec_start_back_kernel(
    images, count_ref, keep_ref, starting_ref, part_ref, other_ref, vec_ref, middle_grad_ref, bridge_ref,
    enc_cot_ref, lifted_ref, pos_ref, sums_ref,
):
    vec = full(vec_ref[...])
    one_grad = pair(part_ref[...], other_ref[...])
    xhat, scale = normalize(starting_ref[...])
    starting_grad = middle_grad_ref[...] + norm_back(one_grad, vec[2:3], xhat, scale)
    sums_ref[2:3] = column_sum(one_grad * xhat)
    sums_ref[3:4] = column_sum(one_grad)
    token = None
    total = None
    for image in range(images):
        grad = starting_grad[image * PAD_D : (image + 1) * PAD_D]
        chosen = selector(keep_ref, image)
        hidden_patch = 1.0 - jnp.sum(chosen, axis=1, keepdims=True)
        term = column_sum(hidden_patch * grad)
        token = term if token is None else token + term
        total = grad if total is None else total + grad
        lifted_ref[image * PAD_E : (image + 1) * PAD_E, :] = low(left_product(low(chosen), low(grad)))
    pos_ref[...] = total
    lifted_grad = lifted_ref[...]
    sums_ref[0:1] = column_sum(lifted_grad)
    sums_ref[1:2] = token
    handed = right_product(lifted_grad, bridge_ref[...])
    enc_cot_ref[...] = low(handed * live_rows(count_ref[0], images * PAD_E, PAD_E))


def enc_hidden_back_kernel(
    place_ref, cot_a, cot_b, slope_a, slope_b, fc1_ref, fc2_ref, part_ref, up_ref, send_ref
):
    slope = jnp.concatenate([slope_a[...], slope_b[...]], axis=0)
    up_grad = low(full(slope) * right_product(stacked_rows(cot_a, cot_b), fc2_ref[...]))
    up_ref[...] = up_grad
    part_ref[...] = low(right_product(up_grad, fc1_ref[...]))
    send_ref[...] = up_ref[:, chunk(2 * (1 - place_ref[0]) + place_ref[1], send_ref.shape[1])]


def enc_attend_back_kernel(
    images, head_size, place_ref, middle_a, middle_b, cot_a, cot_b, part_in_ref, other_ref, vec_ref, proj_a, proj_b,
    weights_a, weights_b, qkv_ref, out_w_ref, up_ref,
    part_ref, middle_grad_ref, middle_low_ref, stacked_ref, sums_ref, bias_sum_ref, up_sum_ref, send_ref,
):
    vec = full(vec_ref[...])
    own = middle_a.shape[0]
    cot = full(stacked_rows(cot_a, cot_b))
    two_grad = pair(part_in_ref[...], other_ref[...])
    xhat, scale = normalize(stacked_rows(middle_a, middle_b))
    middle_grad = cot + norm_back(two_grad, vec[3:4], xhat, scale)
    middle_grad_ref[...] = middle_grad
    middle_low = low(middle_grad)
    middle_low_ref[...] = middle_low
    mixture_grad = low(right_product(middle_low, out_w_ref[...]))
    attention_back(0, images, PAD_E, True, head_size, mixture_grad, proj_a, weights_a, stacked_ref)
    attention_back(own, images, PAD_E, True, head_size, mixture_grad, proj_b, weights_b, stacked_ref)
    part_ref[...] = normed_back(stacked_ref, qkv_ref)
    width = qkv_ref.shape[2]

    @pl.when(place_ref[1] == 0)
    def _():
        send_ref[:, :width] = stacked_ref[0]
        send_ref[:, width:] = stacked_ref[1]

    @pl.when(place_ref[1] == 1)
    def _():
        send_ref[:, :width] = stacked_ref[2]
        send_ref[:, width:] = middle_low_ref[:, chunk(1 - place_ref[0], width)]

    sums_ref[0:1] = column_sum(middle_grad)
    sums_ref[1:2] = column_sum(two_grad * xhat)
    sums_ref[2:3] = column_sum(two_grad)
    sums_ref[3:4] = column_sum(cot)
    bias_sum_ref[0:1] = column_sum(stacked_ref[0])
    bias_sum_ref[1:2] = column_sum(stacked_ref[2])
    up_sum_ref[...] = column_sum(up_ref[...])


def enc_start_back_kernel(
    images, x_a, x_b, part_ref, other_ref, vec_ref, middle_grad_ref, sums_ref, up_sum_ref, bias_sum_ref,
    grad_in_ref, small_ref, rows_ref,
):
    vec = full(vec_ref[...])
    own = x_a.shape[0]
    one_grad = pair(part_ref[...], other_ref[...])
    xhat, scale = normalize(full(stacked_rows(x_a, x_b)))
    grad = middle_grad_ref[:own] + norm_back(one_grad[:own], vec[0:1], xhat[:own], scale[:own])
    take = full(one_hot_rows(PAD_E, VIS, images, True))
    grad_in_ref[:, 0, :] = jnp.dot(
        take, grad, preferred_element_type=FULL, precision=lax.Precision.HIGHEST
    )
    rows_ref[...] = jnp.zeros_like(rows_ref)
    rows_ref[0:1] = column_sum(one_grad * xhat)
    rows_ref[1:2] = column_sum(one_grad)
    rows_ref[2:6] = sums_ref[...]
    put_rows(rows_ref, 6, up_sum_ref, bias_sum_ref)
    small_ref[...] = low(rows_ref[...])


def tall(*parts):
    return jnp.concatenate(parts, axis=0)


def by_side(place_ref, mine_ref, theirs_ref, blocks):
    first = place_ref[1] == 0
    rows = mine_ref.shape[1]
    for part in range(2):
        zero, one = (low(block[part * rows : (part + 1) * rows]) for block in blocks)
        mine_ref[part] = jnp.where(first, zero, one)
        theirs_ref[part] = jnp.where(first, one, zero)


def dec_hidden_weights_kernel(
    place_ref, hidden_ref, out_low_ref, normed_ref, up_ref, over_ref, mine_ref, theirs_ref
):
    core = place_ref[0]
    width, wide = out_low_ref.shape[1], up_ref.shape[1]
    half = width // 2
    over_up = over_ref[:, wide // 2 + half : wide // 2 + half + wide]
    over_out = over_ref[:, wide // 2 + half + wide :]
    down = left_product(
        tall(hidden_ref[:, chunk(core, wide // 2)], over_ref[:, : wide // 2]), tall(out_low_ref[...], over_out)
    )
    up = left_product(
        tall(normed_ref[:, chunk(core, half)], over_ref[:, wide // 2 : wide // 2 + half]),
        tall(up_ref[...], over_up),
    )
    by_side(place_ref, mine_ref, theirs_ref, (down, tall(up[:, :width], up[:, width:])))


def dec_head_weights_kernel(
    place_ref, normed_ref, stacked_ref, mix_ref, middle_low_ref, over_ref, mine_ref, theirs_ref
):
    core = place_ref[0]
    width = mix_ref.shape[1]
    half = normed_ref.shape[1] // 2
    left = tall(normed_ref[:, chunk(core, half)], over_ref[:, 4 * width : 4 * width + half])
    grads = [
        left_product(left, tall(stacked_ref[j], over_ref[:, j * width : (j + 1) * width])) for j in range(3)
    ]
    out = left_product(
        tall(mix_ref[...], over_ref[:, 3 * width : 4 * width]),
        tall(middle_low_ref[:, chunk(core, half)], over_ref[:, 4 * width + half :]),
    )
    by_side(
        place_ref, mine_ref, theirs_ref,
        (jnp.concatenate(grads[:2], axis=1), jnp.concatenate([grads[2], out], axis=1)),
    )


def put_rows(rows_ref, row, up_sum_ref, bias_sum_ref):
    cols = rows_ref.shape[1]
    for piece in range(up_sum_ref.shape[1] // cols):
        rows_ref[row : row + 1] = up_sum_ref[:, piece * cols : (piece + 1) * cols]
        row += 1
    width = bias_sum_ref.shape[1]
    for piece in range(2):
        here, lane = row + piece * width // cols, piece * width % cols
        rows_ref[here : here + 1, lane : lane + width] = bias_sum_ref[piece : piece + 1]


def take_rows(rows_ref, row, up_sum_ref, bias_sum_ref):
    cols = rows_ref.shape[1]
    for piece in range(up_sum_ref.shape[1] // cols):
        up_sum_ref[:, piece * cols : (piece + 1) * cols] = rows_ref[row : row + 1]
        row += 1
    width = bias_sum_ref.shape[1]
    for piece in range(2):
        here, lane = row + piece * width // cols, piece * width % cols
        bias_sum_ref[piece : piece + 1] = rows_ref[here : here + 1, lane : lane + width]


def dec_bridge_weights_kernel(
    place_ref, enc_pad_ref, lifted_ref, pos_ref, sums_ref, middle_sums_ref, out_sum_ref, up_sum_ref,
    bias_sum_ref, keep_ref, send_ref, small_ref,
):
    core = place_ref[0]
    cols = lifted_ref.shape[1]
    bridge = low(left_product(enc_pad_ref[...], lifted_ref[...]))
    quarter = bridge.shape[0] // 4
    small_ref[...] = jnp.zeros_like(small_ref)
    small_ref[0:PAD_D] = pos_ref[...]
    row = PAD_D
    for ref, count in ((sums_ref, 4), (middle_sums_ref, 3), (out_sum_ref, 1)):
        small_ref[row : row + count] = ref[...]
        row += count
    put_rows(small_ref, row, up_sum_ref, bias_sum_ref)
    few = small_ref.shape[0] // 4
    first = core == 0

    def block(index):
        return jnp.concatenate(
            [bridge[index * quarter : (index + 1) * quarter], low(small_ref[index * few : (index + 1) * few])],
            axis=0,
        )

    for side in range(2):
        zero, one = block(side), block(2 + side)
        half = zero.shape[0] // 2
        for part in range(2):
            rows = slice(part * half, (part + 1) * half)
            keep_ref[side, part] = jnp.where(first, zero[rows], one[rows])
            send_ref[side, part] = jnp.where(first, one[rows], zero[rows])


def stacked_rows(first, second, lanes=slice(None)):
    return jnp.concatenate([first[:, lanes], second[:, lanes]], axis=0)


def enc_hidden_weights_kernel(
    place_ref, hidden_a, hidden_b, cot_a, cot_b, normed_a, normed_b, up_ref,
    forward_a, forward_b, over_cot_a, over_cot_b, over_up, mine_ref, theirs_ref,
):
    core, side, half = place_ref[0], place_ref[1], place_ref[2]
    rows = mine_ref.shape[0] // 2
    width = 2 * rows
    features = cot_a.shape[1]
    lanes = chunk(2 * core + side, width)
    down = low(
        left_product(
            tall(hidden_a[:, lanes], hidden_b[:, lanes], forward_a[:, :width], forward_b[:, :width]),
            tall(cot_a[...], cot_b[...], over_cot_a[...], over_cot_b[...]),
        )
    )
    here = slice(width, width + features)
    up = low(
        left_product(
            tall(normed_a[...], normed_b[...], forward_a[:, here], forward_b[:, here]),
            tall(up_ref[:, lanes], over_up[...]),
        )
    )
    for part in range(2):
        block = (
            down[part * rows : (part + 1) * rows],
            up[2 * part * rows : (2 * part + 1) * rows],
            up[(2 * part + 1) * rows : (2 * part + 2) * rows],
        )
        for ref, index in ((mine_ref, half), (theirs_ref, 1 - half)):

            @pl.when(index == part)
            def _(ref=ref, block=block):
                ref[:rows] = block[0]
                ref[rows:, :width] = block[1]
                ref[rows:, width:] = block[2]


def last_weights_kernel(
    place_ref, normed_a, normed_b, stacked_ref, mix_a, mix_b, middle_low_ref, forward_a, forward_b, over_ref,
    small_ref, rest_mine, rest_other, mine_ref, theirs_ref,
):
    core, half = place_ref[0], place_ref[2]
    width = mix_a.shape[1]
    half_width = normed_a.shape[1] // 2
    lanes = chunk(core, half_width)
    start = forward_a.shape[1] - half_width - width
    left = tall(
        normed_a[:, lanes], normed_b[:, lanes],
        forward_a[:, start : start + half_width], forward_b[:, start : start + half_width],
    )
    few = small_ref.shape[0] // 2
    columns = mine_ref.shape[1]

    def put(first, second):
        rows = first.shape[0] // 2
        for part in range(2):
            here = slice(part * rows, (part + 1) * rows)
            block = jnp.concatenate([first[here], second[here]], axis=1)
            block = tall(low(block), small_ref[part * few : (part + 1) * few])
            for ref, index in ((mine_ref, half), (theirs_ref, 1 - half)):

                @pl.when(index == part)
                def _(ref=ref, block=block):
                    for i in range(block.shape[1] // columns):
                        ref[i * block.shape[0] : (i + 1) * block.shape[0]] = block[
                            :, i * columns : (i + 1) * columns
                        ]

    @pl.when(place_ref[1] == 0)
    def _():
        put(
            left_product(left, tall(stacked_ref[0], over_ref[:, :width])),
            left_product(left, tall(stacked_ref[1], over_ref[:, width:])),
        )

    @pl.when(place_ref[1] == 1)
    def _():
        put(
            left_product(left, tall(stacked_ref[2], over_ref[:, :width])),
            left_product(
                tall(mix_a[...], mix_b[...], forward_a[:, start + half_width :], forward_b[:, start + half_width :]),
                tall(middle_low_ref[:, lanes], over_ref[:, width:]),
            ),
        )

    for ref, index in ((mine_ref, half), (theirs_ref, 1 - half)):
        total = low(pair(rest_mine[index], rest_other[index]))
        count = total.shape[0]
        row = ref.shape[0] - count * (total.shape[1] // columns)
        for i in range(total.shape[1] // columns):
            ref[row + i * count : row + (i + 1) * count] = total[:, i * columns : (i + 1) * columns]


def fold_kernel(axis, place_ref, *refs):
    index = place_ref[axis]
    mine_ref, theirs_ref = refs[-2:]
    rows = 0
    for keep_ref, other_ref in zip(refs[:-2:2], refs[1:-2:2]):
        here = (slice(None),) * (len(keep_ref.shape) - 3) + (slice(rows, rows + keep_ref.shape[-2]),)
        rows += keep_ref.shape[-2]
        mine_ref[here] = low(pair(keep_ref[index], other_ref[index]))
        theirs_ref[here] = low(pair(keep_ref[1 - index], other_ref[1 - index]))


def fold_more_kernel(place_ref, keep_ref, other_ref, before_mine, before_theirs, mine_ref, theirs_ref):
    index = place_ref[2]
    rows = before_mine.shape[0]
    mine_ref[:rows] = before_mine[...]
    theirs_ref[:rows] = before_theirs[...]
    mine_ref[rows:] = low(pair(keep_ref[index], other_ref[index]))
    theirs_ref[rows:] = low(pair(keep_ref[1 - index], other_ref[1 - index]))


def add_kernel(first_ref, second_ref, sum_ref):
    sum_ref[...] = low(pair(first_ref[...], second_ref[...]))


def fold(order, place, axis, *arrays, after=()):
    shape = arrays[0].shape[1:-2] + (sum(x.shape[-2] for x in arrays[::2]), arrays[0].shape[-1])
    return kernel_call(
        order, functools.partial(fold_kernel, axis), [shaped(shape)] * 2, place, *arrays,
        scalars=1, after=after, name="fold",
    )


def add(order, first, second, after=()):
    return kernel_call(order, add_kernel, [shaped(first.shape)], first, second, after=after, name="add")[0]


def mark_kernel(out_ref):
    out_ref[...] = jnp.zeros_like(out_ref)


def mark(order, *values):
    kernel_call(order, mark_kernel, [shaped((8, LANES), FULL)], after=values, name="mark")


def flip(value, step):
    return lax.ppermute(value, "dp", [(i, i ^ step) for i in range(lax.axis_size("dp"))])


def cross_start(value):
    return flip(value, 4) if lax.axis_size("dp") > 4 else jnp.zeros_like(value)


def cross_end(order, value, arrived, after=()):
    value = add(order, value, arrived, after)
    step = 8
    while step < lax.axis_size("dp"):
        value = add(order, value, flip(value, step))
        step *= 2
    return value


def pack_kernel(place_ref, mine_ref, other_ref, across_ref, there_ref, packed_ref):
    side, half = place_ref[1], place_ref[2]
    packed_ref[side, half] = mine_ref[...]
    packed_ref[side, 1 - half] = other_ref[...]
    packed_ref[1 - side, half] = across_ref[...]
    packed_ref[1 - side, 1 - half] = there_ref[...]


def pieces_of(place_ref, own_ref, over_ref):
    core = place_ref[0]
    return [
        (ref.at[side, half], index, side, half)
        for ref, index in ((own_ref, core), (over_ref, 1 - core))
        for side in range(2)
        for half in range(2)
    ]


def aligned(index, size):
    return pl.ds(pl.multiple_of(index * size, size), size)


def put_heads(block, core, side, half, qkv_ref, out_w_ref):
    rows, width = block.shape[0], qkv_ref.shape[2]
    here = aligned(2 * core + half, rows)
    if side == 0:
        qkv_ref[0, here, :] = full(block[:, :width])
        qkv_ref[1, here, :] = full(block[:, width:])
    else:
        qkv_ref[2, here, :] = full(block[:, :width])
        out_w_ref[half * rows : (half + 1) * rows, aligned(core, width)] = full(block[:, width:])


def dec_whole_kernel(place_ref, own_ref, over_ref, fc1_ref, fc2_ref, qkv_ref, out_w_ref):
    rows, cols = fc1_ref.shape[0] // 2, fc1_ref.shape[1] // 2
    for ref, core, side, half in pieces_of(place_ref, own_ref, over_ref):
        if side == 0:
            fc2_ref[aligned(2 * core + half, rows), :] = full(ref[:rows])
        else:
            fc1_ref[aligned(core, rows), half * cols : (half + 1) * cols] = full(ref[:rows])
        put_heads(ref[rows:], core, side, half, qkv_ref, out_w_ref)


def last_whole_kernel(
    place_ref, own_ref, over_ref, qkv_ref, out_w_ref, vec_ref, up_sum_ref, bias_sum_ref,
    bridge_ref, pos_ref, dec_vec_ref, dec_up_sum_ref, dec_bias_sum_ref, rows_ref, small_ref,
):
    few = rows_ref.shape[0] // 2
    rows = qkv_ref.shape[1] // 4 + few
    width = own_ref.shape[3]
    wide, cols = 2 * qkv_ref.shape[2], bridge_ref.shape[1]
    rest = (own_ref.shape[2] - rows * (wide // width)) * width // cols
    quarter, part = bridge_ref.shape[0] // 4, small_ref.shape[0] // 4

    def take(ref, row, count, lanes):
        return jnp.concatenate(
            [ref[row + i * count : row + (i + 1) * count] for i in range(lanes // width)], axis=1
        )

    for ref, core, side, half in pieces_of(place_ref, own_ref, over_ref):
        heads = take(ref, 0, rows, wide)
        put_heads(heads[: rows - few], core, side, half, qkv_ref, out_w_ref)
        block = take(ref, rows * (wide // width), rest, cols)
        index = 2 * core + side
        start = pl.multiple_of(index * quarter, 8)
        if half == 0:
            bridge_ref[pl.ds(start, rest), :] = full(block)
        else:
            left = quarter - rest
            bridge_ref[pl.ds(start + rest, left), :] = full(block[:left])
            small_ref[aligned(index, part), :] = full(block[left:])
    for half in range(2):
        rows_ref[half * few : (half + 1) * few] = pair(
            take(own_ref.at[0, half], 0, rows, wide)[rows - few :],
            take(over_ref.at[0, half], 0, rows, wide)[rows - few :],
        )
    vec_ref[...] = rows_ref[0:6]
    take_rows(rows_ref, 6, up_sum_ref, bias_sum_ref)
    pos_ref[...] = small_ref[0:PATCHES]
    dec_vec_ref[...] = small_ref[PAD_D : PAD_D + 8]
    take_rows(small_ref, PAD_D + 8, dec_up_sum_ref, dec_bias_sum_ref)


def enc_hidden_whole_kernel(place_ref, own_ref, over_ref, fc1_ref, fc2_ref):
    for ref, core, side, half in pieces_of(place_ref, own_ref, over_ref):
        rows = ref.shape[0] // 2
        width = 2 * rows
        fc2_ref[aligned(4 * core + 2 * side + half, rows), :] = full(ref[:rows])
        lanes = aligned(2 * core + side, width)
        for part in range(2):
            fc1_ref[(2 * half + part) * rows : (2 * half + part + 1) * rows, lanes] = full(
                ref[rows:, part * width : (part + 1) * width]
            )


def spread(piece):
    other = flip(piece, 2)
    return piece, other, flip(piece, 1), flip(other, 1)


def pack(order, place, pieces, after=()):
    (packed,) = kernel_call(
        order, pack_kernel, [shaped((2, 2) + pieces[0].shape)], place, *pieces, scalars=1, after=after, name="pack"
    )
    return packed, swap(packed, "section")


def pick(stacked, index):
    return lax.dynamic_index_in_dim(stacked, index, 0, keepdims=False)


def body(
    enc_in, keep_index, image_count, enc_vec, enc_qkv, enc_qv_bias, enc_out_w, enc_fc1, enc_fc1_bias, enc_fc2,
    bridge_w, dec_vec, dec_pos, dec_qkv, dec_qv_bias, dec_out_w, dec_fc1, dec_fc1_bias, dec_fc2, dec_cot,
):
    core = lax.axis_index("section")
    group = lax.axis_index("dp")
    place = jnp.stack([core, group % 2, group // 2 % 2]).astype(jnp.int32)
    images = keep_index.shape[1]
    enc_width, dec_width = bridge_w.shape
    enc_local, dec_local = enc_qkv.shape[2], dec_qkv.shape[2]
    enc_size, dec_size = enc_width // HE, dec_width // HD
    enc_mlp, dec_mlp = enc_fc1.shape[1], dec_fc1.shape[1]
    rows_e, rows_d = images * PAD_E, images * PAD_D
    enc_groups, dec_groups = enc_local // LANES, dec_local // LANES
    enc_heads, dec_heads = LANES // enc_size, LANES // dec_size
    enc_qkv, dec_qkv = jnp.transpose(enc_qkv, (1, 0, 2)), jnp.transpose(dec_qkv, (1, 0, 2))
    enc_fc1_bias, dec_fc1_bias = enc_fc1_bias[None], dec_fc1_bias[None]
    raw_in = enc_in
    enc_in = jnp.transpose(enc_in, (1, 0, 2))
    keep = jnp.pad(pick(keep_index, core), ((0, 0), (0, PAD_E - VIS)), constant_values=-1)
    cot = pick(dec_cot, core)
    count = pick(image_count, core)
    dec_rows = images * PATCHES

    order = []
    call = functools.partial(kernel_call, order)

    def enc_attend(rows, memory=24):
        return call(
            functools.partial(enc_attend_kernel, images, enc_size),
            [
                shaped((rows_e, enc_width)),
                shaped((rows_e, enc_width)),
                shaped((rows_e, enc_width)),
                shaped((3, rows_e, enc_local)),
                shaped((enc_groups, enc_heads * rows_e, rows_e)),
                shaped((rows_e, enc_local)),
            ],
            place, rows, enc_vec, enc_qkv, enc_qv_bias, enc_out_w,
            scalars=1, memory=memory, name="enc_attend",
        )

    part, x, normed, proj, weights, mix = enc_attend(enc_in, 60)
    part_other = swap(part, "tensor")
    raw_in, x = lax.optimization_barrier((raw_in, x))
    side_in = flip(pick(raw_in, core), 1)
    side_part, side_x, side_normed, side_proj, side_weights, side_mix = enc_attend(side_in)
    part_two, middle, normed_two, hidden, slope, forward_send = call(
        enc_hidden_kernel,
        [
            shaped((rows_e, enc_width)),
            shaped((rows_e, enc_width), FULL),
            shaped((rows_e, enc_width)),
            shaped((rows_e, enc_mlp)),
            shaped((rows_e, enc_mlp)),
            shaped((rows_e, enc_mlp // 4 + enc_width + enc_width // 2 + enc_local)),
        ],
        place, x, enc_vec, part, part_other, enc_fc1, enc_fc1_bias, normed, mix, enc_fc2,
        scalars=1, name="enc_hidden",
    )
    part_two_other = swap(part_two, "tensor")
    side_part_other = swap(side_part, "tensor")

    (
        dec_part, enc_out, enc_pad, starting, dec_normed, dec_proj, dec_weights, dec_mix,
    ) = call(
        functools.partial(dec_attend_kernel, images, dec_size),
        [
            shaped((rows_d, dec_width)),
            shaped((images * VIS, enc_width)),
            shaped((rows_e, enc_width)),
            shaped((rows_d, dec_width), FULL),
            shaped((rows_d, dec_width)),
            shaped((3, rows_d, dec_local)),
            shaped((images * dec_groups, dec_heads * PAD_D, PAD_D)),
            shaped((rows_d, dec_local)),
        ],
        count, keep, middle, part_two, part_two_other, enc_vec, bridge_w,
        dec_vec, dec_pos, dec_qkv, dec_qv_bias, dec_out_w,
        scalars=1, name="dec_attend",
    )
    dec_part_other = swap(dec_part, "tensor")
    enc_out_over = swap(enc_out, "section")
    forward_over = swap(forward_send, "section")
    side_middle, side_normed_two, side_hidden, side_slope, side_forward_send = call(
        enc_side_hidden_kernel,
        [
            shaped((rows_e, enc_width), FULL),
            shaped((rows_e, enc_width)),
            shaped((rows_e, enc_mlp)),
            shaped((rows_e, enc_mlp)),
            shaped((rows_e, enc_mlp // 4 + enc_width + enc_width // 2 + enc_local)),
        ],
        place, side_x, enc_vec, side_part, side_part_other, enc_fc1, enc_fc1_bias, side_normed, side_mix,
        scalars=1, name="enc_side_hidden",
    )
    (
        dec_part_back, dec_part_two, dec_middle, dec_normed_two, dec_hid, out_low, dec_up, up_sum, out_sum, d1_send,
    ) = call(
        functools.partial(dec_hidden_kernel, images),
        [
            shaped((rows_d, dec_width)),
            shaped((rows_d, dec_width)),
            shaped((rows_d, dec_width), FULL),
            shaped((rows_d, dec_width)),
            shaped((rows_d, dec_mlp)),
            shaped((rows_d, dec_width)),
            shaped((rows_d, dec_mlp)),
            shaped((1, dec_mlp), FULL),
            shaped((1, dec_width), FULL),
            shaped((rows_d, dec_mlp // 2 + dec_width // 2 + dec_mlp + dec_width)),
        ],
        count, place, starting, dec_part, dec_part_other, dec_vec, dec_fc1, dec_fc1_bias, dec_fc2, cot,
        scalars=2, after=[forward_over], name="dec_hidden",
    )

    side_forward_over = swap(side_forward_send, "section")
    d1_over = swap(d1_send, "section")
    dec_part_back_other = swap(dec_part_back, "tensor")
    (enc_out_both,) = call(
        both_cores_kernel, [shaped((images * VIS, 2, enc_width))],
        place, enc_out, enc_out_over, scalars=1, name="enc_out_both",
    )
    d1_mine, d1_theirs = call(
        dec_hidden_weights_kernel,
        [shaped((2, dec_mlp // 4, dec_width))] * 2,
        place, dec_hid, out_low, dec_normed_two, dec_up, d1_over,
        scalars=1, after=[side_forward_over], name="dec_hidden_weights",
    )
    d1_arrived = flip(d1_theirs, 1)
    dec_part_one, dec_middle_grad, dec_middle_low, dec_stacked, middle_sums, dec_bias_sum, d2_send = call(
        functools.partial(dec_attend_back_kernel, images, dec_size),
        [
            shaped((rows_d, dec_width)),
            shaped((rows_d, dec_width), FULL),
            shaped((rows_d, dec_width)),
            shaped((3, rows_d, dec_local)),
            shaped((3, dec_width), FULL),
            shaped((2, dec_local), FULL),
            shaped((rows_d, 4 * dec_local + dec_width)),
        ],
        place, dec_middle, out_low, dec_part_back, dec_part_back_other, dec_vec, dec_proj, dec_weights, dec_qkv, dec_out_w,
        dec_normed, dec_mix,
        scalars=1, name="dec_attend_back",
    )
    d2_over = swap(d2_send, "section")
    dec_part_one_other = swap(dec_part_one, "tensor")
    d1_mine, d1_theirs = fold(order, place, 2, d1_mine, d1_arrived)
    d2_mine, d2_theirs = call(
        dec_head_weights_kernel,
        [shaped((2, dec_width // 4, 2 * dec_local))] * 2,
        place, dec_normed, dec_stacked, dec_mix, dec_middle_low, d2_over,
        scalars=1, name="dec_head_weights",
    )
    d2_arrived = flip(d2_theirs, 1)
    enc_cot, lifted_grad, pos_grad, start_sums = call(
        functools.partial(dec_start_back_kernel, images),
        [
            shaped((rows_e, enc_width)),
            shaped((rows_e, dec_width)),
            shaped((PAD_D, dec_width), FULL),
            shaped((4, dec_width), FULL),
        ],
        count, keep, starting, dec_part_one, dec_part_one_other, dec_vec, dec_middle_grad, bridge_w,
        scalars=1, name="dec_start_back",
    )
    side_cot = flip(enc_cot, 1)
    over_cot = swap(enc_cot, "section")
    d1_mine, d1_theirs = call(
        fold_more_kernel,
        [shaped((dec_mlp // 4 + dec_width // 4, dec_width))] * 2,
        place, d2_mine, d2_arrived, d1_mine, d1_theirs,
        scalars=1, name="fold_more",
    )
    d1_arrived = flip(d1_theirs, 2)
    small_rows = 256
    d3_keep, d3_send = call(
        dec_bridge_weights_kernel,
        [shaped((2, 2, enc_width // 8 + small_rows // 8, dec_width))] * 2,
        place, enc_pad, lifted_grad, pos_grad, start_sums, middle_sums, out_sum, up_sum, dec_bias_sum,
        scalars=1, scratch=[pltpu.VMEM((small_rows, dec_width), FULL)], name="dec_bridge_weights",
    )
    d3_other = swap(d3_send, "section")
    side_cot, d3_keep = lax.optimization_barrier((side_cot, d3_keep))
    side_over_cot = swap(side_cot, "section")

    part, up, up_send = call(
        enc_hidden_back_kernel,
        [
            shaped((2 * rows_e, enc_width)),
            shaped((2 * rows_e, enc_mlp)),
            shaped((2 * rows_e, enc_mlp // 4)),
        ],
        place, enc_cot, side_cot, slope, side_slope, enc_fc1, enc_fc2,
        scalars=1, after=[over_cot], name="enc_hidden_back",
    )
    up_over = swap(up_send, "section")
    part_other = swap(part, "tensor")
    d3_mine, d3_theirs = fold(order, place, 1, d3_keep, d3_other, after=[side_over_cot])
    d3_arrived = flip(d3_theirs, 1)
    e1_mine, e1_theirs = call(
        enc_hidden_weights_kernel,
        [shaped((enc_mlp // 4, enc_width))] * 2,
        place, hidden, side_hidden, enc_cot, side_cot, normed_two, side_normed_two, up,
        forward_over, side_forward_over, over_cot, side_over_cot, up_over,
        scalars=1, name="enc_hidden_weights",
    )
    e1_arrived = flip(e1_theirs, 2)
    d1 = add(order, d1_mine, d1_arrived)
    d1_arrived = cross_start(d1)
    back_part, middle_grad, middle_low, stacked, middle_two_sums, bias_sum, enc_up_sum, e3_send = call(
        functools.partial(enc_attend_back_kernel, images, enc_size),
        [
            shaped((2 * rows_e, enc_width)),
            shaped((2 * rows_e, enc_width), FULL),
            shaped((2 * rows_e, enc_width)),
            shaped((3, 2 * rows_e, enc_local)),
            shaped((4, enc_width), FULL),
            shaped((2, enc_local), FULL),
            shaped((1, enc_mlp), FULL),
            shaped((2 * rows_e, 2 * enc_local)),
        ],
        place, middle, side_middle, enc_cot, side_cot, part, part_other, enc_vec, proj, side_proj,
        weights, side_weights, enc_qkv, enc_out_w, up,
        scalars=1, after=[d3_arrived], name="enc_attend_back",
    )
    e3_over = swap(e3_send, "section")
    back_part_other = swap(back_part, "tensor")
    d1 = cross_end(order, d1, d1_arrived)
    d1_spread = spread(d1)
    e1 = add(order, e1_mine, e1_arrived, [e3_over])
    dec_part_two, e1 = lax.optimization_barrier((dec_part_two, e1))
    dec_part_two_other = swap(dec_part_two, "tensor")
    e1_arrived = cross_start(e1)
    few = 32
    grad_in, small = call(
        functools.partial(enc_start_back_kernel, images),
        [shaped((images * VIS, 1, enc_width), FULL), shaped((few, enc_width))],
        x, side_x, back_part, back_part_other, enc_vec, middle_grad, middle_two_sums, enc_up_sum, bias_sum,
        scratch=[pltpu.VMEM((few, enc_width), FULL)], name="enc_start_back",
    )
    e3_mine, e3_theirs = call(
        last_weights_kernel,
        [
            shaped(
                (
                    ((enc_width // 4 + few // 2) * 2 * enc_local + (enc_width + small_rows) // 8 * dec_width)
                    // (dec_width // 2),
                    dec_width // 2,
                )
            )
        ] * 2,
        place, normed, side_normed, stacked, mix, side_mix, middle_low, forward_over, side_forward_over, e3_over,
        small, d3_mine, d3_arrived,
        scalars=1, after=[d1_spread[1]], name="last_weights",
    )
    e3_arrived = flip(e3_theirs, 2)
    d1_packed = pack(order, place, d1_spread)
    (dec_out,) = call(
        functools.partial(dec_out_kernel, images),
        [shaped((dec_rows, dec_width))],
        count, dec_middle, dec_part_two, dec_part_two_other, dec_vec,
        scalars=1, name="dec_out",
    )
    e1 = cross_end(order, e1, e1_arrived)
    e1_spread = spread(e1)
    e3 = add(order, e3_mine, e3_arrived)
    e3_arrived = cross_start(e3)
    g_dec_fc1, g_dec_fc2, g_dec_qkv, g_dec_out_w = call(
        dec_whole_kernel,
        [shaped(x.shape, FULL) for x in (dec_fc1, dec_fc2, dec_qkv, dec_out_w)],
        place, *d1_packed, scalars=1, name="dec_whole",
    )
    mark(order, e1_spread[1])
    e3 = cross_end(order, e3, e3_arrived)
    e3_spread = spread(e3)
    e1_packed = pack(order, place, e1_spread)
    mark(order, e3_spread[1])
    g_enc_fc1, g_enc_fc2 = call(
        enc_hidden_whole_kernel,
        [shaped(enc_fc1.shape, FULL), shaped(enc_fc2.shape, FULL)],
        place, *e1_packed, scalars=1, name="enc_hidden_whole",
    )
    e3_packed = pack(order, place, e3_spread)
    (
        g_enc_qkv, g_enc_out_w, g_enc_vec, g_enc_fc1_bias, g_enc_qv_bias,
        g_bridge, g_dec_pos, g_dec_vec, g_dec_fc1_bias, g_dec_qv_bias,
    ) = call(
        last_whole_kernel,
        [
            shaped(x.shape, FULL)
            for x in (
                enc_qkv, enc_out_w, enc_vec, enc_fc1_bias, enc_qv_bias,
                bridge_w, dec_pos, dec_vec, dec_fc1_bias, dec_qv_bias,
            )
        ],
        place, *e3_packed, scalars=1,
        scratch=[pltpu.VMEM((few, enc_width), FULL), pltpu.VMEM((small_rows, dec_width), FULL)],
        name="last_whole",
    )

    return (
        jnp.transpose(enc_out_both, (1, 0, 2)),
        dec_out[None],
        jnp.transpose(grad_in, (1, 0, 2)),
        g_enc_vec,
        jnp.transpose(g_enc_qkv, (1, 0, 2)),
        g_enc_qv_bias,
        g_enc_out_w,
        g_enc_fc1,
        g_enc_fc1_bias.reshape(-1),
        g_enc_fc2,
        g_bridge,
        g_dec_vec,
        g_dec_pos,
        jnp.transpose(g_dec_qkv, (1, 0, 2)),
        g_dec_qv_bias,
        g_dec_out_w,
        g_dec_fc1,
        g_dec_fc1_bias.reshape(-1),
        g_dec_fc2,
    )


def solution(mesh):
    return jax.shard_map(
        body,
        mesh=mesh,
        in_specs=(
            P(None, "dp", None),
            P(None, "dp", None),
            P(None, "dp"),
            P(),
            P(None, None, "tensor"),
            P(None, "tensor"),
            P("tensor", None),
            P(None, "tensor"),
            P("tensor"),
            P("tensor", None),
            P(),
            P(),
            P(),
            P(None, None, "tensor"),
            P(None, "tensor"),
            P("tensor", None),
            P(None, "tensor"),
            P("tensor"),
            P("tensor", None),
            P(None, "dp", None),
        ),
        out_specs=(
            P(None, "dp", None),
            P("section", "dp", None),
            P("section", "dp", None),
            P(),
            P(None, None, "tensor"),
            P(None, "tensor"),
            P("tensor", None),
            P(None, "tensor"),
            P("tensor"),
            P("tensor", None),
            P(),
            P(),
            P(),
            P(None, None, "tensor"),
            P(None, "tensor"),
            P("tensor", None),
            P(None, "tensor"),
            P("tensor"),
            P("tensor", None),
        ),
        check_vma=False,
    )
```

```python
import functools
import math

import jax
import jax.numpy as jnp
from jax import lax
from jax.experimental import pallas as pl
from jax.experimental.pallas import tpu as pltpu
from jax.sharding import PartitionSpec as P

HE = 12
HD = 16
PATCHES = 196
VIS = 49
PAD_E = 64
PAD_D = 208
LANES = 128
EPSILON = 1e-06
LOW = jnp.bfloat16
FULL = jnp.float32
MIB = 2**20


def low(values):
    return values.astype(LOW)


def full(values):
    return values.astype(FULL)


def matmul(left, right):
    return jnp.dot(left, right, preferred_element_type=FULL)


def left_product(left, right):
    return lax.dot_general(left, right, (((0,), (0,)), ((), ())), preferred_element_type=FULL)


def right_product(left, right):
    return lax.dot_general(left, right, (((1,), (1,)), ((), ())), preferred_element_type=FULL)


def pair(first, second):
    return full(first) + full(second)


def swap(value, axis):
    return lax.ppermute(value, axis, [(i, i ^ 1) for i in range(lax.axis_size(axis))])


def normalize(values):
    center = values - jnp.mean(values, axis=-1, keepdims=True)
    scale = lax.rsqrt(jnp.mean(center * center, axis=-1, keepdims=True) + EPSILON)
    return center * scale, scale


def norm_back(grad, gain, xhat, scale):
    inner = grad * gain
    return scale * (
        inner
        - jnp.mean(inner, axis=-1, keepdims=True)
        - xhat * jnp.mean(inner * xhat, axis=-1, keepdims=True)
    )


def column_sum(values):
    return jnp.sum(full(values), axis=0, keepdims=True)


def one_hot_rows(padded, length, images, packed_first=False):
    shape = (images * length, images * padded) if packed_first else (images * padded, images * length)
    first = lax.broadcasted_iota(jnp.int32, shape, 0)
    second = lax.broadcasted_iota(jnp.int32, shape, 1)
    packed, wide = (first, second) if packed_first else (second, first)
    hit = None
    for image in range(images):
        here = (
            (packed >= image * length)
            & (packed < (image + 1) * length)
            & (wide - image * padded == packed - image * length)
        )
        hit = here if hit is None else hit | here
    return low(jnp.where(hit, 1.0, 0.0))


def packed_rows(values, images):
    return low(matmul(one_hot_rows(PAD_E, VIS, images, True), low(values)))


def padded_sum(part_ref, other_ref, images):
    spread = one_hot_rows(PAD_E, VIS, images)
    return matmul(spread, part_ref[...]) + matmul(spread, other_ref[...])


def head_masks(head_size):
    lane = lax.broadcasted_iota(jnp.int32, (1, LANES), 1)
    return [
        jnp.where((lane >= j * head_size) & (lane < (j + 1) * head_size), 1.0, 0.0)
        for j in range(LANES // head_size)
    ]


def spread_heads(values, masks):
    wide = full(values)
    return jnp.concatenate([low(wide * mask) for mask in masks], axis=0)


def gather_heads(stacked, masks):
    rows = stacked.shape[0] // len(masks)
    total = None
    for j, mask in enumerate(masks):
        term = stacked[j * rows : (j + 1) * rows] * mask
        total = term if total is None else total + term
    return total


def attend(queries, key_rows, value_rows, masks, allowed, factor):
    scores = right_product(spread_heads(queries, masks), key_rows) * factor
    scores = jnp.where(allowed, scores, -1e30)
    exponent = jnp.exp(scores - jnp.max(scores, axis=-1, keepdims=True))
    weights_low = low(exponent * (1.0 / jnp.sum(exponent, axis=-1, keepdims=True)))
    return weights_low, low(gather_heads(matmul(weights_low, value_rows), masks))


def attend_back(queries, key_rows, value_rows, weights_low, upstream, masks, factor):
    spread_up = spread_heads(upstream, masks)
    weight_grad = right_product(spread_up, value_rows)
    weights = full(weights_low)
    product = weights * weight_grad
    score_grad = low(product - weights * jnp.sum(product, axis=-1, keepdims=True))
    query_grad = gather_heads(matmul(score_grad, key_rows), masks) * factor
    key_grad = left_product(score_grad, spread_heads(queries, masks)) * factor
    value_grad = left_product(weights_low, spread_up)
    return low(query_grad), low(key_grad), low(value_grad)


def same_image(heads, images, padded, length):
    shape = (heads * images * padded, images * padded)
    row = lax.broadcasted_iota(jnp.int32, shape, 0)
    key = lax.broadcasted_iota(jnp.int32, shape, 1)
    hit = None
    for head in range(heads):
        for image in range(images):
            start = (head * images + image) * padded
            here = (
                (row >= start)
                & (row < start + padded)
                & (key >= image * padded)
                & (key < image * padded + length)
            )
            hit = here if hit is None else hit | here
    return hit


def live_rows(count, rows, padded):
    row = lax.broadcasted_iota(jnp.int32, (rows, 1), 0)
    return jnp.where(row < count * padded, 1.0, 0.0)


def kernel_call(order, kernel, outs, *arguments, scalars=0, scratch=(), after=(), memory=24, name=None):
    count = len(arguments)
    before = order[-1:] + list(after)

    def run(*refs):
        mark = count + len(before) + len(outs)
        refs[mark][...] = jnp.zeros((8, LANES), FULL)
        kernel(*refs[:count], *refs[count + len(before) : mark], *refs[mark + 1 :])

    specs = [pl.BlockSpec(memory_space=pltpu.SMEM)] * scalars
    specs += [pl.BlockSpec(memory_space=pltpu.VMEM)] * (count - scalars)
    specs += [pl.BlockSpec(memory_space=pl.ANY)] * len(before)
    results = pl.pallas_call(
        run,
        out_shape=[jax.ShapeDtypeStruct(x.shape, x.dtype) for x in outs] + [shaped((8, LANES), FULL)],
        in_specs=specs,
        out_specs=[pl.BlockSpec(memory_space=pltpu.VMEM)] * (len(outs) + 1),
        scratch_shapes=scratch,
        compiler_params=pltpu.CompilerParams(vmem_limit_bytes=memory * MIB),
        cost_estimate=pl.CostEstimate(flops=36000000000, bytes_accessed=1, transcendentals=0),
        name=name,
    )(*arguments, *before)
    order.append(results[-1])
    return results[:-1]


def chunk(index, size):
    return pl.ds(pl.multiple_of(index * size, LANES), size)


def shaped(shape, dtype=LOW):
    return jax.ShapeDtypeStruct(shape, dtype)


def project_heads(normed, qkv_ref, bias, proj_ref, width):
    queries = low(matmul(normed, qkv_ref[0]) + bias[0:1])
    key_rows = low(matmul(normed, qkv_ref[1]))
    value_rows = low(matmul(normed, qkv_ref[2]) + bias[1:2])
    proj_ref[0] = queries
    proj_ref[1] = key_rows
    proj_ref[2] = value_rows


def enc_attend_kernel(
    images, head_size, place_ref, x_ref, vec_ref, qkv_ref, bias_ref, out_w_ref,
    part_ref, x_out_ref, normed_ref, proj_ref, weights_ref, mix_ref,
):
    width = qkv_ref.shape[2]
    if len(x_ref.shape) == 2:
        rows = x_ref[...]
    else:
        rows = low(jnp.where(place_ref[0] == 0, full(x_ref[:, 0, :]), full(x_ref[:, 1, :])))
    x = matmul(one_hot_rows(PAD_E, VIS, images), rows)
    x_out_ref[...] = low(x)
    vec = full(vec_ref[...])
    xhat, _ = normalize(x)
    normed = low(xhat * vec[0:1] + vec[1:2])
    normed_ref[...] = normed
    project_heads(normed, qkv_ref, full(bias_ref[...]), proj_ref, width)
    masks = head_masks(head_size)
    allowed = same_image(len(masks), images, PAD_E, VIS)
    for group in range(width // LANES):
        lanes = slice(group * LANES, (group + 1) * LANES)
        weights_low, mixture = attend(
            proj_ref[0, :, lanes],
            proj_ref[1, :, lanes],
            proj_ref[2, :, lanes],
            masks,
            allowed,
            1.0 / math.sqrt(head_size),
        )
        weights_ref[group] = weights_low
        mix_ref[:, lanes] = mixture
    part_ref[...] = packed_rows(matmul(mix_ref[...], out_w_ref[...]), images)


def mlp_forward(middle, gain, shift, fc1_ref, bias_ref, fc2_ref, normed_ref, hidden_ref, slope_ref):
    xhat, _ = normalize(middle)
    normed = low(xhat * gain + shift)
    normed_ref[...] = normed
    pre = matmul(normed, fc1_ref[...]) + full(bias_ref[...])
    share = 0.5 + 0.5 * lax.erf(pre * math.sqrt(0.5))
    hidden = low(pre * share)
    hidden_ref[...] = hidden
    slope = share + pre * jnp.exp(-0.5 * pre * pre) * (1.0 / math.sqrt(2.0 * math.pi))
    if slope_ref is not None:
        slope_ref[...] = low(slope)
    return None if fc2_ref is None else low(matmul(hidden, fc2_ref[...])), slope


def enc_forward_send(place_ref, first_normed_ref, mix_ref, normed_ref, hidden_ref, send_ref):
    core, side = 1 - place_ref[0], place_ref[1]
    width, wide = normed_ref.shape[1], hidden_ref.shape[1] // 4
    half = width // 2
    send_ref[:, :wide] = hidden_ref[:, chunk(2 * core + side, wide)]
    send_ref[:, wide : wide + width] = normed_ref[...]
    send_ref[:, wide + width : wide + width + half] = first_normed_ref[:, chunk(core, half)]
    send_ref[:, wide + width + half :] = mix_ref[...]


def enc_hidden_kernel(
    place_ref, x_ref, vec_ref, part_ref, other_ref, fc1_ref, bias_ref, first_normed_ref, mix_ref, fc2_ref,
    part_two_ref, middle_ref, normed_ref, hidden_ref, slope_ref, send_ref,
):
    vec = full(vec_ref[...])
    middle = full(x_ref[...]) + padded_sum(part_ref, other_ref, x_ref.shape[0] // PAD_E) + vec[2:3]
    middle_ref[...] = middle
    part, _ = mlp_forward(
        middle, vec[3:4], vec[4:5], fc1_ref, bias_ref, fc2_ref, normed_ref, hidden_ref, slope_ref
    )
    part_two_ref[...] = packed_rows(part, x_ref.shape[0] // PAD_E)
    enc_forward_send(place_ref, first_normed_ref, mix_ref, normed_ref, hidden_ref, send_ref)


def enc_side_hidden_kernel(
    place_ref, x_ref, vec_ref, part_ref, other_ref, fc1_ref, bias_ref, first_normed_ref, mix_ref,
    middle_ref, normed_ref, hidden_ref, slope_ref, send_ref,
):
    vec = full(vec_ref[...])
    middle = full(x_ref[...]) + padded_sum(part_ref, other_ref, x_ref.shape[0] // PAD_E) + vec[2:3]
    middle_ref[...] = middle
    mlp_forward(middle, vec[3:4], vec[4:5], fc1_ref, bias_ref, None, normed_ref, hidden_ref, slope_ref)
    enc_forward_send(place_ref, first_normed_ref, mix_ref, normed_ref, hidden_ref, send_ref)


def both_cores_kernel(place_ref, own_ref, over_ref, both_ref):
    first = place_ref[0] == 0
    own, over = full(own_ref[...]), full(over_ref[...])
    both_ref[:, 0, :] = low(jnp.where(first, own, over))
    both_ref[:, 1, :] = low(jnp.where(first, over, own))


def selector(keep_ref, image):
    patch = lax.broadcasted_iota(jnp.int32, (PAD_D, PAD_E), 0)
    return jnp.where(patch == keep_ref[image : image + 1, :], 1.0, 0.0)


def dec_attend_kernel(
    images, head_size, count_ref, keep_ref, middle_ref, part_ref, other_ref, enc_vec_ref, bridge_ref,
    vec_ref, pos_ref, qkv_ref, bias_ref, out_w_ref,
    part_out_ref, enc_out_ref, enc_pad_ref, starting_ref, normed_ref, proj_ref, weights_ref, mix_ref,
):
    width = qkv_ref.shape[2]
    vec = full(vec_ref[...])
    encoded = middle_ref[...] + padded_sum(part_ref, other_ref, images) + full(enc_vec_ref[...])[5:6]
    enc_pad = low(encoded * live_rows(count_ref[0], images * PAD_E, PAD_E))
    enc_pad_ref[...] = enc_pad
    enc_out_ref[...] = low(matmul(one_hot_rows(PAD_E, VIS, images, True), enc_pad))
    lifted = matmul(enc_pad, bridge_ref[...]) + vec[0:1]
    lifted_high = low(lifted)
    lifted_rest = low(lifted - full(lifted_high))
    pos = matmul(one_hot_rows(PAD_D, PATCHES, 1), pos_ref[...])
    for image in range(images):
        chosen = selector(keep_ref, image)
        rows = slice(image * PAD_E, (image + 1) * PAD_E)
        placed = matmul(low(chosen), lifted_high[rows]) + matmul(low(chosen), lifted_rest[rows])
        hidden_patch = 1.0 - jnp.sum(chosen, axis=1, keepdims=True)
        starting_ref[image * PAD_D : (image + 1) * PAD_D, :] = placed + hidden_patch * vec[1:2] + pos
    xhat, _ = normalize(starting_ref[...])
    normed = low(xhat * vec[2:3] + vec[3:4])
    normed_ref[...] = normed
    project_heads(normed, qkv_ref, full(bias_ref[...]), proj_ref, width)
    masks = head_masks(head_size)
    allowed = lax.broadcasted_iota(jnp.int32, (1, PAD_D), 1) < PATCHES
    groups = width // LANES
    for image in range(images):
        rows = slice(image * PAD_D, (image + 1) * PAD_D)
        for group in range(groups):
            lanes = slice(group * LANES, (group + 1) * LANES)
            weights_low, mixture = attend(
                proj_ref[0, rows, lanes],
                proj_ref[1, rows, lanes],
                proj_ref[2, rows, lanes],
                masks,
                allowed,
                1.0 / math.sqrt(head_size),
            )
            weights_ref[image * groups + group] = weights_low
            mix_ref[rows, lanes] = mixture
    part_out_ref[...] = low(matmul(mix_ref[...], out_w_ref[...]))


def dec_hidden_kernel(
    images, count_ref, place_ref, starting_ref, part_ref, other_ref, vec_ref, fc1_ref, bias_ref, fc2_ref, cot_ref,
    part_back_ref, part_two_ref, middle_ref, normed_ref, hidden_ref, out_low_ref, up_ref,
    up_sum_ref, out_sum_ref, send_ref,
):
    vec = full(vec_ref[...])
    middle = starting_ref[...] + pair(part_ref[...], other_ref[...]) + vec[4:5]
    middle_ref[...] = middle
    part, slope = mlp_forward(
        middle, vec[5:6], vec[6:7], fc1_ref, bias_ref, fc2_ref, normed_ref, hidden_ref, None
    )
    part_two_ref[...] = part
    spread = matmul(one_hot_rows(PAD_D, PATCHES, images), cot_ref[...])
    out_low = low(spread * live_rows(count_ref[0], images * PAD_D, PAD_D))
    out_low_ref[...] = out_low
    up_grad = low(slope * right_product(out_low, fc2_ref[...]))
    up_ref[...] = up_grad
    part_back_ref[...] = low(right_product(up_grad, fc1_ref[...]))
    up_sum_ref[...] = column_sum(up_grad)
    out_sum_ref[...] = column_sum(out_low)
    core = 1 - place_ref[0]
    width, wide = out_low.shape[1], up_grad.shape[1]
    half = width // 2
    send_ref[:, : wide // 2] = hidden_ref[:, chunk(core, wide // 2)]
    send_ref[:, wide // 2 : wide // 2 + half] = normed_ref[:, chunk(core, half)]
    send_ref[:, wide // 2 + half : wide // 2 + half + wide] = up_grad
    send_ref[:, wide // 2 + half + wide :] = out_low


def dec_out_kernel(images, count_ref, middle_ref, part_ref, other_ref, vec_ref, out_ref):
    decoded = middle_ref[...] + pair(part_ref[...], other_ref[...]) + full(vec_ref[...])[7:8]
    decoded = low(decoded * live_rows(count_ref[0], images * PAD_D, PAD_D))
    out_ref[...] = low(matmul(one_hot_rows(PAD_D, PATCHES, images, True), decoded))


def attention_back(
    first_row, images, padded, together, head_size, mixture_grad, proj_ref, weights_ref, stacked_ref
):
    masks = head_masks(head_size)
    groups = proj_ref.shape[2] // LANES
    step = images if together else 1
    for first in range(0, images, step):
        rows = slice(first * padded, (first + step) * padded)
        out_rows = slice(first_row + first * padded, first_row + (first + step) * padded)
        for group in range(groups):
            lanes = slice(group * LANES, (group + 1) * LANES)
            grads = attend_back(
                proj_ref[0, rows, lanes],
                proj_ref[1, rows, lanes],
                proj_ref[2, rows, lanes],
                weights_ref[first // step * groups + group],
                mixture_grad[out_rows, lanes],
                masks,
                1.0 / math.sqrt(head_size),
            )
            for j in range(3):
                stacked_ref[j, out_rows, lanes] = grads[j]


def normed_back(stacked_ref, qkv_ref):
    total = right_product(stacked_ref[0], qkv_ref[0])
    for j in (1, 2):
        total = total + right_product(stacked_ref[j], qkv_ref[j])
    return low(total)


def dec_attend_back_kernel(
    images, head_size, place_ref, middle_ref, out_low_ref, part_in_ref, other_ref, vec_ref, proj_ref, weights_ref,
    qkv_ref, out_w_ref, normed_ref, mix_ref,
    part_ref, middle_grad_ref, middle_low_ref, stacked_ref, sums_ref, bias_sum_ref, send_ref,
):
    vec = full(vec_ref[...])
    two_grad = pair(part_in_ref[...], other_ref[...])
    xhat, scale = normalize(middle_ref[...])
    middle_grad = full(out_low_ref[...]) + norm_back(two_grad, vec[5:6], xhat, scale)
    middle_grad_ref[...] = middle_grad
    middle_low = low(middle_grad)
    middle_low_ref[...] = middle_low
    mixture_grad = low(right_product(middle_low, out_w_ref[...]))
    attention_back(0, images, PAD_D, False, head_size, mixture_grad, proj_ref, weights_ref, stacked_ref)
    part_ref[...] = normed_back(stacked_ref, qkv_ref)
    core = 1 - place_ref[0]
    width = mix_ref.shape[1]
    half = middle_low.shape[1] // 2
    for j in range(3):
        send_ref[:, j * width : (j + 1) * width] = stacked_ref[j]
    send_ref[:, 3 * width : 4 * width] = mix_ref[...]
    send_ref[:, 4 * width : 4 * width + half] = normed_ref[:, chunk(core, half)]
    send_ref[:, 4 * width + half :] = middle_low_ref[:, chunk(core, half)]
    sums_ref[0:1] = column_sum(middle_grad)
    sums_ref[1:2] = column_sum(two_grad * xhat)
    sums_ref[2:3] = column_sum(two_grad)
    bias_sum_ref[0:1] = column_sum(stacked_ref[0])
    bias_sum_ref[1:2] = column_sum(stacked_ref[2])


def dec_start_back_kernel(
    images, count_ref, keep_ref, starting_ref, part_ref, other_ref, vec_ref, middle_grad_ref, bridge_ref,
    enc_cot_ref, lifted_ref, pos_ref, sums_ref,
):
    vec = full(vec_ref[...])
    one_grad = pair(part_ref[...], other_ref[...])
    xhat, scale = normalize(starting_ref[...])
    starting_grad = middle_grad_ref[...] + norm_back(one_grad, vec[2:3], xhat, scale)
    sums_ref[2:3] = column_sum(one_grad * xhat)
    sums_ref[3:4] = column_sum(one_grad)
    token = None
    total = None
    for image in range(images):
        grad = starting_grad[image * PAD_D : (image + 1) * PAD_D]
        chosen = selector(keep_ref, image)
        hidden_patch = 1.0 - jnp.sum(chosen, axis=1, keepdims=True)
        term = column_sum(hidden_patch * grad)
        token = term if token is None else token + term
        total = grad if total is None else total + grad
        lifted_ref[image * PAD_E : (image + 1) * PAD_E, :] = low(left_product(low(chosen), low(grad)))
    pos_ref[...] = total
    lifted_grad = lifted_ref[...]
    sums_ref[0:1] = column_sum(lifted_grad)
    sums_ref[1:2] = token
    handed = right_product(lifted_grad, bridge_ref[...])
    enc_cot_ref[...] = low(handed * live_rows(count_ref[0], images * PAD_E, PAD_E))


def enc_hidden_back_kernel(
    place_ref, cot_a, cot_b, slope_a, slope_b, fc1_ref, fc2_ref, part_ref, up_ref, send_ref
):
    slope = jnp.concatenate([slope_a[...], slope_b[...]], axis=0)
    up_grad = low(full(slope) * right_product(stacked_rows(cot_a, cot_b), fc2_ref[...]))
    up_ref[...] = up_grad
    part_ref[...] = packed_rows(right_product(up_grad, fc1_ref[...]), up_grad.shape[0] // PAD_E)
    send_ref[...] = up_ref[:, chunk(2 * (1 - place_ref[0]) + place_ref[1], send_ref.shape[1])]


def enc_attend_back_kernel(
    images, head_size, place_ref, middle_a, middle_b, cot_a, cot_b, part_in_ref, other_ref, vec_ref, proj_a, proj_b,
    weights_a, weights_b, qkv_ref, out_w_ref, up_ref,
    part_ref, middle_grad_ref, middle_low_ref, stacked_ref, sums_ref, bias_sum_ref, up_sum_ref, send_ref,
):
    vec = full(vec_ref[...])
    own = middle_a.shape[0]
    cot = full(stacked_rows(cot_a, cot_b))
    two_grad = padded_sum(part_in_ref, other_ref, 2 * images)
    xhat, scale = normalize(stacked_rows(middle_a, middle_b))
    middle_grad = cot + norm_back(two_grad, vec[3:4], xhat, scale)
    middle_grad_ref[...] = middle_grad
    middle_low = low(middle_grad)
    middle_low_ref[...] = middle_low
    mixture_grad = low(right_product(middle_low, out_w_ref[...]))
    attention_back(0, images, PAD_E, True, head_size, mixture_grad, proj_a, weights_a, stacked_ref)
    attention_back(own, images, PAD_E, True, head_size, mixture_grad, proj_b, weights_b, stacked_ref)
    part_ref[...] = packed_rows(normed_back(stacked_ref, qkv_ref), 2 * images)
    width = qkv_ref.shape[2]

    @pl.when(place_ref[1] == 0)
    def _():
        send_ref[:, :width] = stacked_ref[0]
        send_ref[:, width:] = stacked_ref[1]

    @pl.when(place_ref[1] == 1)
    def _():
        send_ref[:, :width] = stacked_ref[2]
        send_ref[:, width:] = middle_low_ref[:, chunk(1 - place_ref[0], width)]

    sums_ref[0:1] = column_sum(middle_grad)
    sums_ref[1:2] = column_sum(two_grad * xhat)
    sums_ref[2:3] = column_sum(two_grad)
    sums_ref[3:4] = column_sum(cot)
    bias_sum_ref[0:1] = column_sum(stacked_ref[0])
    bias_sum_ref[1:2] = column_sum(stacked_ref[2])
    up_sum_ref[...] = column_sum(up_ref[...])


def enc_start_back_kernel(
    images, x_a, x_b, part_ref, other_ref, vec_ref, middle_grad_ref, sums_ref, up_sum_ref, bias_sum_ref,
    grad_in_ref, small_ref, rows_ref,
):
    vec = full(vec_ref[...])
    own = x_a.shape[0]
    one_grad = padded_sum(part_ref, other_ref, 2 * images)
    xhat, scale = normalize(full(stacked_rows(x_a, x_b)))
    grad = middle_grad_ref[:own] + norm_back(one_grad[:own], vec[0:1], xhat[:own], scale[:own])
    take = full(one_hot_rows(PAD_E, VIS, images, True))
    grad_in_ref[:, 0, :] = jnp.dot(
        take, grad, preferred_element_type=FULL, precision=lax.Precision.HIGHEST
    )
    rows_ref[...] = jnp.zeros_like(rows_ref)
    rows_ref[0:1] = column_sum(one_grad * xhat)
    rows_ref[1:2] = column_sum(one_grad)
    rows_ref[2:6] = sums_ref[...]
    put_rows(rows_ref, 6, up_sum_ref, bias_sum_ref)
    small_ref[...] = low(rows_ref[...])


def tall(*parts):
    return jnp.concatenate(parts, axis=0)


def by_side(place_ref, mine_ref, theirs_ref, blocks):
    first = place_ref[1] == 0
    rows = mine_ref.shape[1]
    for part in range(2):
        zero, one = (low(block[part * rows : (part + 1) * rows]) for block in blocks)
        mine_ref[part] = jnp.where(first, zero, one)
        theirs_ref[part] = jnp.where(first, one, zero)


def dec_hidden_weights_kernel(
    place_ref, hidden_ref, out_low_ref, normed_ref, up_ref, over_ref, mine_ref, theirs_ref
):
    core = place_ref[0]
    width, wide = out_low_ref.shape[1], up_ref.shape[1]
    half = width // 2
    over_up = over_ref[:, wide // 2 + half : wide // 2 + half + wide]
    over_out = over_ref[:, wide // 2 + half + wide :]
    down = left_product(
        tall(hidden_ref[:, chunk(core, wide // 2)], over_ref[:, : wide // 2]), tall(out_low_ref[...], over_out)
    )
    up = left_product(
        tall(normed_ref[:, chunk(core, half)], over_ref[:, wide // 2 : wide // 2 + half]),
        tall(up_ref[...], over_up),
    )
    by_side(place_ref, mine_ref, theirs_ref, (down, tall(up[:, :width], up[:, width:])))


def dec_head_weights_kernel(
    place_ref, normed_ref, stacked_ref, mix_ref, middle_low_ref, over_ref, mine_ref, theirs_ref
):
    core = place_ref[0]
    width = mix_ref.shape[1]
    half = normed_ref.shape[1] // 2
    left = tall(normed_ref[:, chunk(core, half)], over_ref[:, 4 * width : 4 * width + half])
    grads = [
        left_product(left, tall(stacked_ref[j], over_ref[:, j * width : (j + 1) * width])) for j in range(3)
    ]
    out = left_product(
        tall(mix_ref[...], over_ref[:, 3 * width : 4 * width]),
        tall(middle_low_ref[:, chunk(core, half)], over_ref[:, 4 * width + half :]),
    )
    by_side(
        place_ref, mine_ref, theirs_ref,
        (jnp.concatenate(grads[:2], axis=1), jnp.concatenate([grads[2], out], axis=1)),
    )


def put_rows(rows_ref, row, up_sum_ref, bias_sum_ref):
    cols = rows_ref.shape[1]
    for piece in range(up_sum_ref.shape[1] // cols):
        rows_ref[row : row + 1] = up_sum_ref[:, piece * cols : (piece + 1) * cols]
        row += 1
    width = bias_sum_ref.shape[1]
    for piece in range(2):
        here, lane = row + piece * width // cols, piece * width % cols
        rows_ref[here : here + 1, lane : lane + width] = bias_sum_ref[piece : piece + 1]


def take_rows(rows_ref, row, up_sum_ref, bias_sum_ref):
    cols = rows_ref.shape[1]
    for piece in range(up_sum_ref.shape[1] // cols):
        up_sum_ref[:, piece * cols : (piece + 1) * cols] = rows_ref[row : row + 1]
        row += 1
    width = bias_sum_ref.shape[1]
    for piece in range(2):
        here, lane = row + piece * width // cols, piece * width % cols
        bias_sum_ref[piece : piece + 1] = rows_ref[here : here + 1, lane : lane + width]


def dec_bridge_weights_kernel(
    place_ref, enc_pad_ref, lifted_ref, pos_ref, sums_ref, middle_sums_ref, out_sum_ref, up_sum_ref,
    bias_sum_ref, keep_ref, send_ref, small_ref,
):
    core = place_ref[0]
    cols = lifted_ref.shape[1]
    bridge = low(left_product(enc_pad_ref[...], lifted_ref[...]))
    quarter = bridge.shape[0] // 4
    small_ref[...] = jnp.zeros_like(small_ref)
    small_ref[0:PAD_D] = pos_ref[...]
    row = PAD_D
    for ref, count in ((sums_ref, 4), (middle_sums_ref, 3), (out_sum_ref, 1)):
        small_ref[row : row + count] = ref[...]
        row += count
    put_rows(small_ref, row, up_sum_ref, bias_sum_ref)
    few = small_ref.shape[0] // 4
    first = core == 0

    def block(index):
        return jnp.concatenate(
            [bridge[index * quarter : (index + 1) * quarter], low(small_ref[index * few : (index + 1) * few])],
            axis=0,
        )

    for side in range(2):
        zero, one = block(side), block(2 + side)
        half = zero.shape[0] // 2
        for part in range(2):
            rows = slice(part * half, (part + 1) * half)
            keep_ref[side, part] = jnp.where(first, zero[rows], one[rows])
            send_ref[side, part] = jnp.where(first, one[rows], zero[rows])


def stacked_rows(first, second, lanes=slice(None)):
    return jnp.concatenate([first[:, lanes], second[:, lanes]], axis=0)


def enc_hidden_weights_kernel(
    place_ref, hidden_a, hidden_b, cot_a, cot_b, normed_a, normed_b, up_ref,
    forward_a, forward_b, over_cot_a, over_cot_b, over_up, mine_ref, theirs_ref,
):
    core, side, half = place_ref[0], place_ref[1], place_ref[2]
    rows = mine_ref.shape[0] // 2
    width = 2 * rows
    features = cot_a.shape[1]
    lanes = chunk(2 * core + side, width)
    down = low(
        left_product(
            tall(hidden_a[:, lanes], hidden_b[:, lanes], forward_a[:, :width], forward_b[:, :width]),
            tall(cot_a[...], cot_b[...], over_cot_a[...], over_cot_b[...]),
        )
    )
    here = slice(width, width + features)
    up = low(
        left_product(
            tall(normed_a[...], normed_b[...], forward_a[:, here], forward_b[:, here]),
            tall(up_ref[:, lanes], over_up[...]),
        )
    )
    for part in range(2):
        block = (
            down[part * rows : (part + 1) * rows],
            up[2 * part * rows : (2 * part + 1) * rows],
            up[(2 * part + 1) * rows : (2 * part + 2) * rows],
        )
        for ref, index in ((mine_ref, half), (theirs_ref, 1 - half)):

            @pl.when(index == part)
            def _(ref=ref, block=block):
                ref[:rows] = block[0]
                ref[rows:, :width] = block[1]
                ref[rows:, width:] = block[2]


def last_weights_kernel(
    place_ref, normed_a, normed_b, stacked_ref, mix_a, mix_b, middle_low_ref, forward_a, forward_b, over_ref,
    small_ref, rest_mine, rest_other, mine_ref, theirs_ref,
):
    core, half = place_ref[0], place_ref[2]
    width = mix_a.shape[1]
    half_width = normed_a.shape[1] // 2
    lanes = chunk(core, half_width)
    start = forward_a.shape[1] - half_width - width
    left = tall(
        normed_a[:, lanes], normed_b[:, lanes],
        forward_a[:, start : start + half_width], forward_b[:, start : start + half_width],
    )
    few = small_ref.shape[0] // 2
    columns = mine_ref.shape[1]

    def put(first, second):
        rows = first.shape[0] // 2
        for part in range(2):
            here = slice(part * rows, (part + 1) * rows)
            block = jnp.concatenate([first[here], second[here]], axis=1)
            block = tall(low(block), small_ref[part * few : (part + 1) * few])
            for ref, index in ((mine_ref, half), (theirs_ref, 1 - half)):

                @pl.when(index == part)
                def _(ref=ref, block=block):
                    for i in range(block.shape[1] // columns):
                        ref[i * block.shape[0] : (i + 1) * block.shape[0]] = block[
                            :, i * columns : (i + 1) * columns
                        ]

    @pl.when(place_ref[1] == 0)
    def _():
        put(
            left_product(left, tall(stacked_ref[0], over_ref[:, :width])),
            left_product(left, tall(stacked_ref[1], over_ref[:, width:])),
        )

    @pl.when(place_ref[1] == 1)
    def _():
        put(
            left_product(left, tall(stacked_ref[2], over_ref[:, :width])),
            left_product(
                tall(mix_a[...], mix_b[...], forward_a[:, start + half_width :], forward_b[:, start + half_width :]),
                tall(middle_low_ref[:, lanes], over_ref[:, width:]),
            ),
        )

    for ref, index in ((mine_ref, half), (theirs_ref, 1 - half)):
        total = low(pair(rest_mine[index], rest_other[index]))
        count = total.shape[0]
        row = ref.shape[0] - count * (total.shape[1] // columns)
        for i in range(total.shape[1] // columns):
            ref[row + i * count : row + (i + 1) * count] = total[:, i * columns : (i + 1) * columns]


def fold_kernel(axis, place_ref, *refs):
    index = place_ref[axis]
    mine_ref, theirs_ref = refs[-2:]
    rows = 0
    for keep_ref, other_ref in zip(refs[:-2:2], refs[1:-2:2]):
        here = (slice(None),) * (len(keep_ref.shape) - 3) + (slice(rows, rows + keep_ref.shape[-2]),)
        rows += keep_ref.shape[-2]
        mine_ref[here] = low(pair(keep_ref[index], other_ref[index]))
        theirs_ref[here] = low(pair(keep_ref[1 - index], other_ref[1 - index]))


def fold_more_kernel(place_ref, keep_ref, other_ref, before_mine, before_theirs, mine_ref, theirs_ref):
    index = place_ref[2]
    rows = before_mine.shape[0]
    mine_ref[:rows] = before_mine[...]
    theirs_ref[:rows] = before_theirs[...]
    mine_ref[rows:] = low(pair(keep_ref[index], other_ref[index]))
    theirs_ref[rows:] = low(pair(keep_ref[1 - index], other_ref[1 - index]))


def add_kernel(first_ref, second_ref, sum_ref):
    sum_ref[...] = low(pair(first_ref[...], second_ref[...]))


def fold(order, place, axis, *arrays, after=()):
    shape = arrays[0].shape[1:-2] + (sum(x.shape[-2] for x in arrays[::2]), arrays[0].shape[-1])
    return kernel_call(
        order, functools.partial(fold_kernel, axis), [shaped(shape)] * 2, place, *arrays,
        scalars=1, after=after, name="fold",
    )


def add(order, first, second, after=()):
    return kernel_call(order, add_kernel, [shaped(first.shape)], first, second, after=after, name="add")[0]


def mark_kernel(out_ref):
    out_ref[...] = jnp.zeros_like(out_ref)


def mark(order, *values):
    kernel_call(order, mark_kernel, [shaped((8, LANES), FULL)], after=values, name="mark")


def flip(value, step):
    return lax.ppermute(value, "dp", [(i, i ^ step) for i in range(lax.axis_size("dp"))])


def cross_start(value):
    return flip(value, 4) if lax.axis_size("dp") > 4 else jnp.zeros_like(value)


def cross_end(order, value, arrived, after=()):
    value = add(order, value, arrived, after)
    step = 8
    while step < lax.axis_size("dp"):
        value = add(order, value, flip(value, step))
        step *= 2
    return value


def pack_kernel(place_ref, mine_ref, other_ref, across_ref, there_ref, packed_ref):
    side, half = place_ref[1], place_ref[2]
    packed_ref[side, half] = mine_ref[...]
    packed_ref[side, 1 - half] = other_ref[...]
    packed_ref[1 - side, half] = across_ref[...]
    packed_ref[1 - side, 1 - half] = there_ref[...]


def pieces_of(place_ref, own_ref, over_ref):
    core = place_ref[0]
    return [
        (ref.at[side, half], index, side, half)
        for ref, index in ((own_ref, core), (over_ref, 1 - core))
        for side in range(2)
        for half in range(2)
    ]


def aligned(index, size):
    return pl.ds(pl.multiple_of(index * size, size), size)


def put_heads(block, core, side, half, qkv_ref, out_w_ref):
    rows, width = block.shape[0], qkv_ref.shape[2]
    here = aligned(2 * core + half, rows)
    if side == 0:
        qkv_ref[0, here, :] = full(block[:, :width])
        qkv_ref[1, here, :] = full(block[:, width:])
    else:
        qkv_ref[2, here, :] = full(block[:, :width])
        out_w_ref[half * rows : (half + 1) * rows, aligned(core, width)] = full(block[:, width:])


def dec_whole_kernel(place_ref, own_ref, over_ref, fc1_ref, fc2_ref, qkv_ref, out_w_ref):
    rows, cols = fc1_ref.shape[0] // 2, fc1_ref.shape[1] // 2
    for ref, core, side, half in pieces_of(place_ref, own_ref, over_ref):
        if side == 0:
            fc2_ref[aligned(2 * core + half, rows), :] = full(ref[:rows])
        else:
            fc1_ref[aligned(core, rows), half * cols : (half + 1) * cols] = full(ref[:rows])
        put_heads(ref[rows:], core, side, half, qkv_ref, out_w_ref)


def last_whole_kernel(
    place_ref, own_ref, over_ref, qkv_ref, out_w_ref, vec_ref, up_sum_ref, bias_sum_ref,
    bridge_ref, pos_ref, dec_vec_ref, dec_up_sum_ref, dec_bias_sum_ref, rows_ref, small_ref,
):
    few = rows_ref.shape[0] // 2
    rows = qkv_ref.shape[1] // 4 + few
    width = own_ref.shape[3]
    wide, cols = 2 * qkv_ref.shape[2], bridge_ref.shape[1]
    rest = (own_ref.shape[2] - rows * (wide // width)) * width // cols
    quarter, part = bridge_ref.shape[0] // 4, small_ref.shape[0] // 4

    def take(ref, row, count, lanes):
        return jnp.concatenate(
            [ref[row + i * count : row + (i + 1) * count] for i in range(lanes // width)], axis=1
        )

    for ref, core, side, half in pieces_of(place_ref, own_ref, over_ref):
        heads = take(ref, 0, rows, wide)
        put_heads(heads[: rows - few], core, side, half, qkv_ref, out_w_ref)
        block = take(ref, rows * (wide // width), rest, cols)
        index = 2 * core + side
        start = pl.multiple_of(index * quarter, 8)
        if half == 0:
            bridge_ref[pl.ds(start, rest), :] = full(block)
        else:
            left = quarter - rest
            bridge_ref[pl.ds(start + rest, left), :] = full(block[:left])
            small_ref[aligned(index, part), :] = full(block[left:])
    for half in range(2):
        rows_ref[half * few : (half + 1) * few] = pair(
            take(own_ref.at[0, half], 0, rows, wide)[rows - few :],
            take(over_ref.at[0, half], 0, rows, wide)[rows - few :],
        )
    vec_ref[...] = rows_ref[0:6]
    take_rows(rows_ref, 6, up_sum_ref, bias_sum_ref)
    pos_ref[...] = small_ref[0:PATCHES]
    dec_vec_ref[...] = small_ref[PAD_D : PAD_D + 8]
    take_rows(small_ref, PAD_D + 8, dec_up_sum_ref, dec_bias_sum_ref)


def enc_hidden_whole_kernel(place_ref, own_ref, over_ref, fc1_ref, fc2_ref):
    for ref, core, side, half in pieces_of(place_ref, own_ref, over_ref):
        rows = ref.shape[0] // 2
        width = 2 * rows
        fc2_ref[aligned(4 * core + 2 * side + half, rows), :] = full(ref[:rows])
        lanes = aligned(2 * core + side, width)
        for part in range(2):
            fc1_ref[(2 * half + part) * rows : (2 * half + part + 1) * rows, lanes] = full(
                ref[rows:, part * width : (part + 1) * width]
            )


def spread(piece):
    other = flip(piece, 2)
    return piece, other, flip(piece, 1), flip(other, 1)


def pack(order, place, pieces, after=()):
    (packed,) = kernel_call(
        order, pack_kernel, [shaped((2, 2) + pieces[0].shape)], place, *pieces, scalars=1, after=after, name="pack"
    )
    return packed, swap(packed, "section")


def pick(stacked, index):
    return lax.dynamic_index_in_dim(stacked, index, 0, keepdims=False)


def body(
    enc_in, keep_index, image_count, enc_vec, enc_qkv, enc_qv_bias, enc_out_w, enc_fc1, enc_fc1_bias, enc_fc2,
    bridge_w, dec_vec, dec_pos, dec_qkv, dec_qv_bias, dec_out_w, dec_fc1, dec_fc1_bias, dec_fc2, dec_cot,
):
    core = lax.axis_index("section")
    group = lax.axis_index("dp")
    place = jnp.stack([core, group % 2, group // 2 % 2]).astype(jnp.int32)
    images = keep_index.shape[1]
    enc_width, dec_width = bridge_w.shape
    enc_local, dec_local = enc_qkv.shape[2], dec_qkv.shape[2]
    enc_size, dec_size = enc_width // HE, dec_width // HD
    enc_mlp, dec_mlp = enc_fc1.shape[1], dec_fc1.shape[1]
    rows_e, rows_d = images * PAD_E, images * PAD_D
    enc_groups, dec_groups = enc_local // LANES, dec_local // LANES
    enc_heads, dec_heads = LANES // enc_size, LANES // dec_size
    enc_qkv, dec_qkv = jnp.transpose(enc_qkv, (1, 0, 2)), jnp.transpose(dec_qkv, (1, 0, 2))
    enc_fc1_bias, dec_fc1_bias = enc_fc1_bias[None], dec_fc1_bias[None]
    raw_in = enc_in
    enc_in = jnp.transpose(enc_in, (1, 0, 2))
    keep = jnp.pad(pick(keep_index, core), ((0, 0), (0, PAD_E - VIS)), constant_values=-1)
    cot = pick(dec_cot, core)
    count = pick(image_count, core)
    dec_rows = images * PATCHES

    order = []
    call = functools.partial(kernel_call, order)

    def enc_attend(rows, memory=24):
        return call(
            functools.partial(enc_attend_kernel, images, enc_size),
            [
                shaped((images * VIS, enc_width)),
                shaped((rows_e, enc_width)),
                shaped((rows_e, enc_width)),
                shaped((3, rows_e, enc_local)),
                shaped((enc_groups, enc_heads * rows_e, rows_e)),
                shaped((rows_e, enc_local)),
            ],
            place, rows, enc_vec, enc_qkv, enc_qv_bias, enc_out_w,
            scalars=1, memory=memory, name="enc_attend",
        )

    part, x, normed, proj, weights, mix = enc_attend(enc_in, 60)
    part_other = swap(part, "tensor")
    raw_in, x = lax.optimization_barrier((raw_in, x))
    side_in = flip(pick(raw_in, core), 1)
    side_part, side_x, side_normed, side_proj, side_weights, side_mix = enc_attend(side_in)
    part_two, middle, normed_two, hidden, slope, forward_send = call(
        enc_hidden_kernel,
        [
            shaped((images * VIS, enc_width)),
            shaped((rows_e, enc_width), FULL),
            shaped((rows_e, enc_width)),
            shaped((rows_e, enc_mlp)),
            shaped((rows_e, enc_mlp)),
            shaped((rows_e, enc_mlp // 4 + enc_width + enc_width // 2 + enc_local)),
        ],
        place, x, enc_vec, part, part_other, enc_fc1, enc_fc1_bias, normed, mix, enc_fc2,
        scalars=1, name="enc_hidden",
    )
    part_two_other = swap(part_two, "tensor")
    side_part_other = swap(side_part, "tensor")

    (
        dec_part, enc_out, enc_pad, starting, dec_normed, dec_proj, dec_weights, dec_mix,
    ) = call(
        functools.partial(dec_attend_kernel, images, dec_size),
        [
            shaped((rows_d, dec_width)),
            shaped((images * VIS, enc_width)),
            shaped((rows_e, enc_width)),
            shaped((rows_d, dec_width), FULL),
            shaped((rows_d, dec_width)),
            shaped((3, rows_d, dec_local)),
            shaped((images * dec_groups, dec_heads * PAD_D, PAD_D)),
            shaped((rows_d, dec_local)),
        ],
        count, keep, middle, part_two, part_two_other, enc_vec, bridge_w,
        dec_vec, dec_pos, dec_qkv, dec_qv_bias, dec_out_w,
        scalars=1, name="dec_attend",
    )
    dec_part_other = swap(dec_part, "tensor")
    enc_out_over = swap(enc_out, "section")
    forward_over = swap(forward_send, "section")
    side_middle, side_normed_two, side_hidden, side_slope, side_forward_send = call(
        enc_side_hidden_kernel,
        [
            shaped((rows_e, enc_width), FULL),
            shaped((rows_e, enc_width)),
            shaped((rows_e, enc_mlp)),
            shaped((rows_e, enc_mlp)),
            shaped((rows_e, enc_mlp // 4 + enc_width + enc_width // 2 + enc_local)),
        ],
        place, side_x, enc_vec, side_part, side_part_other, enc_fc1, enc_fc1_bias, side_normed, side_mix,
        scalars=1, name="enc_side_hidden",
    )
    (
        dec_part_back, dec_part_two, dec_middle, dec_normed_two, dec_hid, out_low, dec_up, up_sum, out_sum, d1_send,
    ) = call(
        functools.partial(dec_hidden_kernel, images),
        [
            shaped((rows_d, dec_width)),
            shaped((rows_d, dec_width)),
            shaped((rows_d, dec_width), FULL),
            shaped((rows_d, dec_width)),
            shaped((rows_d, dec_mlp)),
            shaped((rows_d, dec_width)),
            shaped((rows_d, dec_mlp)),
            shaped((1, dec_mlp), FULL),
            shaped((1, dec_width), FULL),
            shaped((rows_d, dec_mlp // 2 + dec_width // 2 + dec_mlp + dec_width)),
        ],
        count, place, starting, dec_part, dec_part_other, dec_vec, dec_fc1, dec_fc1_bias, dec_fc2, cot,
        scalars=2, after=[forward_over], name="dec_hidden",
    )

    side_forward_over = swap(side_forward_send, "section")
    d1_over = swap(d1_send, "section")
    dec_part_back_other = swap(dec_part_back, "tensor")
    (enc_out_both,) = call(
        both_cores_kernel, [shaped((images * VIS, 2, enc_width))],
        place, enc_out, enc_out_over, scalars=1, name="enc_out_both",
    )
    d1_mine, d1_theirs = call(
        dec_hidden_weights_kernel,
        [shaped((2, dec_mlp // 4, dec_width))] * 2,
        place, dec_hid, out_low, dec_normed_two, dec_up, d1_over,
        scalars=1, after=[side_forward_over], name="dec_hidden_weights",
    )
    d1_arrived = flip(d1_theirs, 1)
    dec_part_one, dec_middle_grad, dec_middle_low, dec_stacked, middle_sums, dec_bias_sum, d2_send = call(
        functools.partial(dec_attend_back_kernel, images, dec_size),
        [
            shaped((rows_d, dec_width)),
            shaped((rows_d, dec_width), FULL),
            shaped((rows_d, dec_width)),
            shaped((3, rows_d, dec_local)),
            shaped((3, dec_width), FULL),
            shaped((2, dec_local), FULL),
            shaped((rows_d, 4 * dec_local + dec_width)),
        ],
        place, dec_middle, out_low, dec_part_back, dec_part_back_other, dec_vec, dec_proj, dec_weights, dec_qkv, dec_out_w,
        dec_normed, dec_mix,
        scalars=1, name="dec_attend_back",
    )
    d2_over = swap(d2_send, "section")
    dec_part_one_other = swap(dec_part_one, "tensor")
    d1_mine, d1_theirs = fold(order, place, 2, d1_mine, d1_arrived)
    d2_mine, d2_theirs = call(
        dec_head_weights_kernel,
        [shaped((2, dec_width // 4, 2 * dec_local))] * 2,
        place, dec_normed, dec_stacked, dec_mix, dec_middle_low, d2_over,
        scalars=1, name="dec_head_weights",
    )
    d2_arrived = flip(d2_theirs, 1)
    enc_cot, lifted_grad, pos_grad, start_sums = call(
        functools.partial(dec_start_back_kernel, images),
        [
            shaped((rows_e, enc_width)),
            shaped((rows_e, dec_width)),
            shaped((PAD_D, dec_width), FULL),
            shaped((4, dec_width), FULL),
        ],
        count, keep, starting, dec_part_one, dec_part_one_other, dec_vec, dec_middle_grad, bridge_w,
        scalars=1, name="dec_start_back",
    )
    side_cot = flip(enc_cot, 1)
    over_cot = swap(enc_cot, "section")
    d1_mine, d1_theirs = call(
        fold_more_kernel,
        [shaped((dec_mlp // 4 + dec_width // 4, dec_width))] * 2,
        place, d2_mine, d2_arrived, d1_mine, d1_theirs,
        scalars=1, name="fold_more",
    )
    d1_arrived = flip(d1_theirs, 2)
    small_rows = 256
    d3_keep, d3_send = call(
        dec_bridge_weights_kernel,
        [shaped((2, 2, enc_width // 8 + small_rows // 8, dec_width))] * 2,
        place, enc_pad, lifted_grad, pos_grad, start_sums, middle_sums, out_sum, up_sum, dec_bias_sum,
        scalars=1, scratch=[pltpu.VMEM((small_rows, dec_width), FULL)], name="dec_bridge_weights",
    )
    d3_other = swap(d3_send, "section")
    side_cot, d3_keep = lax.optimization_barrier((side_cot, d3_keep))
    side_over_cot = swap(side_cot, "section")
    part, up, up_send = call(
        enc_hidden_back_kernel,
        [
            shaped((2 * images * VIS, enc_width)),
            shaped((2 * rows_e, enc_mlp)),
            shaped((2 * rows_e, enc_mlp // 4)),
        ],
        place, enc_cot, side_cot, slope, side_slope, enc_fc1, enc_fc2,
        scalars=1, after=[over_cot], name="enc_hidden_back",
    )
    up_over = swap(up_send, "section")
    part_other = swap(part, "tensor")
    d3_mine, d3_theirs = fold(order, place, 1, d3_keep, d3_other, after=[side_over_cot])
    d3_arrived = flip(d3_theirs, 1)
    e1_mine, e1_theirs = call(
        enc_hidden_weights_kernel,
        [shaped((enc_mlp // 4, enc_width))] * 2,
        place, hidden, side_hidden, enc_cot, side_cot, normed_two, side_normed_two, up,
        forward_over, side_forward_over, over_cot, side_over_cot, up_over,
        scalars=1, name="enc_hidden_weights",
    )
    e1_arrived = flip(e1_theirs, 2)
    d1 = add(order, d1_mine, d1_arrived)
    d1_arrived = cross_start(d1)
    back_part, middle_grad, middle_low, stacked, middle_two_sums, bias_sum, enc_up_sum, e3_send = call(
        functools.partial(enc_attend_back_kernel, images, enc_size),
        [
            shaped((2 * images * VIS, enc_width)),
            shaped((2 * rows_e, enc_width), FULL),
            shaped((2 * rows_e, enc_width)),
            shaped((3, 2 * rows_e, enc_local)),
            shaped((4, enc_width), FULL),
            shaped((2, enc_local), FULL),
            shaped((1, enc_mlp), FULL),
            shaped((2 * rows_e, 2 * enc_local)),
        ],
        place, middle, side_middle, enc_cot, side_cot, part, part_other, enc_vec, proj, side_proj,
        weights, side_weights, enc_qkv, enc_out_w, up,
        scalars=1, after=[d3_arrived], name="enc_attend_back",
    )
    e3_over = swap(e3_send, "section")
    back_part_other = swap(back_part, "tensor")
    d1 = cross_end(order, d1, d1_arrived)
    d1_spread = spread(d1)
    few = 32
    grad_in, small = call(
        functools.partial(enc_start_back_kernel, images),
        [shaped((images * VIS, 1, enc_width), FULL), shaped((few, enc_width))],
        x, side_x, back_part, back_part_other, enc_vec, middle_grad, middle_two_sums, enc_up_sum, bias_sum,
        scratch=[pltpu.VMEM((few, enc_width), FULL)], name="enc_start_back",
    )
    e1 = add(order, e1_mine, e1_arrived, after=[e3_over])
    dec_part_two, e1 = lax.optimization_barrier((dec_part_two, e1))
    dec_part_two_other = swap(dec_part_two, "tensor")
    e1_arrived = cross_start(e1)
    e3_mine, e3_theirs = call(
        last_weights_kernel,
        [
            shaped(
                (
                    ((enc_width // 4 + few // 2) * 2 * enc_local + (enc_width + small_rows) // 8 * dec_width)
                    // (dec_width // 2),
                    dec_width // 2,
                )
            )
        ] * 2,
        place, normed, side_normed, stacked, mix, side_mix, middle_low, forward_over, side_forward_over, e3_over,
        small, d3_mine, d3_arrived,
        scalars=1, after=[d1_spread[1]], name="last_weights",
    )
    e3_arrived = flip(e3_theirs, 2)
    d1_packed = pack(order, place, d1_spread)
    (dec_out,) = call(
        functools.partial(dec_out_kernel, images),
        [shaped((dec_rows, dec_width))],
        count, dec_middle, dec_part_two, dec_part_two_other, dec_vec,
        scalars=1, name="dec_out",
    )
    e1 = cross_end(order, e1, e1_arrived)
    e1_spread = spread(e1)
    e3 = add(order, e3_mine, e3_arrived)
    e3_arrived = cross_start(e3)
    g_dec_fc1, g_dec_fc2, g_dec_qkv, g_dec_out_w = call(
        dec_whole_kernel,
        [shaped(x.shape, FULL) for x in (dec_fc1, dec_fc2, dec_qkv, dec_out_w)],
        place, *d1_packed, scalars=1, name="dec_whole",
    )
    mark(order, e1_spread[1])
    e3 = cross_end(order, e3, e3_arrived)
    e3_spread = spread(e3)
    e1_packed = pack(order, place, e1_spread)
    mark(order, e3_spread[1])
    g_enc_fc1, g_enc_fc2 = call(
        enc_hidden_whole_kernel,
        [shaped(enc_fc1.shape, FULL), shaped(enc_fc2.shape, FULL)],
        place, *e1_packed, scalars=1, name="enc_hidden_whole",
    )
    e3_packed = pack(order, place, e3_spread)
    (
        g_enc_qkv, g_enc_out_w, g_enc_vec, g_enc_fc1_bias, g_enc_qv_bias,
        g_bridge, g_dec_pos, g_dec_vec, g_dec_fc1_bias, g_dec_qv_bias,
    ) = call(
        last_whole_kernel,
        [
            shaped(x.shape, FULL)
            for x in (
                enc_qkv, enc_out_w, enc_vec, enc_fc1_bias, enc_qv_bias,
                bridge_w, dec_pos, dec_vec, dec_fc1_bias, dec_qv_bias,
            )
        ],
        place, *e3_packed, scalars=1,
        scratch=[pltpu.VMEM((few, enc_width), FULL), pltpu.VMEM((small_rows, dec_width), FULL)],
        name="last_whole",
    )

    return (
        jnp.transpose(enc_out_both, (1, 0, 2)),
        dec_out[None],
        jnp.transpose(grad_in, (1, 0, 2)),
        g_enc_vec,
        jnp.transpose(g_enc_qkv, (1, 0, 2)),
        g_enc_qv_bias,
        g_enc_out_w,
        g_enc_fc1,
        g_enc_fc1_bias.reshape(-1),
        g_enc_fc2,
        g_bridge,
        g_dec_vec,
        g_dec_pos,
        jnp.transpose(g_dec_qkv, (1, 0, 2)),
        g_dec_qv_bias,
        g_dec_out_w,
        g_dec_fc1,
        g_dec_fc1_bias.reshape(-1),
        g_dec_fc2,
    )


def solution(mesh):
    return jax.shard_map(
        body,
        mesh=mesh,
        in_specs=(
            P(None, "dp", None),
            P(None, "dp", None),
            P(None, "dp"),
            P(),
            P(None, None, "tensor"),
            P(None, "tensor"),
            P("tensor", None),
            P(None, "tensor"),
            P("tensor"),
            P("tensor", None),
            P(),
            P(),
            P(),
            P(None, None, "tensor"),
            P(None, "tensor"),
            P("tensor", None),
            P(None, "tensor"),
            P("tensor"),
            P("tensor", None),
            P(None, "dp", None),
        ),
        out_specs=(
            P(None, "dp", None),
            P("section", "dp", None),
            P("section", "dp", None),
            P(),
            P(None, None, "tensor"),
            P(None, "tensor"),
            P("tensor", None),
            P(None, "tensor"),
            P("tensor"),
            P("tensor", None),
            P(),
            P(),
            P(),
            P(None, None, "tensor"),
            P(None, "tensor"),
            P("tensor", None),
            P(None, "tensor"),
            P("tensor"),
            P("tensor", None),
        ),
        check_vma=False,
    )
```

```python
import functools
import math

import jax
import jax.numpy as jnp
from jax import lax
from jax.experimental import pallas as pl
from jax.experimental.pallas import tpu as pltpu
from jax.sharding import PartitionSpec as P

HE = 12
HD = 16
PATCHES = 196
VIS = 49
PAD_E = 64
PAD_D = 208
LANES = 128
EPSILON = 1e-06
LOW = jnp.bfloat16
FULL = jnp.float32
MIB = 2**20


def low(values):
    return values.astype(LOW)


def full(values):
    return values.astype(FULL)


def matmul(left, right):
    return jnp.dot(left, right, preferred_element_type=FULL)


def left_product(left, right):
    return lax.dot_general(left, right, (((0,), (0,)), ((), ())), preferred_element_type=FULL)


def right_product(left, right):
    return lax.dot_general(left, right, (((1,), (1,)), ((), ())), preferred_element_type=FULL)


def pair(first, second):
    return full(first) + full(second)


def swap(value, axis):
    return lax.ppermute(value, axis, [(i, i ^ 1) for i in range(lax.axis_size(axis))])


def normalize(values):
    center = values - jnp.mean(values, axis=-1, keepdims=True)
    scale = lax.rsqrt(jnp.mean(center * center, axis=-1, keepdims=True) + EPSILON)
    return center * scale, scale


def norm_back(grad, gain, xhat, scale):
    inner = grad * gain
    return scale * (
        inner
        - jnp.mean(inner, axis=-1, keepdims=True)
        - xhat * jnp.mean(inner * xhat, axis=-1, keepdims=True)
    )


def column_sum(values):
    return jnp.sum(full(values), axis=0, keepdims=True)


def one_hot_rows(padded, length, images, packed_first=False):
    shape = (images * length, images * padded) if packed_first else (images * padded, images * length)
    first = lax.broadcasted_iota(jnp.int32, shape, 0)
    second = lax.broadcasted_iota(jnp.int32, shape, 1)
    packed, wide = (first, second) if packed_first else (second, first)
    hit = None
    for image in range(images):
        here = (
            (packed >= image * length)
            & (packed < (image + 1) * length)
            & (wide - image * padded == packed - image * length)
        )
        hit = here if hit is None else hit | here
    return low(jnp.where(hit, 1.0, 0.0))


def packed_rows(values, images):
    return low(matmul(one_hot_rows(PAD_E, VIS, images, True), low(values)))


def padded_sum(part_ref, other_ref, images):
    spread = one_hot_rows(PAD_E, VIS, images)
    return matmul(spread, part_ref[...]) + matmul(spread, other_ref[...])


def head_masks(head_size):
    lane = lax.broadcasted_iota(jnp.int32, (1, LANES), 1)
    return [
        jnp.where((lane >= j * head_size) & (lane < (j + 1) * head_size), 1.0, 0.0)
        for j in range(LANES // head_size)
    ]


def spread_heads(values, masks):
    wide = full(values)
    return jnp.concatenate([low(wide * mask) for mask in masks], axis=0)


def gather_heads(stacked, masks):
    rows = stacked.shape[0] // len(masks)
    total = None
    for j, mask in enumerate(masks):
        term = stacked[j * rows : (j + 1) * rows] * mask
        total = term if total is None else total + term
    return total


def attend(queries, key_rows, value_rows, masks, allowed, factor):
    scores = right_product(spread_heads(queries, masks), key_rows) * factor
    scores = jnp.where(allowed, scores, -1e30)
    exponent = jnp.exp(scores - jnp.max(scores, axis=-1, keepdims=True))
    weights_low = low(exponent * (1.0 / jnp.sum(exponent, axis=-1, keepdims=True)))
    return weights_low, low(gather_heads(matmul(weights_low, value_rows), masks))


def attend_back(queries, key_rows, value_rows, weights_low, upstream, masks, factor):
    spread_up = spread_heads(upstream, masks)
    weight_grad = right_product(spread_up, value_rows)
    weights = full(weights_low)
    product = weights * weight_grad
    score_grad = low(product - weights * jnp.sum(product, axis=-1, keepdims=True))
    query_grad = gather_heads(matmul(score_grad, key_rows), masks) * factor
    key_grad = left_product(score_grad, spread_heads(queries, masks)) * factor
    value_grad = left_product(weights_low, spread_up)
    return low(query_grad), low(key_grad), low(value_grad)


def same_image(heads, images, padded, length):
    shape = (heads * images * padded, images * padded)
    row = lax.broadcasted_iota(jnp.int32, shape, 0)
    key = lax.broadcasted_iota(jnp.int32, shape, 1)
    hit = None
    for head in range(heads):
        for image in range(images):
            start = (head * images + image) * padded
            here = (
                (row >= start)
                & (row < start + padded)
                & (key >= image * padded)
                & (key < image * padded + length)
            )
            hit = here if hit is None else hit | here
    return hit


def live_rows(count, rows, padded):
    row = lax.broadcasted_iota(jnp.int32, (rows, 1), 0)
    return jnp.where(row < count * padded, 1.0, 0.0)


def kernel_call(order, kernel, outs, *arguments, scalars=0, scratch=(), after=(), memory=24, name=None):
    count = len(arguments)
    before = order[-1:] + list(after)

    def run(*refs):
        mark = count + len(before) + len(outs)
        refs[mark][...] = jnp.zeros((8, LANES), FULL)
        kernel(*refs[:count], *refs[count + len(before) : mark], *refs[mark + 1 :])

    specs = [pl.BlockSpec(memory_space=pltpu.SMEM)] * scalars
    specs += [pl.BlockSpec(memory_space=pltpu.VMEM)] * (count - scalars)
    specs += [pl.BlockSpec(memory_space=pl.ANY)] * len(before)
    results = pl.pallas_call(
        run,
        out_shape=[jax.ShapeDtypeStruct(x.shape, x.dtype) for x in outs] + [shaped((8, LANES), FULL)],
        in_specs=specs,
        out_specs=[pl.BlockSpec(memory_space=pltpu.VMEM)] * (len(outs) + 1),
        scratch_shapes=scratch,
        compiler_params=pltpu.CompilerParams(vmem_limit_bytes=memory * MIB),
        cost_estimate=pl.CostEstimate(flops=36000000000, bytes_accessed=1, transcendentals=0),
        name=name,
    )(*arguments, *before)
    order.append(results[-1])
    return results[:-1]


def chunk(index, size):
    return pl.ds(pl.multiple_of(index * size, LANES), size)


def shaped(shape, dtype=LOW):
    return jax.ShapeDtypeStruct(shape, dtype)


def project_heads(normed, qkv_ref, bias, proj_ref, width):
    queries = low(matmul(normed, qkv_ref[0]) + bias[0:1])
    key_rows = low(matmul(normed, qkv_ref[1]))
    value_rows = low(matmul(normed, qkv_ref[2]) + bias[1:2])
    proj_ref[0] = queries
    proj_ref[1] = key_rows
    proj_ref[2] = value_rows


def enc_attend_kernel(
    images, head_size, place_ref, x_ref, vec_ref, qkv_ref, bias_ref, out_w_ref,
    part_ref, x_out_ref, normed_ref, proj_ref, weights_ref, mix_ref,
):
    width = qkv_ref.shape[2]
    if len(x_ref.shape) == 2:
        rows = x_ref[...]
    else:
        rows = low(jnp.where(place_ref[0] == 0, full(x_ref[:, 0, :]), full(x_ref[:, 1, :])))
    x = matmul(one_hot_rows(PAD_E, VIS, images), rows)
    x_out_ref[...] = low(x)
    vec = full(vec_ref[...])
    xhat, _ = normalize(x)
    normed = low(xhat * vec[0:1] + vec[1:2])
    normed_ref[...] = normed
    project_heads(normed, qkv_ref, full(bias_ref[...]), proj_ref, width)
    masks = head_masks(head_size)
    allowed = same_image(len(masks), images, PAD_E, VIS)
    for group in range(width // LANES):
        lanes = slice(group * LANES, (group + 1) * LANES)
        weights_low, mixture = attend(
            proj_ref[0, :, lanes],
            proj_ref[1, :, lanes],
            proj_ref[2, :, lanes],
            masks,
            allowed,
            1.0 / math.sqrt(head_size),
        )
        weights_ref[group] = weights_low
        mix_ref[:, lanes] = mixture
    part_ref[...] = packed_rows(matmul(mix_ref[...], out_w_ref[...]), images)


def mlp_forward(middle, gain, shift, fc1_ref, bias_ref, fc2_ref, normed_ref, hidden_ref, slope_ref):
    xhat, _ = normalize(middle)
    normed = low(xhat * gain + shift)
    normed_ref[...] = normed
    pre = matmul(normed, fc1_ref[...]) + full(bias_ref[...])
    share = 0.5 + 0.5 * lax.erf(pre * math.sqrt(0.5))
    hidden = low(pre * share)
    hidden_ref[...] = hidden
    slope = share + pre * jnp.exp(-0.5 * pre * pre) * (1.0 / math.sqrt(2.0 * math.pi))
    if slope_ref is not None:
        slope_ref[...] = low(slope)
    return None if fc2_ref is None else low(matmul(hidden, fc2_ref[...])), slope


def enc_forward_send(place_ref, first_normed_ref, mix_ref, normed_ref, hidden_ref, send_ref):
    core, side = 1 - place_ref[0], place_ref[1]
    width, wide = normed_ref.shape[1], hidden_ref.shape[1] // 4
    half = width // 2
    send_ref[:, :wide] = hidden_ref[:, chunk(2 * core + side, wide)]
    send_ref[:, wide : wide + width] = normed_ref[...]
    send_ref[:, wide + width : wide + width + half] = first_normed_ref[:, chunk(core, half)]
    send_ref[:, wide + width + half :] = mix_ref[...]


def enc_hidden_kernel(
    place_ref, x_ref, vec_ref, part_ref, other_ref, fc1_ref, bias_ref, first_normed_ref, mix_ref, fc2_ref,
    part_two_ref, middle_ref, normed_ref, hidden_ref, slope_ref, send_ref,
):
    vec = full(vec_ref[...])
    middle = full(x_ref[...]) + padded_sum(part_ref, other_ref, x_ref.shape[0] // PAD_E) + vec[2:3]
    middle_ref[...] = middle
    part, _ = mlp_forward(
        middle, vec[3:4], vec[4:5], fc1_ref, bias_ref, fc2_ref, normed_ref, hidden_ref, slope_ref
    )
    part_two_ref[...] = packed_rows(part, x_ref.shape[0] // PAD_E)
    enc_forward_send(place_ref, first_normed_ref, mix_ref, normed_ref, hidden_ref, send_ref)


def enc_side_hidden_kernel(
    place_ref, x_ref, vec_ref, part_ref, other_ref, fc1_ref, bias_ref, first_normed_ref, mix_ref,
    middle_ref, normed_ref, hidden_ref, slope_ref, send_ref,
):
    vec = full(vec_ref[...])
    middle = full(x_ref[...]) + padded_sum(part_ref, other_ref, x_ref.shape[0] // PAD_E) + vec[2:3]
    middle_ref[...] = middle
    mlp_forward(middle, vec[3:4], vec[4:5], fc1_ref, bias_ref, None, normed_ref, hidden_ref, slope_ref)
    enc_forward_send(place_ref, first_normed_ref, mix_ref, normed_ref, hidden_ref, send_ref)


def both_cores_kernel(place_ref, own_ref, over_ref, both_ref):
    first = place_ref[0] == 0
    own, over = full(own_ref[...]), full(over_ref[...])
    both_ref[:, 0, :] = low(jnp.where(first, own, over))
    both_ref[:, 1, :] = low(jnp.where(first, over, own))


def selector(keep_ref, image):
    patch = lax.broadcasted_iota(jnp.int32, (PAD_D, PAD_E), 0)
    return jnp.where(patch == keep_ref[image : image + 1, :], 1.0, 0.0)


def dec_attend_kernel(
    images, head_size, count_ref, keep_ref, middle_ref, part_ref, other_ref, enc_vec_ref, bridge_ref,
    vec_ref, pos_ref, qkv_ref, bias_ref, out_w_ref,
    part_out_ref, enc_out_ref, enc_pad_ref, starting_ref, normed_ref, proj_ref, weights_ref, mix_ref,
):
    width = qkv_ref.shape[2]
    vec = full(vec_ref[...])
    encoded = middle_ref[...] + padded_sum(part_ref, other_ref, images) + full(enc_vec_ref[...])[5:6]
    enc_pad = low(encoded * live_rows(count_ref[0], images * PAD_E, PAD_E))
    enc_pad_ref[...] = enc_pad
    enc_out_ref[...] = low(matmul(one_hot_rows(PAD_E, VIS, images, True), enc_pad))
    lifted = matmul(enc_pad, bridge_ref[...]) + vec[0:1]
    lifted_high = low(lifted)
    lifted_rest = low(lifted - full(lifted_high))
    pos = matmul(one_hot_rows(PAD_D, PATCHES, 1), pos_ref[...])
    for image in range(images):
        chosen = selector(keep_ref, image)
        rows = slice(image * PAD_E, (image + 1) * PAD_E)
        placed = matmul(low(chosen), lifted_high[rows]) + matmul(low(chosen), lifted_rest[rows])
        hidden_patch = 1.0 - jnp.sum(chosen, axis=1, keepdims=True)
        starting_ref[image * PAD_D : (image + 1) * PAD_D, :] = placed + hidden_patch * vec[1:2] + pos
    xhat, _ = normalize(starting_ref[...])
    normed = low(xhat * vec[2:3] + vec[3:4])
    normed_ref[...] = normed
    project_heads(normed, qkv_ref, full(bias_ref[...]), proj_ref, width)
    masks = head_masks(head_size)
    allowed = lax.broadcasted_iota(jnp.int32, (1, PAD_D), 1) < PATCHES
    groups = width // LANES
    for image in range(images):
        rows = slice(image * PAD_D, (image + 1) * PAD_D)
        for group in range(groups):
            lanes = slice(group * LANES, (group + 1) * LANES)
            weights_low, mixture = attend(
                proj_ref[0, rows, lanes],
                proj_ref[1, rows, lanes],
                proj_ref[2, rows, lanes],
                masks,
                allowed,
                1.0 / math.sqrt(head_size),
            )
            weights_ref[image * groups + group] = weights_low
            mix_ref[rows, lanes] = mixture
    part_out_ref[...] = low(matmul(mix_ref[...], out_w_ref[...]))


def dec_hidden_kernel(
    images, count_ref, place_ref, starting_ref, part_ref, other_ref, vec_ref, fc1_ref, bias_ref, fc2_ref, cot_ref,
    part_back_ref, part_two_ref, middle_ref, normed_ref, hidden_ref, out_low_ref, up_ref,
    up_sum_ref, out_sum_ref, send_ref,
):
    vec = full(vec_ref[...])
    middle = starting_ref[...] + pair(part_ref[...], other_ref[...]) + vec[4:5]
    middle_ref[...] = middle
    part, slope = mlp_forward(
        middle, vec[5:6], vec[6:7], fc1_ref, bias_ref, fc2_ref, normed_ref, hidden_ref, None
    )
    part_two_ref[...] = part
    spread = matmul(one_hot_rows(PAD_D, PATCHES, images), cot_ref[...])
    out_low = low(spread * live_rows(count_ref[0], images * PAD_D, PAD_D))
    out_low_ref[...] = out_low
    up_grad = low(slope * right_product(out_low, fc2_ref[...]))
    up_ref[...] = up_grad
    part_back_ref[...] = low(right_product(up_grad, fc1_ref[...]))
    up_sum_ref[...] = column_sum(up_grad)
    out_sum_ref[...] = column_sum(out_low)
    core = 1 - place_ref[0]
    width, wide = out_low.shape[1], up_grad.shape[1]
    half = width // 2
    send_ref[:, : wide // 2] = hidden_ref[:, chunk(core, wide // 2)]
    send_ref[:, wide // 2 : wide // 2 + half] = normed_ref[:, chunk(core, half)]
    send_ref[:, wide // 2 + half : wide // 2 + half + wide] = up_grad
    send_ref[:, wide // 2 + half + wide :] = out_low


def dec_out_kernel(images, count_ref, middle_ref, part_ref, other_ref, vec_ref, out_ref):
    decoded = middle_ref[...] + pair(part_ref[...], other_ref[...]) + full(vec_ref[...])[7:8]
    decoded = low(decoded * live_rows(count_ref[0], images * PAD_D, PAD_D))
    out_ref[...] = low(matmul(one_hot_rows(PAD_D, PATCHES, images, True), decoded))


def attention_back(
    first_row, images, padded, together, head_size, mixture_grad, proj_ref, weights_ref, stacked_ref
):
    masks = head_masks(head_size)
    groups = proj_ref.shape[2] // LANES
    step = images if together else 1
    for first in range(0, images, step):
        rows = slice(first * padded, (first + step) * padded)
        out_rows = slice(first_row + first * padded, first_row + (first + step) * padded)
        for group in range(groups):
            lanes = slice(group * LANES, (group + 1) * LANES)
            grads = attend_back(
                proj_ref[0, rows, lanes],
                proj_ref[1, rows, lanes],
                proj_ref[2, rows, lanes],
                weights_ref[first // step * groups + group],
                mixture_grad[out_rows, lanes],
                masks,
                1.0 / math.sqrt(head_size),
            )
            for j in range(3):
                stacked_ref[j, out_rows, lanes] = grads[j]


def normed_back(stacked_ref, qkv_ref):
    total = right_product(stacked_ref[0], qkv_ref[0])
    for j in (1, 2):
        total = total + right_product(stacked_ref[j], qkv_ref[j])
    return low(total)


def dec_attend_back_kernel(
    images, head_size, place_ref, middle_ref, out_low_ref, part_in_ref, other_ref, vec_ref, proj_ref, weights_ref,
    qkv_ref, out_w_ref, normed_ref, mix_ref,
    part_ref, middle_grad_ref, middle_low_ref, stacked_ref, sums_ref, bias_sum_ref, send_ref,
):
    vec = full(vec_ref[...])
    two_grad = pair(part_in_ref[...], other_ref[...])
    xhat, scale = normalize(middle_ref[...])
    middle_grad = full(out_low_ref[...]) + norm_back(two_grad, vec[5:6], xhat, scale)
    middle_grad_ref[...] = middle_grad
    middle_low = low(middle_grad)
    middle_low_ref[...] = middle_low
    mixture_grad = low(right_product(middle_low, out_w_ref[...]))
    attention_back(0, images, PAD_D, False, head_size, mixture_grad, proj_ref, weights_ref, stacked_ref)
    part_ref[...] = normed_back(stacked_ref, qkv_ref)
    core = 1 - place_ref[0]
    width = mix_ref.shape[1]
    half = middle_low.shape[1] // 2
    for j in range(3):
        send_ref[:, j * width : (j + 1) * width] = stacked_ref[j]
    send_ref[:, 3 * width : 4 * width] = mix_ref[...]
    send_ref[:, 4 * width : 4 * width + half] = normed_ref[:, chunk(core, half)]
    send_ref[:, 4 * width + half :] = middle_low_ref[:, chunk(core, half)]
    sums_ref[0:1] = column_sum(middle_grad)
    sums_ref[1:2] = column_sum(two_grad * xhat)
    sums_ref[2:3] = column_sum(two_grad)
    bias_sum_ref[0:1] = column_sum(stacked_ref[0])
    bias_sum_ref[1:2] = column_sum(stacked_ref[2])


def dec_start_back_kernel(
    images, count_ref, keep_ref, starting_ref, part_ref, other_ref, vec_ref, middle_grad_ref, bridge_ref,
    enc_cot_ref, lifted_ref, pos_ref, sums_ref,
):
    vec = full(vec_ref[...])
    one_grad = pair(part_ref[...], other_ref[...])
    xhat, scale = normalize(starting_ref[...])
    starting_grad = middle_grad_ref[...] + norm_back(one_grad, vec[2:3], xhat, scale)
    sums_ref[2:3] = column_sum(one_grad * xhat)
    sums_ref[3:4] = column_sum(one_grad)
    token = None
    total = None
    for image in range(images):
        grad = starting_grad[image * PAD_D : (image + 1) * PAD_D]
        chosen = selector(keep_ref, image)
        hidden_patch = 1.0 - jnp.sum(chosen, axis=1, keepdims=True)
        term = column_sum(hidden_patch * grad)
        token = term if token is None else token + term
        total = grad if total is None else total + grad
        lifted_ref[image * PAD_E : (image + 1) * PAD_E, :] = low(left_product(low(chosen), low(grad)))
    pos_ref[...] = total
    lifted_grad = lifted_ref[...]
    sums_ref[0:1] = column_sum(lifted_grad)
    sums_ref[1:2] = token
    handed = right_product(lifted_grad, bridge_ref[...])
    enc_cot_ref[...] = low(handed * live_rows(count_ref[0], images * PAD_E, PAD_E))


def enc_hidden_back_kernel(
    place_ref, cot_a, cot_b, slope_a, slope_b, fc1_ref, fc2_ref, part_ref, up_ref, send_ref
):
    slope = jnp.concatenate([slope_a[...], slope_b[...]], axis=0)
    up_grad = low(full(slope) * right_product(stacked_rows(cot_a, cot_b), fc2_ref[...]))
    up_ref[...] = up_grad
    part_ref[...] = packed_rows(right_product(up_grad, fc1_ref[...]), up_grad.shape[0] // PAD_E)
    send_ref[...] = up_ref[:, chunk(2 * (1 - place_ref[0]) + place_ref[1], send_ref.shape[1])]


def enc_attend_back_kernel(
    images, head_size, place_ref, middle_a, middle_b, cot_a, cot_b, part_in_ref, other_ref, vec_ref, proj_a, proj_b,
    weights_a, weights_b, qkv_ref, out_w_ref, up_ref,
    part_ref, middle_grad_ref, middle_low_ref, stacked_ref, sums_ref, bias_sum_ref, up_sum_ref, send_ref,
):
    vec = full(vec_ref[...])
    own = middle_a.shape[0]
    cot = full(stacked_rows(cot_a, cot_b))
    two_grad = padded_sum(part_in_ref, other_ref, 2 * images)
    xhat, scale = normalize(stacked_rows(middle_a, middle_b))
    middle_grad = cot + norm_back(two_grad, vec[3:4], xhat, scale)
    middle_grad_ref[...] = middle_grad
    middle_low = low(middle_grad)
    middle_low_ref[...] = middle_low
    mixture_grad = low(right_product(middle_low, out_w_ref[...]))
    attention_back(0, images, PAD_E, True, head_size, mixture_grad, proj_a, weights_a, stacked_ref)
    attention_back(own, images, PAD_E, True, head_size, mixture_grad, proj_b, weights_b, stacked_ref)
    part_ref[...] = packed_rows(normed_back(stacked_ref, qkv_ref), 2 * images)
    width = qkv_ref.shape[2]

    @pl.when(place_ref[1] == 0)
    def _():
        send_ref[:, :width] = stacked_ref[0]
        send_ref[:, width:] = stacked_ref[1]

    @pl.when(place_ref[1] == 1)
    def _():
        send_ref[:, :width] = stacked_ref[2]
        send_ref[:, width:] = middle_low_ref[:, chunk(1 - place_ref[0], width)]

    sums_ref[0:1] = column_sum(middle_grad)
    sums_ref[1:2] = column_sum(two_grad * xhat)
    sums_ref[2:3] = column_sum(two_grad)
    sums_ref[3:4] = column_sum(cot)
    bias_sum_ref[0:1] = column_sum(stacked_ref[0])
    bias_sum_ref[1:2] = column_sum(stacked_ref[2])
    up_sum_ref[...] = column_sum(up_ref[...])


def enc_start_back_kernel(
    images, x_a, x_b, part_ref, other_ref, vec_ref, middle_grad_ref, sums_ref, up_sum_ref, bias_sum_ref,
    grad_in_ref, small_ref, rows_ref,
):
    vec = full(vec_ref[...])
    own = x_a.shape[0]
    one_grad = padded_sum(part_ref, other_ref, 2 * images)
    xhat, scale = normalize(full(stacked_rows(x_a, x_b)))
    grad = middle_grad_ref[:own] + norm_back(one_grad[:own], vec[0:1], xhat[:own], scale[:own])
    take = full(one_hot_rows(PAD_E, VIS, images, True))
    grad_in_ref[:, 0, :] = jnp.dot(
        take, grad, preferred_element_type=FULL, precision=lax.Precision.HIGHEST
    )
    rows_ref[...] = jnp.zeros_like(rows_ref)
    rows_ref[0:1] = column_sum(one_grad * xhat)
    rows_ref[1:2] = column_sum(one_grad)
    rows_ref[2:6] = sums_ref[...]
    put_rows(rows_ref, 6, up_sum_ref, bias_sum_ref)
    small_ref[...] = low(rows_ref[...])


def tall(*parts):
    return jnp.concatenate(parts, axis=0)


def by_side(place_ref, mine_ref, theirs_ref, blocks):
    first = place_ref[1] == 0
    rows = mine_ref.shape[1]
    for part in range(2):
        zero, one = (low(block[part * rows : (part + 1) * rows]) for block in blocks)
        mine_ref[part] = jnp.where(first, zero, one)
        theirs_ref[part] = jnp.where(first, one, zero)


def dec_hidden_weights_kernel(
    place_ref, hidden_ref, out_low_ref, normed_ref, up_ref, over_ref, mine_ref, theirs_ref
):
    core = place_ref[0]
    width, wide = out_low_ref.shape[1], up_ref.shape[1]
    half = width // 2
    over_up = over_ref[:, wide // 2 + half : wide // 2 + half + wide]
    over_out = over_ref[:, wide // 2 + half + wide :]
    down = left_product(
        tall(hidden_ref[:, chunk(core, wide // 2)], over_ref[:, : wide // 2]), tall(out_low_ref[...], over_out)
    )
    up = left_product(
        tall(normed_ref[:, chunk(core, half)], over_ref[:, wide // 2 : wide // 2 + half]),
        tall(up_ref[...], over_up),
    )
    by_side(place_ref, mine_ref, theirs_ref, (down, tall(up[:, :width], up[:, width:])))


def dec_head_weights_kernel(
    place_ref, normed_ref, stacked_ref, mix_ref, middle_low_ref, over_ref, mine_ref, theirs_ref
):
    core = place_ref[0]
    width = mix_ref.shape[1]
    half = normed_ref.shape[1] // 2
    left = tall(normed_ref[:, chunk(core, half)], over_ref[:, 4 * width : 4 * width + half])
    grads = [
        left_product(left, tall(stacked_ref[j], over_ref[:, j * width : (j + 1) * width])) for j in range(3)
    ]
    out = left_product(
        tall(mix_ref[...], over_ref[:, 3 * width : 4 * width]),
        tall(middle_low_ref[:, chunk(core, half)], over_ref[:, 4 * width + half :]),
    )
    by_side(
        place_ref, mine_ref, theirs_ref,
        (jnp.concatenate(grads[:2], axis=1), jnp.concatenate([grads[2], out], axis=1)),
    )


def put_rows(rows_ref, row, up_sum_ref, bias_sum_ref):
    cols = rows_ref.shape[1]
    for piece in range(up_sum_ref.shape[1] // cols):
        rows_ref[row : row + 1] = up_sum_ref[:, piece * cols : (piece + 1) * cols]
        row += 1
    width = bias_sum_ref.shape[1]
    for piece in range(2):
        here, lane = row + piece * width // cols, piece * width % cols
        rows_ref[here : here + 1, lane : lane + width] = bias_sum_ref[piece : piece + 1]


def take_rows(rows_ref, row, up_sum_ref, bias_sum_ref):
    cols = rows_ref.shape[1]
    for line in range(up_sum_ref.shape[0]):
        here, lane = row + line * LANES // cols, line * LANES % cols
        up_sum_ref[line : line + 1] = rows_ref[here : here + 1, lane : lane + LANES]
    row += up_sum_ref.shape[0] * LANES // cols
    width = bias_sum_ref.shape[1]
    for piece in range(2):
        here, lane = row + piece * width // cols, piece * width % cols
        bias_sum_ref[piece : piece + 1] = rows_ref[here : here + 1, lane : lane + width]


def dec_bridge_weights_kernel(
    place_ref, enc_pad_ref, lifted_ref, pos_ref, sums_ref, middle_sums_ref, out_sum_ref, up_sum_ref,
    bias_sum_ref, keep_ref, send_ref, small_ref,
):
    core = place_ref[0]
    cols = lifted_ref.shape[1]
    bridge = low(left_product(enc_pad_ref[...], lifted_ref[...]))
    quarter = bridge.shape[0] // 4
    small_ref[...] = jnp.zeros_like(small_ref)
    small_ref[0:PAD_D] = pos_ref[...]
    row = PAD_D
    for ref, count in ((sums_ref, 4), (middle_sums_ref, 3), (out_sum_ref, 1)):
        small_ref[row : row + count] = ref[...]
        row += count
    put_rows(small_ref, row, up_sum_ref, bias_sum_ref)
    few = small_ref.shape[0] // 4
    first = core == 0

    def block(index):
        return jnp.concatenate(
            [bridge[index * quarter : (index + 1) * quarter], low(small_ref[index * few : (index + 1) * few])],
            axis=0,
        )

    for side in range(2):
        zero, one = block(side), block(2 + side)
        half = zero.shape[0] // 2
        for part in range(2):
            rows = slice(part * half, (part + 1) * half)
            keep_ref[side, part] = jnp.where(first, zero[rows], one[rows])
            send_ref[side, part] = jnp.where(first, one[rows], zero[rows])


def stacked_rows(first, second, lanes=slice(None)):
    return jnp.concatenate([first[:, lanes], second[:, lanes]], axis=0)


def enc_hidden_weights_kernel(
    place_ref, hidden_a, hidden_b, cot_a, cot_b, normed_a, normed_b, up_ref,
    forward_a, forward_b, over_cot_a, over_cot_b, over_up, mine_ref, theirs_ref,
):
    core, side, half = place_ref[0], place_ref[1], place_ref[2]
    rows = mine_ref.shape[0] // 2
    width = 2 * rows
    features = cot_a.shape[1]
    lanes = chunk(2 * core + side, width)
    down = low(
        left_product(
            tall(hidden_a[:, lanes], hidden_b[:, lanes], forward_a[:, :width], forward_b[:, :width]),
            tall(cot_a[...], cot_b[...], over_cot_a[...], over_cot_b[...]),
        )
    )
    here = slice(width, width + features)
    up = low(
        left_product(
            tall(normed_a[...], normed_b[...], forward_a[:, here], forward_b[:, here]),
            tall(up_ref[:, lanes], over_up[...]),
        )
    )
    for part in range(2):
        block = (
            down[part * rows : (part + 1) * rows],
            up[2 * part * rows : (2 * part + 1) * rows],
            up[(2 * part + 1) * rows : (2 * part + 2) * rows],
        )
        for ref, index in ((mine_ref, half), (theirs_ref, 1 - half)):

            @pl.when(index == part)
            def _(ref=ref, block=block):
                ref[:rows] = block[0]
                ref[rows:, :width] = block[1]
                ref[rows:, width:] = block[2]


def last_weights_kernel(
    place_ref, normed_a, normed_b, stacked_ref, mix_a, mix_b, middle_low_ref, forward_a, forward_b, over_ref,
    small_ref, rest_mine, rest_other, mine_ref, theirs_ref,
):
    core, half = place_ref[0], place_ref[2]
    width = mix_a.shape[1]
    half_width = normed_a.shape[1] // 2
    lanes = chunk(core, half_width)
    start = forward_a.shape[1] - half_width - width
    left = tall(
        normed_a[:, lanes], normed_b[:, lanes],
        forward_a[:, start : start + half_width], forward_b[:, start : start + half_width],
    )
    few = small_ref.shape[0] // 2
    columns = mine_ref.shape[1]

    def put(first, second):
        rows = first.shape[0] // 2
        for part in range(2):
            here = slice(part * rows, (part + 1) * rows)
            block = jnp.concatenate([first[here], second[here]], axis=1)
            block = tall(low(block), small_ref[part * few : (part + 1) * few])
            for ref, index in ((mine_ref, half), (theirs_ref, 1 - half)):

                @pl.when(index == part)
                def _(ref=ref, block=block):
                    for i in range(block.shape[1] // columns):
                        ref[i * block.shape[0] : (i + 1) * block.shape[0]] = block[
                            :, i * columns : (i + 1) * columns
                        ]

    @pl.when(place_ref[1] == 0)
    def _():
        put(
            left_product(left, tall(stacked_ref[0], over_ref[:, :width])),
            left_product(left, tall(stacked_ref[1], over_ref[:, width:])),
        )

    @pl.when(place_ref[1] == 1)
    def _():
        put(
            left_product(left, tall(stacked_ref[2], over_ref[:, :width])),
            left_product(
                tall(mix_a[...], mix_b[...], forward_a[:, start + half_width :], forward_b[:, start + half_width :]),
                tall(middle_low_ref[:, lanes], over_ref[:, width:]),
            ),
        )

    for ref, index in ((mine_ref, half), (theirs_ref, 1 - half)):
        total = low(pair(rest_mine[index], rest_other[index]))
        count = total.shape[0]
        row = ref.shape[0] - count * (total.shape[1] // columns)
        for i in range(total.shape[1] // columns):
            ref[row + i * count : row + (i + 1) * count] = total[:, i * columns : (i + 1) * columns]


def fold_kernel(axis, place_ref, *refs):
    index = place_ref[axis]
    mine_ref, theirs_ref = refs[-2:]
    rows = 0
    for keep_ref, other_ref in zip(refs[:-2:2], refs[1:-2:2]):
        here = (slice(None),) * (len(keep_ref.shape) - 3) + (slice(rows, rows + keep_ref.shape[-2]),)
        rows += keep_ref.shape[-2]
        mine_ref[here] = low(pair(keep_ref[index], other_ref[index]))
        theirs_ref[here] = low(pair(keep_ref[1 - index], other_ref[1 - index]))


def fold_more_kernel(place_ref, keep_ref, other_ref, before_mine, before_theirs, mine_ref, theirs_ref):
    index = place_ref[2]
    rows = before_mine.shape[0]
    mine_ref[:rows] = before_mine[...]
    theirs_ref[:rows] = before_theirs[...]
    mine_ref[rows:] = low(pair(keep_ref[index], other_ref[index]))
    theirs_ref[rows:] = low(pair(keep_ref[1 - index], other_ref[1 - index]))


def add_kernel(first_ref, second_ref, sum_ref):
    sum_ref[...] = low(pair(first_ref[...], second_ref[...]))


def fold(order, place, axis, *arrays, after=()):
    shape = arrays[0].shape[1:-2] + (sum(x.shape[-2] for x in arrays[::2]), arrays[0].shape[-1])
    return kernel_call(
        order, functools.partial(fold_kernel, axis), [shaped(shape)] * 2, place, *arrays,
        scalars=1, after=after, name="fold",
    )


def add(order, first, second, after=()):
    return kernel_call(order, add_kernel, [shaped(first.shape)], first, second, after=after, name="add")[0]


def mark_kernel(out_ref):
    out_ref[...] = jnp.zeros_like(out_ref)


def mark(order, *values):
    kernel_call(order, mark_kernel, [shaped((8, LANES), FULL)], after=values, name="mark")


def flip(value, step):
    return lax.ppermute(value, "dp", [(i, i ^ step) for i in range(lax.axis_size("dp"))])


def cross_start(value):
    return flip(value, 4) if lax.axis_size("dp") > 4 else jnp.zeros_like(value)


def cross_end(order, value, arrived, after=()):
    value = add(order, value, arrived, after)
    step = 8
    while step < lax.axis_size("dp"):
        value = add(order, value, flip(value, step))
        step *= 2
    return value


def pack_kernel(place_ref, mine_ref, other_ref, across_ref, there_ref, packed_ref):
    side, half = place_ref[1], place_ref[2]
    packed_ref[side, half] = mine_ref[...]
    packed_ref[side, 1 - half] = other_ref[...]
    packed_ref[1 - side, half] = across_ref[...]
    packed_ref[1 - side, 1 - half] = there_ref[...]


def pieces_of(place_ref, own_ref, over_ref):
    core = place_ref[0]
    return [
        (ref.at[side, half], index, side, half)
        for ref, index in ((own_ref, core), (over_ref, 1 - core))
        for side in range(2)
        for half in range(2)
    ]


def aligned(index, size):
    return pl.ds(pl.multiple_of(index * size, size), size)


def put_heads(block, core, side, half, qkv_ref, out_w_ref):
    rows, width = block.shape[0], qkv_ref.shape[2]
    here = aligned(2 * core + half, rows)
    if side == 0:
        qkv_ref[0, here, :] = full(block[:, :width])
        qkv_ref[1, here, :] = full(block[:, width:])
    else:
        qkv_ref[2, here, :] = full(block[:, :width])
        out_w_ref[half * rows : (half + 1) * rows, aligned(core, width)] = full(block[:, width:])


def dec_whole_kernel(place_ref, own_ref, over_ref, fc1_ref, fc2_ref, qkv_ref, out_w_ref):
    rows, cols = fc1_ref.shape[0] // 2, fc1_ref.shape[1] // 2
    for ref, core, side, half in pieces_of(place_ref, own_ref, over_ref):
        if side == 0:
            fc2_ref[aligned(2 * core + half, rows), :] = full(ref[:rows])
        else:
            fc1_ref[aligned(core, rows), half * cols : (half + 1) * cols] = full(ref[:rows])
        put_heads(ref[rows:], core, side, half, qkv_ref, out_w_ref)


def last_whole_kernel(
    place_ref, own_ref, over_ref, qkv_ref, out_w_ref, vec_ref, up_sum_ref, bias_sum_ref,
    bridge_ref, pos_ref, dec_vec_ref, dec_up_sum_ref, dec_bias_sum_ref, rows_ref, small_ref,
):
    few = rows_ref.shape[0] // 2
    rows = qkv_ref.shape[1] // 4 + few
    width = own_ref.shape[3]
    wide, cols = 2 * qkv_ref.shape[2], bridge_ref.shape[1]
    rest = (own_ref.shape[2] - rows * (wide // width)) * width // cols
    quarter, part = bridge_ref.shape[0] // 4, small_ref.shape[0] // 4

    def take(ref, row, count, lanes):
        return jnp.concatenate(
            [ref[row + i * count : row + (i + 1) * count] for i in range(lanes // width)], axis=1
        )

    for ref, core, side, half in pieces_of(place_ref, own_ref, over_ref):
        heads = take(ref, 0, rows, wide)
        put_heads(heads[: rows - few], core, side, half, qkv_ref, out_w_ref)
        block = take(ref, rows * (wide // width), rest, cols)
        index = 2 * core + side
        start = pl.multiple_of(index * quarter, 8)
        if half == 0:
            bridge_ref[pl.ds(start, rest), :] = full(block)
        else:
            left = quarter - rest
            bridge_ref[pl.ds(start + rest, left), :] = full(block[:left])
            small_ref[aligned(index, part), :] = full(block[left:])
    for half in range(2):
        rows_ref[half * few : (half + 1) * few] = pair(
            take(own_ref.at[0, half], 0, rows, wide)[rows - few :],
            take(over_ref.at[0, half], 0, rows, wide)[rows - few :],
        )
    vec_ref[...] = rows_ref[0:6]
    take_rows(rows_ref, 6, up_sum_ref, bias_sum_ref)
    pos_ref[...] = small_ref[0:PATCHES]
    dec_vec_ref[...] = small_ref[PAD_D : PAD_D + 8]
    take_rows(small_ref, PAD_D + 8, dec_up_sum_ref, dec_bias_sum_ref)


def enc_hidden_whole_kernel(place_ref, own_ref, over_ref, fc1_ref, fc2_ref):
    for ref, core, side, half in pieces_of(place_ref, own_ref, over_ref):
        rows = ref.shape[0] // 2
        width = 2 * rows
        fc2_ref[aligned(4 * core + 2 * side + half, rows), :] = full(ref[:rows])
        lanes = aligned(2 * core + side, width)
        for part in range(2):
            fc1_ref[(2 * half + part) * rows : (2 * half + part + 1) * rows, lanes] = full(
                ref[rows:, part * width : (part + 1) * width]
            )


def spread(piece):
    other = flip(piece, 2)
    return piece, other, flip(piece, 1), flip(other, 1)


def pack(order, place, pieces, after=()):
    (packed,) = kernel_call(
        order, pack_kernel, [shaped((2, 2) + pieces[0].shape)], place, *pieces, scalars=1, after=after, name="pack"
    )
    return packed, swap(packed, "section")


def pick(stacked, index):
    return lax.dynamic_index_in_dim(stacked, index, 0, keepdims=False)


def body(
    enc_in, keep_index, image_count, enc_vec, enc_qkv, enc_qv_bias, enc_out_w, enc_fc1, enc_fc1_bias, enc_fc2,
    bridge_w, dec_vec, dec_pos, dec_qkv, dec_qv_bias, dec_out_w, dec_fc1, dec_fc1_bias, dec_fc2, dec_cot,
):
    core = lax.axis_index("section")
    group = lax.axis_index("dp")
    place = jnp.stack([core, group % 2, group // 2 % 2]).astype(jnp.int32)
    images = keep_index.shape[1]
    enc_width, dec_width = bridge_w.shape
    enc_local, dec_local = enc_qkv.shape[2], dec_qkv.shape[2]
    enc_size, dec_size = enc_width // HE, dec_width // HD
    enc_mlp, dec_mlp = enc_fc1.shape[1], dec_fc1.shape[1]
    rows_e, rows_d = images * PAD_E, images * PAD_D
    enc_groups, dec_groups = enc_local // LANES, dec_local // LANES
    enc_heads, dec_heads = LANES // enc_size, LANES // dec_size
    enc_qkv, dec_qkv = jnp.transpose(enc_qkv, (1, 0, 2)), jnp.transpose(dec_qkv, (1, 0, 2))
    enc_fc1_bias, dec_fc1_bias = enc_fc1_bias[None], dec_fc1_bias[None]
    raw_in = enc_in
    enc_in = jnp.transpose(enc_in, (1, 0, 2))
    keep = jnp.pad(pick(keep_index, core), ((0, 0), (0, PAD_E - VIS)), constant_values=-1)
    cot = pick(dec_cot, core)
    count = pick(image_count, core)
    dec_rows = images * PATCHES

    order = []
    call = functools.partial(kernel_call, order)

    def enc_attend(rows, memory=24):
        return call(
            functools.partial(enc_attend_kernel, images, enc_size),
            [
                shaped((images * VIS, enc_width)),
                shaped((rows_e, enc_width)),
                shaped((rows_e, enc_width)),
                shaped((3, rows_e, enc_local)),
                shaped((enc_groups, enc_heads * rows_e, rows_e)),
                shaped((rows_e, enc_local)),
            ],
            place, rows, enc_vec, enc_qkv, enc_qv_bias, enc_out_w,
            scalars=1, memory=memory, name="enc_attend",
        )

    part, x, normed, proj, weights, mix = enc_attend(enc_in, 60)
    part_other = swap(part, "tensor")
    raw_in, x = lax.optimization_barrier((raw_in, x))
    side_in = flip(pick(raw_in, core), 1)
    side_part, side_x, side_normed, side_proj, side_weights, side_mix = enc_attend(side_in)
    part_two, middle, normed_two, hidden, slope, forward_send = call(
        enc_hidden_kernel,
        [
            shaped((images * VIS, enc_width)),
            shaped((rows_e, enc_width), FULL),
            shaped((rows_e, enc_width)),
            shaped((rows_e, enc_mlp)),
            shaped((rows_e, enc_mlp)),
            shaped((rows_e, enc_mlp // 4 + enc_width + enc_width // 2 + enc_local)),
        ],
        place, x, enc_vec, part, part_other, enc_fc1, enc_fc1_bias, normed, mix, enc_fc2,
        scalars=1, name="enc_hidden",
    )
    part_two_other = swap(part_two, "tensor")
    side_part_other = swap(side_part, "tensor")

    (
        dec_part, enc_out, enc_pad, starting, dec_normed, dec_proj, dec_weights, dec_mix,
    ) = call(
        functools.partial(dec_attend_kernel, images, dec_size),
        [
            shaped((rows_d, dec_width)),
            shaped((images * VIS, enc_width)),
            shaped((rows_e, enc_width)),
            shaped((rows_d, dec_width), FULL),
            shaped((rows_d, dec_width)),
            shaped((3, rows_d, dec_local)),
            shaped((images * dec_groups, dec_heads * PAD_D, PAD_D)),
            shaped((rows_d, dec_local)),
        ],
        count, keep, middle, part_two, part_two_other, enc_vec, bridge_w,
        dec_vec, dec_pos, dec_qkv, dec_qv_bias, dec_out_w,
        scalars=1, name="dec_attend",
    )
    dec_part_other = swap(dec_part, "tensor")
    enc_out_over = swap(enc_out, "section")
    forward_over = swap(forward_send, "section")
    side_middle, side_normed_two, side_hidden, side_slope, side_forward_send = call(
        enc_side_hidden_kernel,
        [
            shaped((rows_e, enc_width), FULL),
            shaped((rows_e, enc_width)),
            shaped((rows_e, enc_mlp)),
            shaped((rows_e, enc_mlp)),
            shaped((rows_e, enc_mlp // 4 + enc_width + enc_width // 2 + enc_local)),
        ],
        place, side_x, enc_vec, side_part, side_part_other, enc_fc1, enc_fc1_bias, side_normed, side_mix,
        scalars=1, name="enc_side_hidden",
    )
    (
        dec_part_back, dec_part_two, dec_middle, dec_normed_two, dec_hid, out_low, dec_up, up_sum, out_sum, d1_send,
    ) = call(
        functools.partial(dec_hidden_kernel, images),
        [
            shaped((rows_d, dec_width)),
            shaped((rows_d, dec_width)),
            shaped((rows_d, dec_width), FULL),
            shaped((rows_d, dec_width)),
            shaped((rows_d, dec_mlp)),
            shaped((rows_d, dec_width)),
            shaped((rows_d, dec_mlp)),
            shaped((1, dec_mlp), FULL),
            shaped((1, dec_width), FULL),
            shaped((rows_d, dec_mlp // 2 + dec_width // 2 + dec_mlp + dec_width)),
        ],
        count, place, starting, dec_part, dec_part_other, dec_vec, dec_fc1, dec_fc1_bias, dec_fc2, cot,
        scalars=2, after=[forward_over], name="dec_hidden",
    )

    side_forward_over = swap(side_forward_send, "section")
    d1_over = swap(d1_send, "section")
    dec_part_back_other = swap(dec_part_back, "tensor")
    (enc_out_both,) = call(
        both_cores_kernel, [shaped((images * VIS, 2, enc_width))],
        place, enc_out, enc_out_over, scalars=1, name="enc_out_both",
    )
    d1_mine, d1_theirs = call(
        dec_hidden_weights_kernel,
        [shaped((2, dec_mlp // 4, dec_width))] * 2,
        place, dec_hid, out_low, dec_normed_two, dec_up, d1_over,
        scalars=1, after=[side_forward_over], name="dec_hidden_weights",
    )
    d1_arrived = flip(d1_theirs, 1)
    dec_part_one, dec_middle_grad, dec_middle_low, dec_stacked, middle_sums, dec_bias_sum, d2_send = call(
        functools.partial(dec_attend_back_kernel, images, dec_size),
        [
            shaped((rows_d, dec_width)),
            shaped((rows_d, dec_width), FULL),
            shaped((rows_d, dec_width)),
            shaped((3, rows_d, dec_local)),
            shaped((3, dec_width), FULL),
            shaped((2, dec_local), FULL),
            shaped((rows_d, 4 * dec_local + dec_width)),
        ],
        place, dec_middle, out_low, dec_part_back, dec_part_back_other, dec_vec, dec_proj, dec_weights, dec_qkv, dec_out_w,
        dec_normed, dec_mix,
        scalars=1, name="dec_attend_back",
    )
    d2_over = swap(d2_send, "section")
    dec_part_one_other = swap(dec_part_one, "tensor")
    d1_mine, d1_theirs = fold(order, place, 2, d1_mine, d1_arrived)
    d2_mine, d2_theirs = call(
        dec_head_weights_kernel,
        [shaped((2, dec_width // 4, 2 * dec_local))] * 2,
        place, dec_normed, dec_stacked, dec_mix, dec_middle_low, d2_over,
        scalars=1, name="dec_head_weights",
    )
    d2_arrived = flip(d2_theirs, 1)
    enc_cot, lifted_grad, pos_grad, start_sums = call(
        functools.partial(dec_start_back_kernel, images),
        [
            shaped((rows_e, enc_width)),
            shaped((rows_e, dec_width)),
            shaped((PAD_D, dec_width), FULL),
            shaped((4, dec_width), FULL),
        ],
        count, keep, starting, dec_part_one, dec_part_one_other, dec_vec, dec_middle_grad, bridge_w,
        scalars=1, name="dec_start_back",
    )
    side_cot = flip(enc_cot, 1)
    over_cot = swap(enc_cot, "section")
    d1_mine, d1_theirs = call(
        fold_more_kernel,
        [shaped((dec_mlp // 4 + dec_width // 4, dec_width))] * 2,
        place, d2_mine, d2_arrived, d1_mine, d1_theirs,
        scalars=1, name="fold_more",
    )
    d1_arrived = flip(d1_theirs, 2)
    small_rows = 256
    d3_keep, d3_send = call(
        dec_bridge_weights_kernel,
        [shaped((2, 2, enc_width // 8 + small_rows // 8, dec_width))] * 2,
        place, enc_pad, lifted_grad, pos_grad, start_sums, middle_sums, out_sum, up_sum, dec_bias_sum,
        scalars=1, scratch=[pltpu.VMEM((small_rows, dec_width), FULL)], name="dec_bridge_weights",
    )
    d3_other = swap(d3_send, "section")
    side_cot, d3_keep = lax.optimization_barrier((side_cot, d3_keep))
    side_over_cot = swap(side_cot, "section")
    part, up, up_send = call(
        enc_hidden_back_kernel,
        [
            shaped((2 * images * VIS, enc_width)),
            shaped((2 * rows_e, enc_mlp)),
            shaped((2 * rows_e, enc_mlp // 4)),
        ],
        place, enc_cot, side_cot, slope, side_slope, enc_fc1, enc_fc2,
        scalars=1, after=[over_cot], name="enc_hidden_back",
    )
    up_over = swap(up_send, "section")
    part_other = swap(part, "tensor")
    d3_mine, d3_theirs = fold(order, place, 1, d3_keep, d3_other, after=[side_over_cot])
    d3_arrived = flip(d3_theirs, 1)
    e1_mine, e1_theirs = call(
        enc_hidden_weights_kernel,
        [shaped((enc_mlp // 4, enc_width))] * 2,
        place, hidden, side_hidden, enc_cot, side_cot, normed_two, side_normed_two, up,
        forward_over, side_forward_over, over_cot, side_over_cot, up_over,
        scalars=1, name="enc_hidden_weights",
    )
    e1_arrived = flip(e1_theirs, 2)
    d1 = add(order, d1_mine, d1_arrived)
    d1_arrived = cross_start(d1)
    back_part, middle_grad, middle_low, stacked, middle_two_sums, bias_sum, enc_up_sum, e3_send = call(
        functools.partial(enc_attend_back_kernel, images, enc_size),
        [
            shaped((2 * images * VIS, enc_width)),
            shaped((2 * rows_e, enc_width), FULL),
            shaped((2 * rows_e, enc_width)),
            shaped((3, 2 * rows_e, enc_local)),
            shaped((4, enc_width), FULL),
            shaped((2, enc_local), FULL),
            shaped((1, enc_mlp), FULL),
            shaped((2 * rows_e, 2 * enc_local)),
        ],
        place, middle, side_middle, enc_cot, side_cot, part, part_other, enc_vec, proj, side_proj,
        weights, side_weights, enc_qkv, enc_out_w, up,
        scalars=1, after=[d3_arrived], name="enc_attend_back",
    )
    e3_over = swap(e3_send, "section")
    back_part_other = swap(back_part, "tensor")
    d1 = cross_end(order, d1, d1_arrived)
    d1_spread = spread(d1)
    few = 32
    grad_in, small = call(
        functools.partial(enc_start_back_kernel, images),
        [shaped((images * VIS, 1, enc_width), FULL), shaped((few, enc_width))],
        x, side_x, back_part, back_part_other, enc_vec, middle_grad, middle_two_sums, enc_up_sum, bias_sum,
        scratch=[pltpu.VMEM((few, enc_width), FULL)], name="enc_start_back",
    )
    e1 = add(order, e1_mine, e1_arrived, after=[e3_over])
    dec_part_two, e1 = lax.optimization_barrier((dec_part_two, e1))
    dec_part_two_other = swap(dec_part_two, "tensor")
    e1_arrived = cross_start(e1)
    e3_mine, e3_theirs = call(
        last_weights_kernel,
        [
            shaped(
                (
                    ((enc_width // 4 + few // 2) * 2 * enc_local + (enc_width + small_rows) // 8 * dec_width)
                    // (dec_width // 2),
                    dec_width // 2,
                )
            )
        ] * 2,
        place, normed, side_normed, stacked, mix, side_mix, middle_low, forward_over, side_forward_over, e3_over,
        small, d3_mine, d3_arrived,
        scalars=1, after=[d1_spread[1]], name="last_weights",
    )
    e3_arrived = flip(e3_theirs, 2)
    d1_packed = pack(order, place, d1_spread)
    (dec_out,) = call(
        functools.partial(dec_out_kernel, images),
        [shaped((dec_rows, dec_width))],
        count, dec_middle, dec_part_two, dec_part_two_other, dec_vec,
        scalars=1, name="dec_out",
    )
    e1 = cross_end(order, e1, e1_arrived)
    e1_spread = spread(e1)
    e3 = add(order, e3_mine, e3_arrived)
    e3_arrived = cross_start(e3)
    g_dec_fc1, g_dec_fc2, g_dec_qkv, g_dec_out_w = call(
        dec_whole_kernel,
        [shaped(x.shape, FULL) for x in (dec_fc1, dec_fc2, dec_qkv, dec_out_w)],
        place, *d1_packed, scalars=1, name="dec_whole",
    )
    mark(order, e1_spread[1])
    e3 = cross_end(order, e3, e3_arrived)
    e3_spread = spread(e3)
    e1_packed = pack(order, place, e1_spread)
    mark(order, e3_spread[1])
    g_enc_fc1, g_enc_fc2 = call(
        enc_hidden_whole_kernel,
        [shaped(enc_fc1.shape, FULL), shaped(enc_fc2.shape, FULL)],
        place, *e1_packed, scalars=1, name="enc_hidden_whole",
    )
    e3_packed = pack(order, place, e3_spread)
    (
        g_enc_qkv, g_enc_out_w, g_enc_vec, g_enc_fc1_bias, g_enc_qv_bias,
        g_bridge, g_dec_pos, g_dec_vec, g_dec_fc1_bias, g_dec_qv_bias,
    ) = call(
        last_whole_kernel,
        [
            shaped(x.shape, FULL)
            for x in (
                enc_qkv, enc_out_w, enc_vec, shaped((enc_mlp // LANES, LANES)), enc_qv_bias,
                bridge_w, dec_pos, dec_vec, shaped((dec_mlp // LANES, LANES)), dec_qv_bias,
            )
        ],
        place, *e3_packed, scalars=1,
        scratch=[pltpu.VMEM((few, enc_width), FULL), pltpu.VMEM((small_rows, dec_width), FULL)],
        name="last_whole",
    )

    return (
        jnp.transpose(enc_out_both, (1, 0, 2)),
        dec_out[None],
        jnp.transpose(grad_in, (1, 0, 2)),
        g_enc_vec,
        jnp.transpose(g_enc_qkv, (1, 0, 2)),
        g_enc_qv_bias,
        g_enc_out_w,
        g_enc_fc1,
        g_enc_fc1_bias.reshape(-1),
        g_enc_fc2,
        g_bridge,
        g_dec_vec,
        g_dec_pos,
        jnp.transpose(g_dec_qkv, (1, 0, 2)),
        g_dec_qv_bias,
        g_dec_out_w,
        g_dec_fc1,
        g_dec_fc1_bias.reshape(-1),
        g_dec_fc2,
    )


def solution(mesh):
    return jax.shard_map(
        body,
        mesh=mesh,
        in_specs=(
            P(None, "dp", None),
            P(None, "dp", None),
            P(None, "dp"),
            P(),
            P(None, None, "tensor"),
            P(None, "tensor"),
            P("tensor", None),
            P(None, "tensor"),
            P("tensor"),
            P("tensor", None),
            P(),
            P(),
            P(),
            P(None, None, "tensor"),
            P(None, "tensor"),
            P("tensor", None),
            P(None, "tensor"),
            P("tensor"),
            P("tensor", None),
            P(None, "dp", None),
        ),
        out_specs=(
            P(None, "dp", None),
            P("section", "dp", None),
            P("section", "dp", None),
            P(),
            P(None, None, "tensor"),
            P(None, "tensor"),
            P("tensor", None),
            P(None, "tensor"),
            P("tensor"),
            P("tensor", None),
            P(),
            P(),
            P(),
            P(None, None, "tensor"),
            P(None, "tensor"),
            P("tensor", None),
            P(None, "tensor"),
            P("tensor"),
            P("tensor", None),
        ),
        check_vma=False,
    )
```
